32 devices in a mesh: tile: 8 (over z, x), ens: 4 (over y, core).
Axes of the slice: x: 2, y: 2, z: 4, core: 2. Of those that a mesh axis runs over, the one named last changes fastest.
Arguments:
- initial_sample_set: float32 [80, 2, 32, 2048], P('ens', None, 'tile'), may hold values from -6 to 6
- flow_velocity: float32 [2, 2, 32, 2048], P(None, None, 'tile'), may hold values from -0.4 to 0.4
- obs_loc: int32 [3, 2, 8192], P(None, None, 'tile'), may hold values from 0 to 2047, as said below
- obs_count: int32 [2, 8], P(None, 'tile'), may hold values from 256 to 1024, as said below
- obs_value: float32 [2, 8192], P(None, 'tile'), may hold values from -6 to 6
- obs_error: float32 [2, 8192], P(None, 'tile'), may hold values from 0.25 to 2
Outputs:
- analysis: float32 [80, 2, 32, 2048], P('ens', None, 'tile')
The draws below stay inside these ranges and needn't reach their ends.
Inputs may be any that keep to these rules, and one draw needn't show every extreme that they name: `obs_loc`: slots 1024 * t to 1024 * (t + 1) - 1 of a batch belong to tile t: their row lies in rows 4 * t to 4 * (t + 1) - 1; columns lie in 0 to 2047 and levels in 0 to 1. `obs_count`: in every batch some tile has exactly 1024 live observations; a tile's live observations are its first slots.
All inputs are finite; a program needn't handle non-finite values.
Results may differ from the reference program's by a relative error of at most 0.0003.
Values sent between devices are 32-bit elements; how exact they have to be, the bound alone decides.
No kernel may reach another device: no remote copies, remote signals or barrier semaphores. Data moves between devices by JAX's collectives and lax.ppermute only.
A program may use at most 128 MiB of HBM per device.

```python
import math
import jax
import jax.numpy as jnp
from jax import lax

MEMBERS = 80
LEVELS = 2
ROWS_DEV = 4
NY = 2048
OBS_TILE = 1024
BATCHES = 2
REACH = 2
TILES = 8
NX = 32
OBS = 8192


def draw_obs_count(key, part):
    random_seed_input = jax.random.fold_in(key, 31)
    key_full = jax.random.fold_in(key, 57)
    fewest = OBS_TILE // 4
    span_count = OBS_TILE - fewest + 1
    draws_load = jax.random.randint(random_seed_input, (BATCHES, TILES), 0, span_count)
    counts = fewest + draws_load * draws_load // span_count
    busiest = jax.random.randint(key_full, (BATCHES, 1), 0, TILES)
    tile_numbers = jnp.arange(TILES)[None, :]
    return jnp.where(tile_numbers == busiest, OBS_TILE, counts).astype(jnp.int32)


def draw_obs_loc(key, part):
    owner = jnp.arange(OBS) // OBS_TILE
    row_inside = jax.random.randint(jax.random.fold_in(key, 71), (BATCHES, OBS), 0, ROWS_DEV)
    column = jax.random.randint(jax.random.fold_in(key, 72), (BATCHES, OBS), 0, NY)
    levels_drawn = jax.random.randint(jax.random.fold_in(key, 73), (BATCHES, OBS), 0, LEVELS)
    row_inside = row_inside.at[:, 0].set(0)
    row_inside = row_inside.at[:, OBS - 1].set(ROWS_DEV - 1)
    column = column.at[:, 0].set(NY - 1)
    column = column.at[:, 1].set(0)
    rows_drawn = owner[None, :] * ROWS_DEV + row_inside
    return jnp.stack([rows_drawn, column, levels_drawn]).astype(jnp.int32)


def block_scale(stream_key, shape, pieces, least, top_value):
    level = 1.0
    for dim, parts in pieces:
        heights = jax.random.uniform(jax.random.fold_in(jax.random.fold_in(stream_key, 6), dim), (parts,), jnp.float32, least / len(pieces), top_value / len(pieces))
        level = level * jnp.repeat(jnp.exp(heights), shape[dim] // parts).reshape((-1,) + (1,) * (len(shape) - 1 - dim))
    return level


def scatter_about(stream_key, dims, width, limit, shards=(), held_as=jnp.bfloat16):
    values = width * jax.random.normal(stream_key, dims, jnp.float32)
    if shards:
        values = values * block_scale(stream_key, dims, shards, -0.22, 0.18)
    return jnp.clip(values, -limit, limit).astype(held_as)


def setup_inputs(seed: int = 0) -> dict:
    keys = jax.random.split(jax.random.key(seed), 7)
    return {
        "initial_sample_set": scatter_about(keys[0], (MEMBERS, LEVELS, NX, NY), 1.0, 6.0, ((0, 4), (2, 8)), jnp.float32),
        "flow_velocity": jnp.clip(jax.random.uniform(keys[1], (2, LEVELS, NX, NY), jnp.float32, -0.4, 0.4) * block_scale(keys[1], (2, LEVELS, NX, NY), ((2, 8),), -0.4, 0.0), -0.4, 0.4),
        "obs_loc": draw_obs_loc(jax.random.fold_in(keys[6], 71), 0),
        "obs_count": draw_obs_count(jax.random.fold_in(keys[6], 71), 0),
        "obs_value": scatter_about(keys[4], (BATCHES, OBS), 1.0, 6.0, ((1, 8),), jnp.float32),
        "obs_error": jnp.clip(jnp.exp(math.log(2.0) - 2.0794415 * jax.random.uniform(keys[5], (BATCHES, OBS), jnp.float32) ** block_scale(keys[5], (BATCHES, OBS), ((1, 8),), -0.2, 0.2)), 0.25, 2.0),
    }


SPREAD_RATE = 0.05
EPSILON = 1e-06
PRECISE = lax.Precision.HIGHEST

def advance(centre, row_above, row_below, col_left, col_right, flow_velocity):
    wind_rows = flow_velocity[0][None]
    wind_cols = flow_velocity[1][None]
    tendency = jnp.maximum(wind_rows, 0.0) * (centre - row_above) + jnp.minimum(wind_rows, 0.0) * (row_below - centre) + jnp.maximum(wind_cols, 0.0) * (centre - col_left) + jnp.minimum(wind_cols, 0.0) * (col_right - centre)
    return centre - tendency + SPREAD_RATE * (row_above + row_below + col_left + col_right - 4.0 * centre)

def increments(prior_obs, row_values, error_row, live_mask):
    members = prior_obs.shape[0]
    average = lax.optimization_barrier(jnp.sum(prior_obs, axis=0)) / members
    deviation = prior_obs - average[None, :]
    var_prior = lax.optimization_barrier(jnp.sum(deviation * deviation, axis=0)) / (members - 1) + EPSILON
    combined = var_prior + error_row
    shrink_factor = jnp.sqrt(error_row / combined)
    mean_post = (error_row * average + var_prior * row_values) / combined
    obs_shift = live_mask[None, :] * ((shrink_factor - 1.0)[None, :] * deviation + (mean_post - average)[None, :])
    weight = live_mask[None, :] * deviation / ((members - 1) * var_prior)[None, :]
    return (weight, obs_shift)

def block_gain(states, weight, obs_shift, obs_place, cell_lev, cell_row, cell_col, radius, col_radius):
    covariance = lax.dot_general(weight, states, (((0,), (0,)), ((), ())), precision=PRECISE, preferred_element_type=jnp.float32)
    row_gap = cell_row[None, :] - obs_place[0][:, None]
    column_spacing = cell_col[None, :] - obs_place[1][:, None]
    level_gap = jnp.abs(cell_lev[None, :] - obs_place[2][:, None])
    closeness = jnp.maximum(1.0 - row_gap * row_gap / (radius * radius) - column_spacing * column_spacing / (col_radius * col_radius), 0.0)
    gain_map = covariance * (closeness * closeness / (1.0 + level_gap))
    return jnp.dot(obs_shift, gain_map, precision=PRECISE, preferred_element_type=jnp.float32)

def reference(initial_sample_set, flow_velocity, obs_loc, obs_count, obs_value, obs_error):
    padded = jnp.pad(initial_sample_set, ((0, 0), (0, 0), (1, 1), (1, 1)))
    current_model_vector = advance(padded[:, :, 1:-1, 1:-1], padded[:, :, :-2, 1:-1], padded[:, :, 2:, 1:-1], padded[:, :, 1:-1, :-2], padded[:, :, 1:-1, 2:], flow_velocity)
    members, levels, row_total, col_total = current_model_vector.shape
    obs_total = obs_value.shape[1]
    slots = jnp.arange(obs_total, dtype=jnp.int32)
    owners = slots // OBS_TILE
    window = 2 * REACH + 1
    radius = float(REACH * ROWS_DEV)
    col_radius = float(col_total // 2)
    cell_index = jnp.arange(levels * ROWS_DEV * col_total, dtype=jnp.int32)
    cell_lev = (cell_index // (ROWS_DEV * col_total)).astype(jnp.float32)
    local_row = cell_index // col_total % ROWS_DEV
    cell_col = (cell_index % col_total).astype(jnp.float32)
    for batch_index in range(BATCHES):
        rows_obs = obs_loc[0, batch_index]
        cols_obs = obs_loc[1, batch_index]
        levs_obs = obs_loc[2, batch_index]
        flat_state = current_model_vector.reshape(members, -1)
        prior_obs = jnp.take(flat_state, (levs_obs * row_total + rows_obs) * col_total + cols_obs, axis=1)
        live_mask = (slots % OBS_TILE < obs_count[batch_index][owners]).astype(jnp.float32)
        weight, obs_shift = increments(prior_obs, obs_value[batch_index], obs_error[batch_index], live_mask)
        obs_place = obs_loc[:, batch_index].astype(jnp.float32)
        border = ((0, 0), (REACH, REACH), (0, 0))
        weight_pad = jnp.pad(weight.reshape(members, TILES, OBS_TILE), border)
        shift_pad = jnp.pad(obs_shift.reshape(members, TILES, OBS_TILE), border)
        place_pad = jnp.pad(obs_place.reshape(3, TILES, OBS_TILE), border)

        def count_per_tile(tile_index, current_grid_array=current_model_vector, weight_pad=weight_pad, shift_pad=shift_pad, place_pad=place_pad):
            near_weight = lax.dynamic_slice_in_dim(weight_pad, tile_index, window, 1).reshape(members, window * OBS_TILE)
            near_shift = lax.dynamic_slice_in_dim(shift_pad, tile_index, window, 1).reshape(members, window * OBS_TILE)
            near_place = lax.dynamic_slice_in_dim(place_pad, tile_index, window, 1).reshape(3, window * OBS_TILE)
            cells = lax.dynamic_slice_in_dim(current_grid_array, tile_index * ROWS_DEV, ROWS_DEV, 2).reshape(members, -1)
            cell_row = (tile_index * ROWS_DEV + local_row).astype(jnp.float32)
            update = block_gain(cells, near_weight, near_shift, near_place, cell_lev, cell_row, cell_col, radius, col_radius)
            return update.reshape(members, levels, ROWS_DEV, col_total)
        updates = lax.map(count_per_tile, jnp.arange(TILES, dtype=jnp.int32))
        current_model_vector = current_model_vector + jnp.transpose(updates, (1, 2, 0, 3, 4)).reshape(current_model_vector.shape)
    return current_model_vector
```

```python
import functools

import jax
import jax.numpy as jnp
from jax import lax
from jax.experimental import pallas as pl
from jax.experimental.pallas import tpu as pltpu
from jax.sharding import PartitionSpec as P

BATCHES = 2
REACH = 2
SPREAD_RATE = 0.05
EPSILON = 1e-06
LANE = 128
DEEP = 256
BLOCK = 512
F32 = jnp.float32
BF16 = jnp.bfloat16
VMEM = pl.BlockSpec(memory_space=pltpu.VMEM)
SMEM = pl.BlockSpec(memory_space=pltpu.SMEM)
PARAMS = pltpu.CompilerParams(vmem_limit_bytes=48 << 20)


def split(value):
    high = value.astype(BF16)
    return high, (value - high.astype(F32)).astype(BF16)


def forecast_kernel(x_ref, top_ref, bottom_ref, flow_ref, out_ref):
    members, levels, rows, cols = x_ref.shape
    height = levels * rows
    parts, bands = out_ref.shape[:2]
    row = lax.broadcasted_iota(jnp.int32, (height, cols), 0)
    col = lax.broadcasted_iota(jnp.int32, (height, cols), 1)
    winds = [
        jnp.concatenate([flow_ref[d, l] for l in range(levels)], axis=0) for d in range(2)
    ]

    def body(m, _):
        x = jnp.concatenate([x_ref[m, l] for l in range(levels)], axis=0)
        above = pltpu.roll(x, 1, 0)
        below = pltpu.roll(x, height - 1, 0)
        for l in range(levels):
            above = jnp.where(row == l * rows, top_ref[m, l : l + 1, :], above)
            below = jnp.where(row == (l + 1) * rows - 1, bottom_ref[m, l : l + 1, :], below)
        left = jnp.where(col == 0, 0.0, pltpu.roll(x, 1, 1))
        right = jnp.where(col == cols - 1, 0.0, pltpu.roll(x, cols - 1, 1))
        tendency = (
            jnp.maximum(winds[0], 0.0) * (x - above)
            + jnp.minimum(winds[0], 0.0) * (below - x)
            + jnp.maximum(winds[1], 0.0) * (x - left)
            + jnp.minimum(winds[1], 0.0) * (right - x)
        )
        ahead = x - tendency + SPREAD_RATE * (above + below + left + right - 4.0 * x)
        at = pl.multiple_of(m * height, height)
        for part in range(parts):
            for band in range(bands):
                first = (part * bands + band) * LANE
                out_ref[part, band, pl.ds(at, height), :] = ahead[:, first : first + LANE]
        return 0

    lax.fori_loop(0, members, body, 0)


def forecast(x, top, bottom, flow, parts):
    members, levels, rows, cols = x.shape
    return pl.pallas_call(
        forecast_kernel,
        out_shape=jax.ShapeDtypeStruct(
            (parts, cols // parts // LANE, members * levels * rows, LANE), F32
        ),
        in_specs=[VMEM] * 4,
        out_specs=VMEM,
        compiler_params=PARAMS,
        name="forecast",
    )(x, top, bottom, flow)


def observe_kernel(height, x_ref, place_ref, out_ref):
    parts, bands, depth, _ = x_ref.shape
    members = depth // height
    total = out_ref.shape[1]
    row = lax.broadcasted_iota(jnp.int32, (height, LANE), 0)

    def body(b, _):
        at = pl.multiple_of(b * LANE, LANE)
        column = place_ref[0:1, pl.ds(at, LANE)]
        flat_row = jnp.broadcast_to(place_ref[1:2, pl.ds(at, LANE)], (height, LANE))
        band_of = jnp.broadcast_to(column // LANE, (height, LANE))
        lane_of = jnp.broadcast_to(column % LANE, (height, LANE))
        mine = flat_row == row
        for m in range(members):
            found = jnp.zeros((height, LANE), F32)
            for k in range(parts * bands):
                block = x_ref[k // bands, k % bands, m * height : (m + 1) * height, :]
                picked = jnp.take_along_axis(block, lane_of, axis=1)
                found = jnp.where(band_of == k, picked, found)
            value = jnp.sum(jnp.where(mine, found, 0.0), axis=0, keepdims=True)
            out_ref[m : m + 1, pl.ds(at, LANE)] = value
        return 0

    lax.fori_loop(0, total // LANE, body, 0)


def observe(x, place, height):
    members = x.shape[2] // height
    return pl.pallas_call(
        functools.partial(observe_kernel, height),
        out_shape=jax.ShapeDtypeStruct((members, place.shape[1]), F32),
        in_specs=[VMEM] * 2,
        out_specs=VMEM,
        compiler_params=PARAMS,
        name="observe",
    )(x, place)


def weigh(prior, value, error, live):
    members = prior.shape[0]
    average = jnp.sum(prior, axis=0, keepdims=True) / members
    deviation = prior - average
    var_prior = jnp.sum(deviation * deviation, axis=0, keepdims=True) / (members - 1) + EPSILON
    combined = var_prior + error
    shrink = jnp.sqrt(error / combined)
    post = (error * average + var_prior * value) / combined
    shift = live * ((shrink - 1.0) * deviation + (post - average))
    weight = (live / ((members - 1) * var_prior)) * deviation
    return weight, shift


def pack(geometry, count_ref, load, att_ref, chunk, w_ref, s_ref, rc_ref):
    levels, _, _, row_scale, col_scale = geometry
    window = att_ref.shape[0]
    off = jnp.int32(0)
    for t in range(window):
        count = count_ref[t]

        def body(k, _, t=t, off=off, count=count):
            src = pl.multiple_of(k * chunk, chunk)
            dst = pl.multiple_of(off + k * chunk, LANE)
            att = att_ref[t, :, pl.ds(src, chunk)]
            slot = lax.broadcasted_iota(jnp.int32, (1, chunk), 1) + k * chunk
            live = (slot < count).astype(F32)
            prior = load(t, k)
            members = prior.shape[0]
            weight, shift = weigh(prior, att[3:4], att[4:5], live)
            pad = jnp.zeros((DEEP - 3 * members, chunk), BF16)
            for l in range(levels):
                high, low = split(weight / (1.0 + jnp.abs(att[2:3] - float(l))))
                w_ref[l, :, pl.ds(dst, chunk)] = jnp.concatenate([high, low, high, pad], axis=0)
            turned = jnp.concatenate([shift, jnp.zeros((LANE - members, chunk), F32)], axis=0).T
            high, low = split(turned)
            s_ref[pl.ds(dst, chunk), 0:LANE] = high
            s_ref[pl.ds(dst, chunk), LANE : 2 * LANE] = low
            rc_ref[0:1, pl.ds(dst, chunk)] = att[0:1] * row_scale
            rc_ref[1:2, pl.ds(dst, chunk)] = att[1:2] * col_scale
            return 0

        lax.fori_loop(0, (count + chunk - 1) // chunk, body, 0)
        off = off + (count + LANE - 1) // LANE * LANE
    dst = pl.multiple_of(off, LANE)
    for l in range(levels):
        w_ref[l, :, pl.ds(dst, BLOCK)] = jnp.zeros((DEEP, BLOCK), BF16)
    s_ref[pl.ds(dst, BLOCK), :] = jnp.zeros((BLOCK, 2 * LANE), BF16)
    rc_ref[:, pl.ds(dst, BLOCK)] = jnp.zeros((8, BLOCK), F32)
    return off


def scratch(levels, window, slots):
    room = window * slots + BLOCK + LANE
    return [
        pltpu.VMEM((levels, DEEP, room), BF16),
        pltpu.VMEM((room, 2 * LANE), BF16),
        pltpu.VMEM((8, room), F32),
    ]


def loader(prior_ref, chunk, own_layout):
    if own_layout:
        groups = prior_ref.shape[1]

        def load(t, k):
            at = pl.multiple_of(k * chunk, chunk)
            return jnp.concatenate(
                [prior_ref[t, g, :, pl.ds(at, chunk)] for g in range(groups)], axis=0
            )
    else:

        def load(t, k):
            return prior_ref[k, t]

    return load


def triple(x):
    high, low = split(x)
    members, width = x.shape
    pad = jnp.zeros((DEEP - 3 * members, width), BF16)
    return jnp.concatenate([high, high, low, pad], axis=0).T


def points_kernel(
    geometry, own_layout, count_ref, span_ref, prior_ref, att_ref, x_ref, place_ref, out_ref,
    w_ref, s_ref, rc_ref, acc_ref,
):
    levels, _, _, row_scale, col_scale = geometry
    chunk = min(2 * LANE, x_ref.shape[2])
    load = loader(prior_ref, chunk, own_layout)
    off = pack(geometry, count_ref, load, att_ref, chunk, w_ref, s_ref, rc_ref)
    x = jnp.concatenate([x_ref[g] for g in range(x_ref.shape[0])], axis=0)
    members, width = x.shape
    cells = triple(x)
    place = jnp.concatenate([place_ref[...], jnp.zeros((LANE - 8, width), F32)], axis=0).T
    cell_row = place[:, 0:1] * row_scale
    cell_col = place[:, 1:2] * col_scale
    cell_lev = place[:, 2:3]
    acc_ref[...] = jnp.zeros(acc_ref.shape, F32)

    def body(b, _):
        at = pl.multiple_of(b * BLOCK, BLOCK)
        row_gap = cell_row - rc_ref[0:1, pl.ds(at, BLOCK)]
        col_gap = cell_col - rc_ref[1:2, pl.ds(at, BLOCK)]
        near = jnp.maximum(1.0 - row_gap * row_gap - col_gap * col_gap, 0.0)
        cov = jnp.zeros((width, BLOCK), F32)
        for l in range(levels):
            cov_l = jnp.dot(cells, w_ref[l, :, pl.ds(at, BLOCK)], preferred_element_type=F32)
            cov = jnp.where(cell_lev == float(l), cov_l, cov)
        high, low = split(cov * (near * near))
        s = s_ref[pl.ds(at, BLOCK), :]
        acc_ref[...] += jnp.dot(high, s, preferred_element_type=F32)
        acc_ref[:, 0:LANE] += jnp.dot(low, s[:, 0:LANE], preferred_element_type=F32)
        return 0

    lax.fori_loop(0, (off + BLOCK - 1) // BLOCK, body, 0)
    out_ref[...] = x + (acc_ref[:, 0:LANE] + acc_ref[:, LANE : 2 * LANE]).T[0:members]


def update_points(geometry, own_layout, count, span, prior, att, x, place):
    window, _, slots = att.shape
    groups, share, width = x.shape
    return pl.pallas_call(
        functools.partial(points_kernel, geometry, own_layout),
        out_shape=jax.ShapeDtypeStruct((groups * share, width), F32),
        in_specs=[SMEM, SMEM, VMEM, VMEM, VMEM, VMEM],
        out_specs=VMEM,
        scratch_shapes=scratch(geometry[0], window, slots)
        + [pltpu.VMEM((width, 2 * LANE), F32)],
        compiler_params=PARAMS,
        name="update_points",
    )(count, span, prior, att, x, place)


def grid_kernel(
    geometry, own_layout, chunk, count_ref, span_ref, prior_ref, att_ref, x_ref, out_ref,
    w_ref, s_ref, rc_ref, xt_ref, acc_ref, q_ref,
):
    levels, rows, share, row_scale, col_scale = geometry
    groups, bands = x_ref.shape[:2]
    height = levels * rows
    cols = bands * LANE
    members = groups * share
    load = loader(prior_ref, chunk, own_layout)
    pack(geometry, count_ref, load, att_ref, chunk, w_ref, s_ref, rc_ref)
    q_ref[...] = (
        lax.broadcasted_iota(jnp.int32, (cols, LANE), 0) + span_ref[2 * rows + 1]
    ).astype(F32) * col_scale

    def cells(i):
        return jnp.concatenate(
            [
                jnp.concatenate(
                    [x_ref.at[g, b][pl.ds(i, share, stride=height), :] for g in range(groups)],
                    axis=0,
                )
                for b in range(bands)
            ],
            axis=1,
        )

    for i in range(height):
        xt_ref[i] = triple(cells(i))

    def row_body(p, _):
        cell_row = (span_ref[2 * rows] + p).astype(F32) * row_scale
        first, last = span_ref[p], span_ref[rows + p]
        acc_ref[...] = jnp.zeros(acc_ref.shape, F32)

        def body(b, _):
            at = pl.multiple_of(first + b * BLOCK, LANE)
            row_gap = cell_row - rc_ref[0:1, pl.ds(at, BLOCK)]
            base = 1.0 - row_gap * row_gap
            q = q_ref[...]
            col_gap = jnp.concatenate([q] * (BLOCK // LANE), axis=1) - rc_ref[1:2, pl.ds(at, BLOCK)]
            near = jnp.maximum(base - col_gap * col_gap, 0.0)
            taper = near * near
            s = s_ref[pl.ds(at, BLOCK), :]
            for l in range(levels):
                cov = jnp.dot(
                    xt_ref[l * rows + p], w_ref[l, :, pl.ds(at, BLOCK)], preferred_element_type=F32
                )
                high, low = split(cov * taper)
                acc_ref[l] += jnp.dot(high, s, preferred_element_type=F32)
                acc_ref[l, :, 0:LANE] += jnp.dot(low, s[:, 0:LANE], preferred_element_type=F32)
            return 0

        lax.fori_loop(0, (last - first + BLOCK - 1) // BLOCK, body, 0)
        for l in range(levels):
            i = l * rows + p
            inc = (acc_ref[l, :, 0:LANE] + acc_ref[l, :, LANE : 2 * LANE]).T[0:members]
            for g in range(groups):
                for b in range(bands):
                    at = pl.ds(i, share, stride=height)
                    out_ref.at[g, b][at, :] = (
                        x_ref.at[g, b][at, :]
                        + inc[g * share : (g + 1) * share, b * LANE : (b + 1) * LANE]
                    )
        return 0

    lax.fori_loop(0, rows, row_body, 0)


def update_grid(geometry, own_layout, count, span, prior, att, x):
    levels, rows = geometry[:2]
    window, _, slots = att.shape
    groups, bands = x.shape[:2]
    cols = bands * LANE
    chunk = min(2 * LANE, slots // groups)
    return pl.pallas_call(
        functools.partial(grid_kernel, geometry, own_layout, chunk),
        out_shape=jax.ShapeDtypeStruct(x.shape, F32),
        in_specs=[SMEM, SMEM, VMEM, VMEM, VMEM],
        out_specs=VMEM,
        scratch_shapes=scratch(levels, window, slots)
        + [
            pltpu.VMEM((levels * rows, cols, DEEP), BF16),
            pltpu.VMEM((levels, cols, 2 * LANE), F32),
            pltpu.VMEM((cols, LANE), F32),
        ],
        compiler_params=PARAMS,
        name="update_grid",
    )(count, span, prior, att, x)


def restore_kernel(x_ref, out_ref):
    members, levels, rows, cols = out_ref.shape
    parts, bands = x_ref.shape[:2]
    height = levels * rows

    def body(m, _):
        at = pl.multiple_of(m * height, height)
        for part in range(parts):
            for band in range(bands):
                block = x_ref[part, band, pl.ds(at, height), :]
                first = (part * bands + band) * LANE
                for l in range(levels):
                    out_ref[m, l, :, first : first + LANE] = block[l * rows : (l + 1) * rows]
        return 0

    lax.fori_loop(0, members, body, 0)


def restore(x, shape):
    return pl.pallas_call(
        restore_kernel,
        out_shape=jax.ShapeDtypeStruct(shape, F32),
        in_specs=[VMEM],
        out_specs=VMEM,
        compiler_params=PARAMS,
        name="restore",
    )(x)


def shifted(value, steps):
    count = lax.axis_size("tile")
    pairs = [(i, i + steps) for i in range(count) if 0 <= i + steps < count]
    return lax.ppermute(value, "tile", pairs)


def window_of(value):
    return jnp.stack(
        [value if d == 0 else shifted(value, -d) for d in range(-REACH, REACH + 1)]
    )


def on_device(initial_sample_set, flow_velocity, obs_loc, obs_count, obs_value, obs_error):
    x = initial_sample_set
    share, levels, rows, col_total = x.shape
    ens = lax.axis_size("ens")
    cols = col_total // ens
    slots = obs_value.shape[1]
    quarter = slots // ens
    tile_index = lax.axis_index("tile")
    ens_index = lax.axis_index("ens")
    geometry = (levels, rows, share, 1.0 / (REACH * rows), 1.0 / (col_total // 2))

    top = shifted(x[:, :, rows - 1, :], 1)
    bottom = shifted(x[:, :, 0, :], -1)

    local_row = obs_loc[0] - tile_index * rows
    slot = jnp.arange(slots, dtype=jnp.int32)
    live = slot[None, :] < obs_count
    att = jnp.stack(
        [obs_loc[0].astype(F32), obs_loc[1].astype(F32), obs_loc[2].astype(F32), obs_value, obs_error]
        + [jnp.zeros_like(obs_value)] * 3,
        axis=1,
    )
    near_att = window_of(att)
    near_count = window_of(obs_count[:, 0].astype(F32)[:, None] * jnp.ones((1, LANE), F32))
    counts = near_count[:, :, 0].astype(jnp.int32)

    place = jnp.stack([obs_loc[1], obs_loc[2] * rows + local_row]).reshape(2, -1)

    def spans(b):
        rounded = (counts[:, b] + LANE - 1) // LANE * LANE
        total = jnp.sum(rounded)
        zero = jnp.zeros((rows,), jnp.int32)
        return jnp.concatenate(
            [zero, zero + total, jnp.stack([tile_index * rows, ens_index * cols])]
        )

    ahead = forecast(x, top, bottom, flow_velocity, ens)
    state = lax.all_to_all(ahead, "ens", split_axis=0, concat_axis=0)
    seen = observe(ahead, place, levels * rows)
    seen0 = lax.all_gather(seen[:, :slots], "ens", axis=0)
    later = lax.all_to_all(
        jnp.transpose(seen[:, slots:].reshape(share, ens, quarter), (1, 0, 2)),
        "ens", split_axis=0, concat_axis=0,
    )
    prior0 = window_of(seen0)
    at = ens_index * quarter
    later_place = lax.dynamic_slice_in_dim(att[1], at, quarter, axis=1)
    later = update_points(
        geometry, True, counts[:, 0], spans(0), prior0, near_att[:, 0], later, later_place
    )
    prior1 = lax.all_gather(window_of(later), "ens", axis=0)
    state = update_grid(geometry, True, counts[:, 0], spans(0), prior0, near_att[:, 0], state)
    state = update_grid(geometry, False, counts[:, 1], spans(1), prior1, near_att[:, 1], state)
    back = lax.all_to_all(state, "ens", split_axis=0, concat_axis=0)
    return restore(back, x.shape)


def solution(mesh):
    in_specs = (
        P("ens", None, "tile", None),
        P(None, None, "tile", None),
        P(None, None, "tile"),
        P(None, "tile"),
        P(None, "tile"),
        P(None, "tile"),
    )
    out_specs = P("ens", None, "tile", None)
    return jax.shard_map(
        on_device, mesh=mesh, in_specs=in_specs, out_specs=out_specs, check_vma=False
    )
```

```python
import functools

import jax
import jax.numpy as jnp
from jax import lax
from jax.experimental import pallas as pl
from jax.experimental.pallas import tpu as pltpu
from jax.sharding import PartitionSpec as P

BATCHES = 2
REACH = 2
SPARE = 4
SPREAD_RATE = 0.05
EPSILON = 1e-06
LANE = 128
DEEP = 256
BLOCK = 512
F32 = jnp.float32
BF16 = jnp.bfloat16
VMEM = pl.BlockSpec(memory_space=pltpu.VMEM)
SMEM = pl.BlockSpec(memory_space=pltpu.SMEM)
PARAMS = pltpu.CompilerParams(vmem_limit_bytes=48 << 20)


def split(value):
    high = value.astype(BF16)
    return high, (value - high.astype(F32)).astype(BF16)


def order_kernel(rows, id_ref, loc_ref, value_ref, error_ref, count_ref, att_ref):
    batches, slots = value_ref.shape
    earlier = (
        lax.broadcasted_iota(jnp.int32, (slots, slots), 0)
        < lax.broadcasted_iota(jnp.int32, (slots, slots), 1)
    ).astype(BF16)
    slot = lax.broadcasted_iota(jnp.int32, (1, slots), 1)
    key_of = lax.broadcasted_iota(jnp.int32, (8, slots), 0)
    for b in range(batches):
        count = count_ref[b, 0]
        local_row = loc_ref[0, b : b + 1, :] - id_ref[0] * rows
        key = jnp.where(slot < count, local_row, rows)
        mine = key_of == jnp.broadcast_to(key, (8, slots))
        ones = mine.astype(F32)
        before = jnp.dot(ones.astype(BF16), earlier, preferred_element_type=F32)
        totals = jnp.sum(ones, axis=1, keepdims=True)
        start = jnp.zeros((1, slots), F32)
        place = jnp.zeros((1, slots), F32)
        cumulative = jnp.where(slot == 0, count.astype(F32), 0.0)
        for r in range(rows + 1):
            place = place + ones[r : r + 1] * (before[r : r + 1] + start)
            start = start + totals[r : r + 1]
            cumulative = jnp.where(slot == r + 1, start, cumulative)
        level = loc_ref[2, b : b + 1, :]
        fields = [
            loc_ref[0, b : b + 1, :].astype(F32),
            loc_ref[1, b : b + 1, :].astype(F32),
            level.astype(F32),
            value_ref[b : b + 1, :],
            error_ref[b : b + 1, :],
            (level * rows + local_row).astype(F32),
        ]
        table = jnp.concatenate(fields + [jnp.zeros((2, slots), F32)], axis=0)
        high, low = split(table)
        rest = (table - high.astype(F32) - low.astype(F32)).astype(BF16)
        target = lax.broadcasted_iota(jnp.int32, (slots, slots), 0)
        moved = (target == jnp.broadcast_to(place.astype(jnp.int32), (slots, slots))).astype(BF16)
        out = lax.dot_general(
            jnp.concatenate([high.astype(F32), low.astype(F32), rest.astype(F32)], axis=0).astype(BF16),
            moved,
            (((1,), (1,)), ((), ())),
            preferred_element_type=F32,
        )
        out = (out[0:8] + out[8:16]) + out[16:24]
        att_ref[b] = jnp.concatenate([out[0:5], cumulative, out[5:6], jnp.zeros((1, slots), F32)], axis=0)


def order(ids, obs_loc, obs_value, obs_error, obs_count, rows):
    batches, slots = obs_value.shape
    return pl.pallas_call(
        functools.partial(order_kernel, rows),
        out_shape=jax.ShapeDtypeStruct((batches, 8, slots), F32),
        in_specs=[SMEM, VMEM, VMEM, VMEM, SMEM],
        out_specs=VMEM,
        compiler_params=PARAMS,
        name="order",
    )(ids, obs_loc, obs_value, obs_error, obs_count)


def forecast_kernel(id_ref, x_ref, top_ref, bottom_ref, flow_ref, *refs):
    outs, row_ref = refs[:-1], refs[-1]
    members, levels, rows, cols = x_ref.shape
    height = levels * rows
    parts, bands = len(outs), outs[0].shape[0]
    row = lax.broadcasted_iota(jnp.int32, (height, cols), 0)
    col = lax.broadcasted_iota(jnp.int32, (height, cols), 1)
    winds = [
        jnp.concatenate([flow_ref[d, l] for l in range(levels)], axis=0) for d in range(2)
    ]

    def body(m, _):
        x = jnp.concatenate([x_ref[m, l] for l in range(levels)], axis=0)
        above = pltpu.roll(x, 1, 0)
        below = pltpu.roll(x, height - 1, 0)
        for l in range(levels):
            above = jnp.where(row == l * rows, top_ref[m, l : l + 1, :], above)
            below = jnp.where(row == (l + 1) * rows - 1, bottom_ref[m, l : l + 1, :], below)
        left = jnp.where(col == 0, 0.0, pltpu.roll(x, 1, 1))
        right = jnp.where(col == cols - 1, 0.0, pltpu.roll(x, cols - 1, 1))
        tendency = (
            jnp.maximum(winds[0], 0.0) * (x - above)
            + jnp.minimum(winds[0], 0.0) * (below - x)
            + jnp.maximum(winds[1], 0.0) * (x - left)
            + jnp.minimum(winds[1], 0.0) * (right - x)
        )
        row_ref[...] = x - tendency + SPREAD_RATE * (above + below + left + right - 4.0 * x)
        at = pl.multiple_of(m * height, height)
        for k in range(parts):
            first = (id_ref[1] ^ k) * (bands * LANE)
            for band in range(bands):
                source = pl.multiple_of(first + band * LANE, LANE)
                outs[k][band, pl.ds(at, height), :] = row_ref[:, pl.ds(source, LANE)]
        return 0

    lax.fori_loop(0, members, body, 0)


def forecast(ids, x, top, bottom, flow, parts):
    members, levels, rows, cols = x.shape
    out = jax.ShapeDtypeStruct((cols // parts // LANE, members * levels * rows, LANE), F32)
    return pl.pallas_call(
        forecast_kernel,
        out_shape=[out] * parts,
        in_specs=[SMEM] + [VMEM] * 4,
        out_specs=[VMEM] * parts,
        scratch_shapes=[pltpu.VMEM((levels * rows, cols), F32)],
        compiler_params=PARAMS,
        name="forecast",
    )(ids, x, top, bottom, flow)


def fill_spare(put, att, odd):
    even_rows = jnp.concatenate([att[0:3], att[5:6]], axis=0)
    odd_rows = jnp.concatenate([att[3:5], att[3:5]], axis=0)
    put(jnp.where(odd, odd_rows, even_rows))


def observe_kernel(height, share, id_ref, att_ref, *refs):
    parts, out_ref = refs[:-1], refs[-1]
    bands = parts[0].shape[0]
    batches, _, slots = att_ref.shape
    row = lax.broadcasted_iota(jnp.int32, (height, LANE), 0)
    for b in range(batches):
        att = att_ref[b]
        odd = (id_ref[1] & 1) == 1

        def put(rows, b=b):
            out_ref[b, share : share + SPARE, :] = rows

        fill_spare(put, att, odd)

        def body(n, _, b=b):
            at = pl.multiple_of(n * LANE, LANE)
            column = att_ref[b, 1:2, pl.ds(at, LANE)].astype(jnp.int32)
            flat_row = att_ref[b, 6:7, pl.ds(at, LANE)].astype(jnp.int32)
            band_of = jnp.broadcast_to(column // LANE, (height, LANE))
            lane_of = jnp.broadcast_to(column % LANE, (height, LANE))
            mine = jnp.broadcast_to(flat_row, (height, LANE)) == row
            here = [
                band_of == (id_ref[1] ^ k) * bands + band
                for k in range(len(parts))
                for band in range(bands)
            ]
            for m in range(share):
                found = jnp.zeros((height, LANE), F32)
                for i in range(len(parts) * bands):
                    block = parts[i // bands][i % bands, m * height : (m + 1) * height, :]
                    picked = jnp.take_along_axis(block, lane_of, axis=1)
                    found = jnp.where(here[i], picked, found)
                value = jnp.sum(jnp.where(mine, found, 0.0), axis=0, keepdims=True)
                out_ref[b, m : m + 1, pl.ds(at, LANE)] = value
            return 0

        lax.fori_loop(0, slots // LANE, body, 0)


def observe(ids, att, parts, height, share):
    batches, _, slots = att.shape
    padded = (share + SPARE + 7) // 8 * 8
    return pl.pallas_call(
        functools.partial(observe_kernel, height, share),
        out_shape=jax.ShapeDtypeStruct((batches, padded, slots), F32),
        in_specs=[SMEM] + [VMEM] * (1 + len(parts)),
        out_specs=VMEM,
        compiler_params=PARAMS,
        name="observe",
    )(ids, att, *parts)


def weigh(prior, value, error, live):
    members = prior.shape[0]
    average = jnp.sum(prior, axis=0, keepdims=True) / members
    deviation = prior - average
    var_prior = jnp.sum(deviation * deviation, axis=0, keepdims=True) / (members - 1) + EPSILON
    combined = var_prior + error
    shrink = jnp.sqrt(error / combined)
    post = (error * average + var_prior * value) / combined
    shift = live * ((shrink - 1.0) * deviation + (post - average))
    weight = (live / ((members - 1) * var_prior)) * deviation
    return weight, shift


def pack(geometry, id_ref, flip, priors, w_ref, s_ref, rc_ref):
    levels, rows, share, row_scale, col_scale = geometry
    halves, groups, _, width = priors[0].shape
    chunk = min(2 * LANE, width)
    lane = lax.broadcasted_iota(jnp.int32, (1, LANE), 1)
    counts = [ref[0, 0, share + 3 : share + 4, 0:LANE] for ref in priors]

    def number(t, at):
        return jnp.sum(jnp.where(lane == at, counts[t], 0.0)).astype(jnp.int32)

    off = jnp.int32(0)
    starts = []
    for t, ref in enumerate(priors):
        count = number(t, 0)
        starts.append(off)

        def body(k, _, ref=ref, off=off, count=count):
            src = k * chunk
            half = (src // width) ^ (id_ref[1] & (halves - 1))
            at = pl.multiple_of(src % width, chunk)
            dst = pl.multiple_of(off + src, LANE)
            slot = lax.broadcasted_iota(jnp.int32, (1, chunk), 1) + src
            live = (slot < count).astype(F32)
            prior = jnp.concatenate(
                [ref[half, flip ^ g, 0:share, pl.ds(at, chunk)] for g in range(groups)], axis=0
            )
            place = ref[half, 0, share : share + SPARE, pl.ds(at, chunk)]
            seen = ref[half, 1, share : share + SPARE, pl.ds(at, chunk)]
            members = prior.shape[0]
            weight, shift = weigh(prior, seen[0:1], seen[1:2], live)
            pad = jnp.zeros((DEEP - 3 * members, chunk), BF16)
            for l in range(levels):
                high, low = split(weight / (1.0 + jnp.abs(place[2:3] - float(l))))
                w_ref[l, :, pl.ds(dst, chunk)] = jnp.concatenate([high, low, high, pad], axis=0)
            turned = jnp.concatenate([shift, jnp.zeros((LANE - members, chunk), F32)], axis=0).T
            high, low = split(turned)
            s_ref[pl.ds(dst, chunk), 0:LANE] = high
            s_ref[pl.ds(dst, chunk), LANE : 2 * LANE] = low
            rc_ref[0:1, pl.ds(dst, chunk)] = place[0:1] * row_scale
            rc_ref[1:2, pl.ds(dst, chunk)] = place[1:2] * col_scale
            return 0

        lax.fori_loop(0, (count + chunk - 1) // chunk, body, 0)
        off = off + (count + LANE - 1) // LANE * LANE
    dst = pl.multiple_of(off, LANE)
    for l in range(levels):
        w_ref[l, :, pl.ds(dst, BLOCK)] = jnp.zeros((DEEP, BLOCK), BF16)
    s_ref[pl.ds(dst, BLOCK), :] = jnp.zeros((BLOCK, 2 * LANE), BF16)
    rc_ref[:, pl.ds(dst, BLOCK)] = jnp.zeros((8, BLOCK), F32)
    first = [number(0, p + 1) // LANE * LANE for p in range(rows)]
    last = [starts[-1] + number(len(priors) - 1, p) if p else starts[-1] for p in range(rows)]
    return off, first, last


def scratch(levels, window, slots):
    room = window * slots + BLOCK + 2 * LANE
    return [
        pltpu.VMEM((levels, DEEP, room), BF16),
        pltpu.VMEM((room, 2 * LANE), BF16),
        pltpu.VMEM((8, room), F32),
    ]


def triple(x):
    high, low = split(x)
    members, width = x.shape
    pad = jnp.zeros((DEEP - 3 * members, width), BF16)
    return jnp.concatenate([high, high, low, pad], axis=0).T


def points_kernel(geometry, window, id_ref, att_ref, seen_ref, *refs):
    levels, _, share, row_scale, col_scale = geometry
    priors, (out_ref, w_ref, s_ref, rc_ref, acc_ref) = refs[:window], refs[window:]
    groups, _, width = out_ref.shape
    off, _, _ = pack(geometry, id_ref, 0, priors, w_ref, s_ref, rc_ref)
    at = pl.multiple_of((id_ref[1] & 1) * width, width)
    x = jnp.concatenate([seen_ref[g, 0:share, pl.ds(at, width)] for g in range(groups)], axis=0)
    att = att_ref[:, pl.ds(at, width)]
    cells = triple(x)
    place = jnp.concatenate([att, jnp.zeros((LANE - 8, width), F32)], axis=0).T
    cell_row = place[:, 0:1] * row_scale
    cell_col = place[:, 1:2] * col_scale
    cell_lev = place[:, 2:3]
    acc_ref[...] = jnp.zeros(acc_ref.shape, F32)

    def body(b, _):
        at = pl.multiple_of(b * BLOCK, BLOCK)
        row_gap = cell_row - rc_ref[0:1, pl.ds(at, BLOCK)]
        col_gap = cell_col - rc_ref[1:2, pl.ds(at, BLOCK)]
        near = jnp.maximum(1.0 - row_gap * row_gap - col_gap * col_gap, 0.0)
        cov = jnp.zeros((width, BLOCK), F32)
        for l in range(levels):
            cov_l = jnp.dot(cells, w_ref[l, :, pl.ds(at, BLOCK)], preferred_element_type=F32)
            cov = jnp.where(cell_lev == float(l), cov_l, cov)
        high, low = split(cov * (near * near))
        s = s_ref[pl.ds(at, BLOCK), :]
        acc_ref[...] += jnp.dot(high, s, preferred_element_type=F32)
        acc_ref[:, 0:LANE] += jnp.dot(low, s[:, 0:LANE], preferred_element_type=F32)
        return 0

    lax.fori_loop(0, (off + BLOCK - 1) // BLOCK, body, 0)
    out = x + (acc_ref[:, 0:LANE] + acc_ref[:, LANE : 2 * LANE]).T[0 : groups * share]
    for g in range(groups):
        out_ref[g, 0:share, :] = out[g * share : (g + 1) * share]

        def put(rows, g=g):
            out_ref[g, share : share + SPARE, :] = rows

        counts = att_ref[5:6, 0:width]
        fill_spare(put, jnp.concatenate([att[0:5], counts, att[6:8]], axis=0), g % 2 == 1)


def update_points(geometry, ids, att, seen, priors):
    groups, padded, slots = seen.shape
    return pl.pallas_call(
        functools.partial(points_kernel, geometry, len(priors)),
        out_shape=jax.ShapeDtypeStruct((groups, padded, slots // 2), F32),
        in_specs=[SMEM] + [VMEM] * (2 + len(priors)),
        out_specs=VMEM,
        scratch_shapes=scratch(geometry[0], len(priors), slots)
        + [pltpu.VMEM((slots // 2, 2 * LANE), F32)],
        compiler_params=PARAMS,
        name="update_points",
    )(ids, att, seen, *priors)


def grid_kernel(geometry, window, groups, id_ref, *refs):
    levels, rows, share, row_scale, col_scale = geometry
    priors, refs = refs[:window], refs[window:]
    xs, outs, refs = refs[:groups], refs[groups : 2 * groups], refs[2 * groups :]
    w_ref, s_ref, rc_ref, xt_ref, acc_ref, q_ref = refs
    bands = xs[0].shape[0]
    height = levels * rows
    cols = bands * LANE
    members = groups * share
    _, first, last = pack(geometry, id_ref, id_ref[1], priors, w_ref, s_ref, rc_ref)
    q_ref[...] = (
        lax.broadcasted_iota(jnp.int32, (cols, LANE), 0) + id_ref[1] * cols
    ).astype(F32) * col_scale

    def cells(i):
        return jnp.concatenate(
            [
                jnp.concatenate(
                    [x.at[b][pl.ds(i, share, stride=height), :] for x in xs], axis=0
                )
                for b in range(bands)
            ],
            axis=1,
        )

    for i in range(height):
        xt_ref[i] = triple(cells(i))

    for p in range(rows):
        cell_row = (id_ref[0] * rows + p).astype(F32) * row_scale
        acc_ref[...] = jnp.zeros(acc_ref.shape, F32)

        def body(b, _, p=p, cell_row=cell_row):
            at = pl.multiple_of(first[p] + b * BLOCK, LANE)
            row_gap = cell_row - rc_ref[0:1, pl.ds(at, BLOCK)]
            base = 1.0 - row_gap * row_gap
            q = q_ref[...]
            col_gap = jnp.concatenate([q] * (BLOCK // LANE), axis=1) - rc_ref[1:2, pl.ds(at, BLOCK)]
            near = jnp.maximum(base - col_gap * col_gap, 0.0)
            taper = near * near
            s = s_ref[pl.ds(at, BLOCK), :]
            for l in range(levels):
                cov = jnp.dot(
                    xt_ref[l * rows + p], w_ref[l, :, pl.ds(at, BLOCK)], preferred_element_type=F32
                )
                high, low = split(cov * taper)
                acc_ref[l] += jnp.dot(high, s, preferred_element_type=F32)
                acc_ref[l, :, 0:LANE] += jnp.dot(low, s[:, 0:LANE], preferred_element_type=F32)
            return 0

        lax.fori_loop(0, jnp.maximum(last[p] - first[p] + BLOCK - 1, 0) // BLOCK, body, 0)
        for l in range(levels):
            at = pl.ds(l * rows + p, share, stride=height)
            inc = (acc_ref[l, :, 0:LANE] + acc_ref[l, :, LANE : 2 * LANE]).T[0:members]
            for g in range(groups):
                for b in range(bands):
                    outs[g].at[b][at, :] = (
                        xs[g].at[b][at, :]
                        + inc[g * share : (g + 1) * share, b * LANE : (b + 1) * LANE]
                    )


def update_grid(geometry, ids, priors, parts):
    levels, rows = geometry[:2]
    halves, groups, _, width = priors[0].shape
    cols = parts[0].shape[0] * LANE
    return pl.pallas_call(
        functools.partial(grid_kernel, geometry, len(priors), groups),
        out_shape=[jax.ShapeDtypeStruct(parts[0].shape, F32)] * groups,
        in_specs=[SMEM] + [VMEM] * (len(priors) + groups),
        out_specs=[VMEM] * groups,
        scratch_shapes=scratch(levels, len(priors), halves * width)
        + [
            pltpu.VMEM((levels * rows, cols, DEEP), BF16),
            pltpu.VMEM((levels, cols, 2 * LANE), F32),
            pltpu.VMEM((cols, LANE), F32),
        ],
        compiler_params=PARAMS,
        name="update_grid",
    )(ids, *priors, *parts)


def restore_kernel(id_ref, *refs):
    parts, out_ref = refs[:-1], refs[-1]
    members, levels, rows, cols = out_ref.shape
    bands = parts[0].shape[0]
    height = levels * rows

    def body(m, _):
        at = pl.multiple_of(m * height, height)
        for k, part in enumerate(parts):
            for band in range(bands):
                block = part[band, pl.ds(at, height), :]
                first = pl.multiple_of((id_ref[1] ^ k) * (bands * LANE) + band * LANE, LANE)
                for l in range(levels):
                    out_ref[m, l, :, pl.ds(first, LANE)] = block[l * rows : (l + 1) * rows]
        return 0

    lax.fori_loop(0, members, body, 0)


def restore(ids, parts, shape):
    return pl.pallas_call(
        restore_kernel,
        out_shape=jax.ShapeDtypeStruct(shape, F32),
        in_specs=[SMEM] + [VMEM] * len(parts),
        out_specs=VMEM,
        compiler_params=PARAMS,
        name="restore",
    )(ids, *parts)


def shifted(value, steps):
    count = lax.axis_size("tile")
    pairs = [(i, i + steps) for i in range(count) if 0 <= i + steps < count]
    return lax.ppermute(value, "tile", pairs)


def window_of(value):
    far = {d: shifted(value, -d) for n in range(REACH, 0, -1) for d in (n, -n)}
    far[0] = value
    return [far[d] for d in range(-REACH, REACH + 1)]


def crossed(value, step):
    count = lax.axis_size("ens")
    return lax.ppermute(value, "ens", [(i, i ^ step) for i in range(count)])


def exchanged(parts):
    return [parts[0]] + [crossed(parts[k], k) for k in range(1, len(parts))]


def on_device(initial_sample_set, flow_velocity, obs_loc, obs_count, obs_value, obs_error):
    x = initial_sample_set
    share, levels, rows, col_total = x.shape
    ens = lax.axis_size("ens")
    ids = jnp.stack([lax.axis_index("tile"), lax.axis_index("ens")]).astype(jnp.int32)
    geometry = (levels, rows, share, 1.0 / (REACH * rows), 1.0 / (col_total // 2))

    top = shifted(x[:, :, rows - 1, :], 1)
    bottom = shifted(x[:, :, 0, :], -1)
    att = order(ids, obs_loc, obs_value, obs_error, obs_count, rows)
    parts = forecast(ids, x, top, bottom, flow_velocity, ens)
    seen = observe(ids, att, parts, levels * rows, share)
    seen = lax.all_gather(seen, "ens", axis=0)
    priors = window_of(seen[:, 0][None])
    parts, _ = lax.optimization_barrier((parts, seen))
    parts = exchanged(parts)
    later = update_points(geometry, ids, att[1], seen[:, 1], priors)
    later = window_of(jnp.stack([later, crossed(later, 1)]))
    parts = update_grid(geometry, ids, priors, parts)
    parts = update_grid(geometry, ids, later, parts)
    return restore(ids, exchanged(parts), x.shape)


def solution(mesh):
    in_specs = (
        P("ens", None, "tile", None),
        P(None, None, "tile", None),
        P(None, None, "tile"),
        P(None, "tile"),
        P(None, "tile"),
        P(None, "tile"),
    )
    out_specs = P("ens", None, "tile", None)
    return jax.shard_map(
        on_device, mesh=mesh, in_specs=in_specs, out_specs=out_specs, check_vma=False
    )
```

```python
import functools

import jax
import jax.numpy as jnp
from jax import lax
from jax.experimental import pallas as pl
from jax.experimental.pallas import tpu as pltpu
from jax.sharding import PartitionSpec as P

BATCHES = 2
REACH = 2
SPARE = 4
SPREAD_RATE = 0.05
EPSILON = 1e-06
LANE = 128
DEEP = 256
BLOCK = 512
F32 = jnp.float32
BF16 = jnp.bfloat16
VMEM = pl.BlockSpec(memory_space=pltpu.VMEM)
SMEM = pl.BlockSpec(memory_space=pltpu.SMEM)
PARAMS = pltpu.CompilerParams(vmem_limit_bytes=32 << 20)


def cost(micros):
    return pl.CostEstimate(flops=int(micros * 1e9), bytes_accessed=0, transcendentals=0)


def split(value):
    high = value.astype(BF16)
    return high, (value - high.astype(F32)).astype(BF16)


def order_kernel(rows, id_ref, loc_ref, value_ref, error_ref, count_ref, att_ref):
    batches, slots = value_ref.shape
    earlier = (
        lax.broadcasted_iota(jnp.int32, (slots, slots), 0)
        < lax.broadcasted_iota(jnp.int32, (slots, slots), 1)
    ).astype(BF16)
    slot = lax.broadcasted_iota(jnp.int32, (1, slots), 1)
    key_of = lax.broadcasted_iota(jnp.int32, (8, slots), 0)
    for b in range(batches):
        count = count_ref[b, 0]
        local_row = loc_ref[0, b : b + 1, :] - id_ref[0] * rows
        key = jnp.where(slot < count, local_row, rows)
        mine = key_of == jnp.broadcast_to(key, (8, slots))
        ones = mine.astype(F32)
        before = jnp.dot(ones.astype(BF16), earlier, preferred_element_type=F32)
        totals = jnp.sum(ones, axis=1, keepdims=True)
        start = jnp.zeros((1, slots), F32)
        place = jnp.zeros((1, slots), F32)
        cumulative = jnp.where(slot == 0, count.astype(F32), 0.0)
        for r in range(rows + 1):
            place = place + ones[r : r + 1] * (before[r : r + 1] + start)
            start = start + totals[r : r + 1]
            cumulative = jnp.where(slot == r + 1, start, cumulative)
        level = loc_ref[2, b : b + 1, :]
        fields = [
            loc_ref[0, b : b + 1, :].astype(F32),
            loc_ref[1, b : b + 1, :].astype(F32),
            level.astype(F32),
            value_ref[b : b + 1, :],
            error_ref[b : b + 1, :],
            (level * rows + local_row).astype(F32),
        ]
        table = jnp.concatenate(fields + [jnp.zeros((2, slots), F32)], axis=0)
        high, low = split(table)
        rest = (table - high.astype(F32) - low.astype(F32)).astype(BF16)
        target = lax.broadcasted_iota(jnp.int32, (slots, slots), 0)
        moved = (target == jnp.broadcast_to(place.astype(jnp.int32), (slots, slots))).astype(BF16)
        out = lax.dot_general(
            jnp.concatenate([high.astype(F32), low.astype(F32), rest.astype(F32)], axis=0).astype(BF16),
            moved,
            (((1,), (1,)), ((), ())),
            preferred_element_type=F32,
        )
        out = (out[0:8] + out[8:16]) + out[16:24]
        att_ref[b] = jnp.concatenate([out[0:5], cumulative, out[5:6], jnp.zeros((1, slots), F32)], axis=0)


def order(ids, obs_loc, obs_value, obs_error, obs_count, rows):
    batches, slots = obs_value.shape
    return pl.pallas_call(
        functools.partial(order_kernel, rows),
        out_shape=jax.ShapeDtypeStruct((batches, 8, slots), F32),
        in_specs=[SMEM, VMEM, VMEM, VMEM, SMEM],
        out_specs=VMEM,
        compiler_params=PARAMS,
        cost_estimate=cost(2),
        name="order",
    )(ids, obs_loc, obs_value, obs_error, obs_count)


def forecast_kernel(id_ref, x_ref, top_ref, bottom_ref, flow_ref, *refs):
    outs, row_ref = refs[:-1], refs[-1]
    members, levels, rows, cols = x_ref.shape
    height = levels * rows
    parts, bands = len(outs), outs[0].shape[0]
    row = lax.broadcasted_iota(jnp.int32, (height, cols), 0)
    col = lax.broadcasted_iota(jnp.int32, (height, cols), 1)
    winds = [
        jnp.concatenate([flow_ref[d, l] for l in range(levels)], axis=0) for d in range(2)
    ]

    def body(m, _):
        x = jnp.concatenate([x_ref[m, l] for l in range(levels)], axis=0)
        above = pltpu.roll(x, 1, 0)
        below = pltpu.roll(x, height - 1, 0)
        for l in range(levels):
            above = jnp.where(row == l * rows, top_ref[m, l : l + 1, :], above)
            below = jnp.where(row == (l + 1) * rows - 1, bottom_ref[m, l : l + 1, :], below)
        left = jnp.where(col == 0, 0.0, pltpu.roll(x, 1, 1))
        right = jnp.where(col == cols - 1, 0.0, pltpu.roll(x, cols - 1, 1))
        tendency = (
            jnp.maximum(winds[0], 0.0) * (x - above)
            + jnp.minimum(winds[0], 0.0) * (below - x)
            + jnp.maximum(winds[1], 0.0) * (x - left)
            + jnp.minimum(winds[1], 0.0) * (right - x)
        )
        row_ref[...] = x - tendency + SPREAD_RATE * (above + below + left + right - 4.0 * x)
        at = pl.multiple_of(m * height, height)
        for k in range(parts):
            first = (id_ref[1] ^ k) * (bands * LANE)
            for band in range(bands):
                source = pl.multiple_of(first + band * LANE, LANE)
                outs[k][band, pl.ds(at, height), :] = row_ref[:, pl.ds(source, LANE)]
        return 0

    lax.fori_loop(0, members, body, 0)


def forecast(ids, x, top, bottom, flow, parts):
    members, levels, rows, cols = x.shape
    out = jax.ShapeDtypeStruct((cols // parts // LANE, members * levels * rows, LANE), F32)
    return pl.pallas_call(
        forecast_kernel,
        out_shape=[out] * parts,
        in_specs=[SMEM] + [VMEM] * 4,
        out_specs=[VMEM] * parts,
        scratch_shapes=[pltpu.VMEM((levels * rows, cols), F32)],
        compiler_params=PARAMS,
        cost_estimate=cost(3),
        name="forecast",
    )(ids, x, top, bottom, flow)


def fill_spare(put, att, odd):
    even_rows = jnp.concatenate([att[0:3], att[5:6]], axis=0)
    odd_rows = jnp.concatenate([att[3:5], att[3:5]], axis=0)
    put(jnp.where(odd, odd_rows, even_rows))


def number(row, at):
    lane = lax.broadcasted_iota(jnp.int32, (1, LANE), 1)
    return jnp.sum(jnp.where(lane == at, row, 0.0)).astype(jnp.int32)


def observe_kernel(levels, share, id_ref, att_ref, *refs):
    parts, out_ref = refs[:-1], refs[-1]
    bands = parts[0].shape[0]
    batches, _, slots = att_ref.shape
    height = parts[0].shape[1] // share
    rows = height // levels
    for b in range(batches):
        att = att_ref[b]
        counts = att[5:6, 0:LANE]
        odd = (id_ref[1] & 1) == 1

        def put(rows, b=b):
            out_ref[b, share : share + SPARE, :] = rows

        fill_spare(put, att, odd)

        count = number(counts, 0)
        ends = [number(counts, r + 1) for r in range(rows)]

        def body(n, _, b=b, count=count, ends=ends):
            at = pl.multiple_of(n * LANE, LANE)
            begin, end = n * LANE, jnp.minimum(n * LANE + LANE, count) - 1
            low = sum((e <= begin).astype(jnp.int32) for e in ends)
            high = sum((e <= end).astype(jnp.int32) for e in ends)
            column = att_ref[b, 1:2, pl.ds(at, LANE)].astype(jnp.int32)
            flat_row = jnp.broadcast_to(att_ref[b, 6:7, pl.ds(at, LANE)].astype(jnp.int32), (8, LANE))
            band_of = jnp.broadcast_to(column >> 7, (8, LANE))
            lane_of = jnp.broadcast_to(column & (LANE - 1), (8, LANE))
            here = [
                band_of == (id_ref[1] ^ k) * bands + band
                for k in range(len(parts))
                for band in range(bands)
            ]

            def one_row(r, found):
                found = list(found)
                for l in range(levels):
                    i = l * rows + r
                    mine = flat_row == i
                    for c, m in enumerate(range(0, share, 8)):
                        size = min(8, share - m)
                        value = jnp.zeros((8, LANE), F32)
                        for j in range(len(parts) * bands):
                            block = parts[j // bands].at[j % bands][
                                pl.ds(m * height + i, size, stride=height), :
                            ]
                            if size < 8:
                                block = jnp.concatenate(
                                    [block, jnp.zeros((8 - size, LANE), F32)], axis=0
                                )
                            picked = jnp.take_along_axis(block, lane_of, axis=1)
                            value = jnp.where(here[j], picked, value)
                        found[c] = jnp.where(mine, value, found[c])
                return tuple(found)

            found = lax.fori_loop(
                low, high + 1, one_row, (jnp.zeros((8, LANE), F32),) * ((share + 7) // 8)
            )
            for c, m in enumerate(range(0, share, 8)):
                size = min(8, share - m)
                out_ref[b, m : m + size, pl.ds(at, LANE)] = found[c][0:size]
            return 0

        out_ref[b, 0:share, :] = jnp.zeros((share, slots), F32)
        lax.fori_loop(0, (count + LANE - 1) // LANE, body, 0)


def observe(ids, att, parts, levels, share):
    batches, _, slots = att.shape
    padded = (share + SPARE + 7) // 8 * 8
    return pl.pallas_call(
        functools.partial(observe_kernel, levels, share),
        out_shape=jax.ShapeDtypeStruct((batches, padded, slots), F32),
        in_specs=[SMEM] + [VMEM] * (1 + len(parts)),
        out_specs=VMEM,
        compiler_params=PARAMS,
        cost_estimate=cost(5),
        name="observe",
    )(ids, att, *parts)


def weigh(prior, value, error, live):
    members = prior.shape[0]
    average = jnp.sum(prior, axis=0, keepdims=True) / members
    deviation = prior - average
    var_prior = jnp.sum(deviation * deviation, axis=0, keepdims=True) / (members - 1) + EPSILON
    combined = var_prior + error
    shrink = jnp.sqrt(error / combined)
    post = (error * average + var_prior * value) / combined
    shift = live * ((shrink - 1.0) * deviation + (post - average))
    weight = (live / ((members - 1) * var_prior)) * deviation
    return weight, shift


def pack_kernel(geometry, window, id_ref, *refs):
    priors, (w_ref, s_ref, rc_ref, span_ref) = refs[:window], refs[window:]
    levels, rows, share, row_scale, col_scale = geometry
    halves, groups, _, width = priors[0].shape
    chunk = min(2 * LANE, width)
    counts = [ref[0, 0, share + 3 : share + 4, 0:LANE] for ref in priors]

    totals = [number(row, 0) for row in counts]
    for p in range(rows):
        span_ref[p] = number(counts[0], p + 1) // LANE * LANE
        span_ref[rows + p] = number(counts[-1], p) if p else jnp.int32(0)
    off = jnp.int32(0)
    starts = []
    for t, ref in enumerate(priors):
        count = totals[t]
        starts.append(off)

        def body(k, _, ref=ref, off=off, count=count):
            src = k * chunk
            half = (k ^ id_ref[1]) & (halves - 1)
            at = pl.multiple_of((k // halves) * chunk, chunk)
            dst = pl.multiple_of(off + src, LANE)
            slot = lax.broadcasted_iota(jnp.int32, (1, chunk), 1) + src
            live = (slot < count).astype(F32)
            prior = jnp.concatenate(
                [ref[half, id_ref[1] ^ g, 0:share, pl.ds(at, chunk)] for g in range(groups)], axis=0
            )
            place = ref[half, 0, share : share + SPARE, pl.ds(at, chunk)]
            seen = ref[half, 1, share : share + SPARE, pl.ds(at, chunk)]
            members = prior.shape[0]
            weight, shift = weigh(prior, seen[0:1], seen[1:2], live)
            pad = jnp.zeros((DEEP - 3 * members, chunk), BF16)
            for l in range(levels):
                high, low = split(weight * (1.0 / (1.0 + jnp.abs(place[2:3] - float(l)))))
                w_ref[l, :, pl.ds(dst, chunk)] = jnp.concatenate([high, low, high, pad], axis=0)
            turned = jnp.concatenate([shift, jnp.zeros((LANE - members, chunk), F32)], axis=0).T
            high, low = split(turned)
            s_ref[pl.ds(dst, chunk), 0:LANE] = high
            s_ref[pl.ds(dst, chunk), LANE : 2 * LANE] = low
            rc_ref[0:1, pl.ds(dst, chunk)] = place[0:1] * row_scale
            rc_ref[1:2, pl.ds(dst, chunk)] = place[1:2] * col_scale
            rc_ref[2:3, pl.ds(dst, chunk)] = place[2:3]
            return 0

        lax.fori_loop(0, (count + chunk - 1) // chunk, body, 0)
        off = off + (count + LANE - 1) // LANE * LANE
    dst = pl.multiple_of(off, LANE)
    for l in range(levels):
        w_ref[l, :, pl.ds(dst, 2 * BLOCK)] = jnp.zeros((DEEP, 2 * BLOCK), BF16)
    s_ref[pl.ds(dst, 2 * BLOCK), :] = jnp.zeros((2 * BLOCK, 2 * LANE), BF16)
    rc_ref[:, pl.ds(dst, 2 * BLOCK)] = jnp.zeros((8, 2 * BLOCK), F32)
    for p in range(rows):
        span_ref[rows + p] = starts[-1] + span_ref[rows + p]
    span_ref[2 * rows] = off


def pack(geometry, ids, priors):
    levels, rows = geometry[:2]
    halves, _, _, width = priors[0].shape
    room = len(priors) * halves * width + 2 * BLOCK + 2 * LANE
    return pl.pallas_call(
        functools.partial(pack_kernel, geometry, len(priors)),
        out_shape=[
            jax.ShapeDtypeStruct((levels, DEEP, room), BF16),
            jax.ShapeDtypeStruct((room, 2 * LANE), BF16),
            jax.ShapeDtypeStruct((8, room), F32),
            jax.ShapeDtypeStruct((2 * rows + 1,), jnp.int32),
        ],
        in_specs=[SMEM] + [VMEM] * len(priors),
        out_specs=[VMEM, VMEM, VMEM, SMEM],
        compiler_params=PARAMS,
        cost_estimate=cost(5),
        name="pack",
    )(ids, *priors)


def triple(x):
    high, low = split(x)
    members, width = x.shape
    pad = jnp.zeros((DEEP - 3 * members, width), BF16)
    return jnp.concatenate([high, high, low, pad], axis=0).T


def points_kernel(
    geometry, id_ref, span_ref, att_ref, seen_ref, w_ref, s_ref, rc_ref, out_ref, acc_ref
):
    levels, rows, share, row_scale, col_scale = geometry
    groups, _, width = out_ref.shape
    chunk = min(2 * LANE, width)
    off = span_ref[2 * rows]
    counts = att_ref[5:6, 0:LANE]
    live = number(counts, 0)
    for c in range(width // chunk):
        lanes = slice(c * chunk, (c + 1) * chunk)
        begin = (2 * c + (id_ref[1] & 1)) * chunk
        at = pl.multiple_of(begin, chunk)
        att = att_ref[:, pl.ds(at, chunk)]
        for g in range(groups):

            def put(rows, g=g):
                out_ref[g, share : share + SPARE, lanes] = rows

            rest = jnp.zeros((1, chunk - LANE), F32)
            head = jnp.concatenate([counts, rest], axis=1) if chunk > LANE else counts
            fill_spare(put, jnp.concatenate([att[0:5], head, att[6:8]], axis=0), g % 2 == 1)

        @pl.when(begin >= live)
        def _():
            for g in range(groups):
                out_ref[g, 0:share, lanes] = jnp.zeros((share, chunk), F32)

        @pl.when(begin < live)
        def _():
            x = jnp.concatenate(
                [seen_ref[id_ref[1] ^ g, 0:share, pl.ds(at, chunk)] for g in range(groups)],
                axis=0,
            )
            cells = triple(x)
            place = jnp.concatenate([att, jnp.zeros((LANE - 8, chunk), F32)], axis=0).T
            cell_row = place[:, 0:1] * row_scale
            cell_col = place[:, 1:2] * col_scale
            cell_lev = place[:, 2:3]
            acc_ref[...] = jnp.zeros(acc_ref.shape, F32)

            def body(b, _):
                at = pl.multiple_of(b * BLOCK, BLOCK)
                row_gap = cell_row - rc_ref[0:1, pl.ds(at, BLOCK)]
                col_gap = cell_col - rc_ref[1:2, pl.ds(at, BLOCK)]
                near = jnp.maximum(1.0 - row_gap * row_gap - col_gap * col_gap, 0.0)
                level = rc_ref[2:3, pl.ds(at, BLOCK)]
                ratio = jnp.ones((chunk, BLOCK), F32)
                for l in range(1, levels):
                    other = (1.0 + level) / (1.0 + jnp.abs(level - float(l)))
                    ratio = jnp.where(cell_lev == float(l), other, ratio)
                cov = jnp.dot(cells, w_ref[0, :, pl.ds(at, BLOCK)], preferred_element_type=F32)
                high, low = split(cov * (near * near) * ratio)
                s = s_ref[pl.ds(at, BLOCK), :]
                acc_ref[...] += jnp.dot(high, s, preferred_element_type=F32)
                acc_ref[:, 0:LANE] += jnp.dot(low, s[:, 0:LANE], preferred_element_type=F32)
                return 0

            def pair(b, _):
                body(2 * b, 0)
                body(2 * b + 1, 0)
                return 0

            lax.fori_loop(0, (off + 2 * BLOCK - 1) // (2 * BLOCK), pair, 0)
            out = x + (acc_ref[:, 0:LANE] + acc_ref[:, LANE : 2 * LANE]).T[0 : groups * share]
            for g in range(groups):
                out_ref[id_ref[1] ^ g, 0:share, lanes] = out[g * share : (g + 1) * share]


def update_points(geometry, ids, att, seen, packed):
    w, s, rc, span = packed
    groups, padded, slots = seen.shape
    return pl.pallas_call(
        functools.partial(points_kernel, geometry),
        out_shape=jax.ShapeDtypeStruct((groups, padded, slots // 2), F32),
        in_specs=[SMEM] * 2 + [VMEM] * 5,
        out_specs=VMEM,
        scratch_shapes=[pltpu.VMEM((min(2 * LANE, slots // 2), 2 * LANE), F32)],
        compiler_params=PARAMS,
        cost_estimate=cost(8),
        name="update_points",
    )(ids, span, att, seen, w, s, rc)


def grid_kernel(geometry, begin, groups, id_ref, span_ref, w_ref, s_ref, rc_ref, *refs):
    levels, all_rows, share, row_scale, col_scale = geometry
    xs, outs, refs = refs[:groups], refs[groups : 2 * groups], refs[2 * groups :]
    xt_ref, acc_ref, q_ref, high_ref, low_ref = refs
    bands = xs[0].shape[0]
    height = levels * all_rows
    rows = outs[0].shape[1] // (share * levels)
    first = [span_ref[begin + p] for p in range(rows)]
    last = [span_ref[all_rows + begin + p] for p in range(rows)]
    cols = bands * LANE
    members = groups * share
    q_ref[...] = (
        lax.broadcasted_iota(jnp.int32, (cols, LANE), 0) + id_ref[1] * cols
    ).astype(F32) * col_scale

    def cells(i):
        return jnp.concatenate(
            [
                jnp.concatenate(
                    [x.at[b][pl.ds(i, share, stride=height), :] for x in xs], axis=0
                )
                for b in range(bands)
            ],
            axis=1,
        )

    for l in range(levels):
        for p in range(rows):
            xt_ref[l * rows + p] = triple(cells(l * all_rows + begin + p))

    steps = [jnp.maximum(last[p] - first[p] + BLOCK - 1, 0) // BLOCK for p in range(rows)]
    ends = [steps[0]]
    for n in steps[1:]:
        ends.append(ends[-1] + n)
    acc_ref[...] = jnp.zeros(acc_ref.shape, F32)

    def locate(i):
        p = jnp.int32(0)
        at = first[0] + i * BLOCK
        for j in range(1, rows):
            past = i >= ends[j - 1]
            p = jnp.where(past, j, p)
            at = jnp.where(past, first[j] + (i - ends[j - 1]) * BLOCK, at)
        return p, pl.multiple_of(at, LANE)

    def spread(i, l):
        p, at = locate(i)
        s = s_ref[pl.ds(at, BLOCK), :]
        acc_ref[p, l] += jnp.dot(high_ref[l], s, preferred_element_type=F32)
        acc_ref[p, l, :, 0:LANE] += jnp.dot(low_ref[l], s[:, 0:LANE], preferred_element_type=F32)

    def step(i, _):
        p, at = locate(i)
        row_gap = (id_ref[0] * all_rows + begin + p).astype(F32) * row_scale - rc_ref[0:1, pl.ds(at, BLOCK)]
        base = 1.0 - row_gap * row_gap
        q = q_ref[...]
        col_gap = jnp.concatenate([q] * (BLOCK // LANE), axis=1) - rc_ref[1:2, pl.ds(at, BLOCK)]
        near = jnp.maximum(base - col_gap * col_gap, 0.0)
        taper = near * near
        for l in range(levels):
            cov = jnp.dot(
                xt_ref[l * rows + p], w_ref[l, :, pl.ds(at, BLOCK)], preferred_element_type=F32
            )
            high, low = split(cov * taper)
            if l == 0:
                spread(jnp.maximum(i - 1, 0), levels - 1)
            else:
                spread(i, l - 1)
            high_ref[l], low_ref[l] = high, low
        return 0

    high_ref[levels - 1] = jnp.zeros(high_ref.shape[1:], BF16)
    low_ref[levels - 1] = jnp.zeros(low_ref.shape[1:], BF16)
    def pair(i, _):
        step(2 * i, 0)
        step(2 * i + 1, 0)
        return 0

    pairs = (ends[-1] + 1) // 2
    lax.fori_loop(0, pairs, pair, 0)
    spread(jnp.maximum(2 * pairs - 1, 0), levels - 1)

    def store(p, _):
        for l in range(levels):
            at = pl.ds(l * all_rows + begin + p, share, stride=height)
            to = pl.ds(l * rows + p, share, stride=levels * rows)
            inc = (acc_ref[p, l, :, 0:LANE] + acc_ref[p, l, :, LANE : 2 * LANE]).T[0:members]
            for g in range(groups):
                for b in range(bands):
                    outs[g].at[b][to, :] = (
                        xs[g].at[b][at, :]
                        + inc[g * share : (g + 1) * share, b * LANE : (b + 1) * LANE]
                    )
        return 0

    lax.fori_loop(0, rows, store, 0)


def update_grid(geometry, ids, packed, parts, begin, rows):
    w, s, rc, span = packed
    levels, all_rows = geometry[:2]
    groups = len(parts)
    bands, depth, _ = parts[0].shape
    cols = bands * LANE
    out = jax.ShapeDtypeStruct((bands, depth // all_rows * rows, LANE), F32)
    return pl.pallas_call(
        functools.partial(grid_kernel, geometry, begin, groups),
        out_shape=[out] * groups,
        in_specs=[SMEM] * 2 + [VMEM] * (3 + groups),
        out_specs=[VMEM] * groups,
        scratch_shapes=[
            pltpu.VMEM((levels * rows, cols, DEEP), BF16),
            pltpu.VMEM((rows, levels, cols, 2 * LANE), F32),
            pltpu.VMEM((cols, LANE), F32),
            pltpu.VMEM((levels, cols, BLOCK), BF16),
            pltpu.VMEM((levels, cols, BLOCK), BF16),
        ],
        compiler_params=PARAMS,
        cost_estimate=cost(7 * rows),
        name="update_grid",
    )(ids, span, w, s, rc, *parts)


def restore_kernel(groups, id_ref, *refs):
    pieces, befores, out_ref = refs[:groups], refs[groups:-1], refs[-1]
    members, levels, all_rows, _ = out_ref.shape
    bands = pieces[0].shape[0]
    height = pieces[0].shape[1] // members
    rows = height // levels
    begin = all_rows - rows

    def body(m, _):
        at = pl.multiple_of(m * height, height)
        for before in befores:
            for l in range(levels):
                out_ref[m, l, 0:begin, :] = before[m, l]
        for k in range(groups):
            for band in range(bands):
                block = pieces[k][band, pl.ds(at, height), :]
                first = pl.multiple_of((id_ref[1] ^ k) * (bands * LANE) + band * LANE, LANE)
                for l in range(levels):
                    out_ref[m, l, begin:all_rows, pl.ds(first, LANE)] = block[
                        l * rows : (l + 1) * rows
                    ]
        return 0

    lax.fori_loop(0, members, body, 0)


def restore(ids, pieces, befores, shape):
    return pl.pallas_call(
        functools.partial(restore_kernel, len(pieces)),
        out_shape=jax.ShapeDtypeStruct(shape, F32),
        in_specs=[SMEM] + [VMEM] * (len(pieces) + len(befores)),
        out_specs=VMEM,
        compiler_params=PARAMS,
        cost_estimate=cost(2),
        name="restore",
    )(ids, *pieces, *befores)


def shifted(value, steps):
    count = lax.axis_size("tile")
    pairs = [(i, i + steps) for i in range(count) if 0 <= i + steps < count]
    return lax.ppermute(value, "tile", pairs)


def paired(value, odd):
    count = lax.axis_size("tile")
    firsts = range(odd, count - 1, 2)
    pairs = [(i, i + 1) for i in firsts] + [(i + 1, i) for i in firsts]
    return lax.ppermute(value, "tile", pairs)


def window_of(value):
    return [
        shifted(value, 2),
        paired(value, 0),
        value,
        paired(value, 1),
        shifted(value, -2),
    ]


def crossed(value, step):
    count = lax.axis_size("ens")
    return lax.ppermute(value, "ens", [(i, i ^ step) for i in range(count)])


def exchanged(parts):
    return [parts[0]] + [crossed(parts[k], k) for k in range(1, len(parts))]


def on_device(initial_sample_set, flow_velocity, obs_loc, obs_count, obs_value, obs_error):
    x = initial_sample_set
    share, levels, rows, col_total = x.shape
    ens = lax.axis_size("ens")
    ids = jnp.stack([lax.axis_index("tile"), lax.axis_index("ens")]).astype(jnp.int32)
    geometry = (levels, rows, share, 1.0 / (REACH * rows), 1.0 / (col_total // 2))

    top = shifted(x[:, :, rows - 1, :], 1)
    bottom = shifted(lax.optimization_barrier(x)[:, :, 0, :], -1)
    att = order(ids, obs_loc, obs_value, obs_error, obs_count, rows)
    parts = forecast(ids, x, top, bottom, flow_velocity, ens)
    seen = observe(ids, att, parts, levels, share)
    seen = lax.all_gather(seen, "ens", axis=0)
    priors = window_of(seen[:, 0][None])
    parts, _ = lax.optimization_barrier((parts, seen))
    parts = exchanged(parts)
    priors, parts = lax.optimization_barrier((priors, parts))
    packed = pack(geometry, ids, priors)
    later = update_points(geometry, ids, att[1], seen[:, 1], packed)
    later = window_of(jnp.stack([later, crossed(later, 1)]))
    parts = update_grid(geometry, ids, packed, parts, 0, rows)
    packed = pack(geometry, ids, later)
    half = rows // 2
    upper = update_grid(geometry, ids, packed, parts, 0, half)
    parts, upper = lax.optimization_barrier((parts, upper))
    lower = update_grid(geometry, ids, packed, parts, half, rows - half)
    done = restore(ids, exchanged(upper), (), (share, levels, half, col_total))
    return restore(ids, exchanged(lower), (done,), x.shape)


def solution(mesh):
    in_specs = (
        P("ens", None, "tile", None),
        P(None, None, "tile", None),
        P(None, None, "tile"),
        P(None, "tile"),
        P(None, "tile"),
        P(None, "tile"),
    )
    out_specs = P("ens", None, "tile", None)
    return jax.shard_map(
        on_device, mesh=mesh, in_specs=in_specs, out_specs=out_specs, check_vma=False
    )
```

```python
import functools

import jax
import jax.numpy as jnp
from jax import lax
from jax.experimental import pallas as pl
from jax.experimental.pallas import tpu as pltpu
from jax.sharding import PartitionSpec as P

BATCHES = 2
REACH = 2
SPARE = 4
SPREAD_RATE = 0.05
EPSILON = 1e-06
LANE = 128
DEEP = 256
BLOCK = 512
F32 = jnp.float32
BF16 = jnp.bfloat16
VMEM = pl.BlockSpec(memory_space=pltpu.VMEM)
SMEM = pl.BlockSpec(memory_space=pltpu.SMEM)
PARAMS = pltpu.CompilerParams(vmem_limit_bytes=32 << 20)


def cost(micros):
    return pl.CostEstimate(flops=int(micros * 1e9), bytes_accessed=0, transcendentals=0)


def split(value):
    high = value.astype(BF16)
    return high, (value - high.astype(F32)).astype(BF16)


def order_kernel(rows, id_ref, loc_ref, value_ref, error_ref, count_ref, att_ref):
    batches, slots = value_ref.shape
    earlier = (
        lax.broadcasted_iota(jnp.int32, (slots, slots), 0)
        < lax.broadcasted_iota(jnp.int32, (slots, slots), 1)
    ).astype(BF16)
    slot = lax.broadcasted_iota(jnp.int32, (1, slots), 1)
    key_of = lax.broadcasted_iota(jnp.int32, (8, slots), 0)
    for b in range(batches):
        count = count_ref[b, 0]
        local_row = loc_ref[0, b : b + 1, :] - id_ref[0] * rows
        key = jnp.where(slot < count, local_row, rows)
        mine = key_of == jnp.broadcast_to(key, (8, slots))
        ones = mine.astype(F32)
        before = jnp.dot(ones.astype(BF16), earlier, preferred_element_type=F32)
        totals = jnp.sum(ones, axis=1, keepdims=True)
        start = jnp.zeros((1, slots), F32)
        place = jnp.zeros((1, slots), F32)
        cumulative = jnp.where(slot == 0, count.astype(F32), 0.0)
        for r in range(rows + 1):
            place = place + ones[r : r + 1] * (before[r : r + 1] + start)
            start = start + totals[r : r + 1]
            cumulative = jnp.where(slot == r + 1, start, cumulative)
        level = loc_ref[2, b : b + 1, :]
        fields = [
            loc_ref[0, b : b + 1, :].astype(F32),
            loc_ref[1, b : b + 1, :].astype(F32),
            level.astype(F32),
            value_ref[b : b + 1, :],
            error_ref[b : b + 1, :],
            (level * rows + local_row).astype(F32),
        ]
        table = jnp.concatenate(fields + [jnp.zeros((2, slots), F32)], axis=0)
        high, low = split(table)
        rest = (table - high.astype(F32) - low.astype(F32)).astype(BF16)
        target = lax.broadcasted_iota(jnp.int32, (slots, slots), 0)
        moved = (target == jnp.broadcast_to(place.astype(jnp.int32), (slots, slots))).astype(BF16)
        out = lax.dot_general(
            jnp.concatenate([high.astype(F32), low.astype(F32), rest.astype(F32)], axis=0).astype(BF16),
            moved,
            (((1,), (1,)), ((), ())),
            preferred_element_type=F32,
        )
        out = (out[0:8] + out[8:16]) + out[16:24]
        att_ref[b] = jnp.concatenate([out[0:5], cumulative, out[5:6], jnp.zeros((1, slots), F32)], axis=0)


def order(ids, obs_loc, obs_value, obs_error, obs_count, rows):
    batches, slots = obs_value.shape
    return pl.pallas_call(
        functools.partial(order_kernel, rows),
        out_shape=jax.ShapeDtypeStruct((batches, 8, slots), F32),
        in_specs=[SMEM, VMEM, VMEM, VMEM, SMEM],
        out_specs=VMEM,
        compiler_params=PARAMS,
        cost_estimate=cost(2),
        name="order",
    )(ids, obs_loc, obs_value, obs_error, obs_count)


def forecast_kernel(id_ref, x_ref, flow_ref, *refs):
    outs, row_ref = refs[:-1], refs[-1]
    members, levels, rows, cols = x_ref.shape
    height = levels * rows
    parts, bands = len(outs), outs[0].shape[0]
    row = lax.broadcasted_iota(jnp.int32, (height, cols), 0)
    col = lax.broadcasted_iota(jnp.int32, (height, cols), 1)
    winds = [
        jnp.concatenate([flow_ref[d, l] for l in range(levels)], axis=0) for d in range(2)
    ]

    def body(m, _):
        x = jnp.concatenate([x_ref[m, l] for l in range(levels)], axis=0)
        above = jnp.where(row % rows == 0, 0.0, pltpu.roll(x, 1, 0))
        below = jnp.where(row % rows == rows - 1, 0.0, pltpu.roll(x, height - 1, 0))
        left = jnp.where(col == 0, 0.0, pltpu.roll(x, 1, 1))
        right = jnp.where(col == cols - 1, 0.0, pltpu.roll(x, cols - 1, 1))
        tendency = (
            jnp.maximum(winds[0], 0.0) * (x - above)
            + jnp.minimum(winds[0], 0.0) * (below - x)
            + jnp.maximum(winds[1], 0.0) * (x - left)
            + jnp.minimum(winds[1], 0.0) * (right - x)
        )
        row_ref[...] = x - tendency + SPREAD_RATE * (above + below + left + right - 4.0 * x)
        at = pl.multiple_of(m * height, height)
        for k in range(parts):
            first = (id_ref[1] ^ k) * (bands * LANE)
            for band in range(bands):
                source = pl.multiple_of(first + band * LANE, LANE)
                outs[k][band, pl.ds(at, height), :] = row_ref[:, pl.ds(source, LANE)]
        return 0

    lax.fori_loop(0, members, body, 0)


def forecast(ids, x, flow, parts):
    members, levels, rows, cols = x.shape
    out = jax.ShapeDtypeStruct((cols // parts // LANE, members * levels * rows, LANE), F32)
    return pl.pallas_call(
        forecast_kernel,
        out_shape=[out] * parts,
        in_specs=[SMEM] + [VMEM] * 2,
        out_specs=[VMEM] * parts,
        scratch_shapes=[pltpu.VMEM((levels * rows, cols), F32)],
        compiler_params=PARAMS,
        cost_estimate=cost(3),
        name="forecast",
    )(ids, x, flow)


def mend_kernel(id_ref, top_ref, bottom_ref, flow_ref, *refs):
    groups = (len(refs) - 1) // 2
    parts, outs, rate_ref = refs[:groups], refs[groups : 2 * groups], refs[-1]
    members, levels, cols = top_ref.shape
    rows = flow_ref.shape[2]
    height = levels * rows
    bands = parts[0].shape[0]
    row = lax.broadcasted_iota(jnp.int32, (height, cols), 0)
    wind = jnp.concatenate([flow_ref[0, l] for l in range(levels)], axis=0)
    rate_ref[0] = jnp.where(row % rows == 0, jnp.maximum(wind, 0.0) + SPREAD_RATE, 0.0)
    rate_ref[1] = jnp.where(row % rows == rows - 1, SPREAD_RATE - jnp.minimum(wind, 0.0), 0.0)

    def spread_rows(value):
        return jnp.concatenate(
            [jnp.broadcast_to(value[l : l + 1], (rows, LANE)) for l in range(levels)], axis=0
        )

    def body(m, _):
        at = pl.multiple_of(m * height, height)
        for k in range(groups):
            for band in range(bands):
                source = pl.multiple_of((id_ref[1] ^ k) * (bands * LANE) + band * LANE, LANE)
                there = pl.ds(source, LANE)
                outs[k][band, pl.ds(at, height), :] = (
                    parts[k][band, pl.ds(at, height), :]
                    + rate_ref[0, :, there] * spread_rows(top_ref[m, :, there])
                    + rate_ref[1, :, there] * spread_rows(bottom_ref[m, :, there])
                )
        return 0

    lax.fori_loop(0, members, body, 0)


def mend(ids, top, bottom, flow, parts):
    _, levels, cols = top.shape
    return pl.pallas_call(
        mend_kernel,
        out_shape=[jax.ShapeDtypeStruct(parts[0].shape, F32)] * len(parts),
        in_specs=[SMEM] + [VMEM] * (3 + len(parts)),
        out_specs=[VMEM] * len(parts),
        scratch_shapes=[pltpu.VMEM((2, levels * flow.shape[2], cols), F32)],
        compiler_params=PARAMS,
        cost_estimate=cost(1),
        name="mend",
    )(ids, top, bottom, flow, *parts)


def fill_spare(put, att, odd):
    even_rows = jnp.concatenate([att[0:3], att[5:6]], axis=0)
    odd_rows = jnp.concatenate([att[3:5], att[3:5]], axis=0)
    put(jnp.where(odd, odd_rows, even_rows))


def number(row, at):
    lane = lax.broadcasted_iota(jnp.int32, (1, LANE), 1)
    return jnp.sum(jnp.where(lane == at, row, 0.0)).astype(jnp.int32)


def observe_kernel(levels, share, groups, ranges, id_ref, att_ref, *refs):
    parts, befores, out_ref = refs[:groups], refs[groups:-1], refs[-1]
    bands = parts[0].shape[0]
    slots = att_ref.shape[1]
    height = parts[0].shape[1] // share
    rows = height // levels
    att = att_ref[...]
    counts = att[5:6, 0:LANE]
    odd = (id_ref[1] & 1) == 1

    def put(rows):
        out_ref[share : share + SPARE, :] = rows

    fill_spare(put, att, odd)

    count = number(counts, 0)
    ends = [number(counts, r + 1) for r in range(rows)]

    def body(n, _, count=count, ends=ends):
        at = pl.multiple_of(n * LANE, LANE)
        begin, end = n * LANE, jnp.minimum(n * LANE + LANE, count) - 1
        low = sum((e <= begin).astype(jnp.int32) for e in ends)
        high = sum((e <= end).astype(jnp.int32) for e in ends)
        column = att_ref[1:2, pl.ds(at, LANE)].astype(jnp.int32)
        flat_row = jnp.broadcast_to(att_ref[6:7, pl.ds(at, LANE)].astype(jnp.int32), (8, LANE))
        band_of = jnp.broadcast_to(column >> 7, (8, LANE))
        lane_of = jnp.broadcast_to(column & (LANE - 1), (8, LANE))
        here = [
            band_of == (id_ref[1] ^ k) * bands + band
            for k in range(len(parts))
            for band in range(bands)
        ]

        def one_row(r, found):
            found = list(found)
            for l in range(levels):
                i = l * rows + r
                mine = flat_row == i
                for c, m in enumerate(range(0, share, 8)):
                    size = min(8, share - m)
                    value = jnp.zeros((8, LANE), F32)
                    for j in range(len(parts) * bands):
                        block = parts[j // bands].at[j % bands][
                            pl.ds(m * height + i, size, stride=height), :
                        ]
                        if size < 8:
                            block = jnp.concatenate(
                                [block, jnp.zeros((8 - size, LANE), F32)], axis=0
                            )
                        picked = jnp.take_along_axis(block, lane_of, axis=1)
                        value = jnp.where(here[j], picked, value)
                    found[c] = jnp.where(mine, value, found[c])
            return tuple(found)

        found = []
        for m in range(0, share, 8):
            size = min(8, share - m)
            value = jnp.zeros((8, LANE), F32)
            for before in befores:
                value = before[m : m + size, pl.ds(at, LANE)]
                if size < 8:
                    value = jnp.concatenate([value, jnp.zeros((8 - size, LANE), F32)], axis=0)
            found.append(value)
        found = tuple(found)
        for begin_row, end_row in ranges:
            found = lax.fori_loop(
                jnp.maximum(low, begin_row), jnp.minimum(high, end_row) + 1, one_row, found
            )
        for c, m in enumerate(range(0, share, 8)):
            size = min(8, share - m)
            out_ref[m : m + size, pl.ds(at, LANE)] = found[c][0:size]
        return 0

    out_ref[0:share, :] = jnp.zeros((share, slots), F32)
    lax.fori_loop(0, (count + LANE - 1) // LANE, body, 0)


def observe(ids, att, parts, levels, share, ranges, befores=()):
    slots = att.shape[1]
    padded = (share + SPARE + 7) // 8 * 8
    return pl.pallas_call(
        functools.partial(observe_kernel, levels, share, len(parts), ranges),
        out_shape=jax.ShapeDtypeStruct((padded, slots), F32),
        in_specs=[SMEM] + [VMEM] * (1 + len(parts) + len(befores)),
        out_specs=VMEM,
        compiler_params=PARAMS,
        cost_estimate=cost(3),
        name="observe",
    )(ids, att, *parts, *befores)


def weigh(prior, value, error, live):
    members = prior.shape[0]
    average = jnp.sum(prior, axis=0, keepdims=True) / members
    deviation = prior - average
    var_prior = jnp.sum(deviation * deviation, axis=0, keepdims=True) / (members - 1) + EPSILON
    combined = var_prior + error
    shrink = jnp.sqrt(error / combined)
    post = (error * average + var_prior * value) / combined
    shift = live * ((shrink - 1.0) * deviation + (post - average))
    weight = (live / ((members - 1) * var_prior)) * deviation
    return weight, shift


def pack_kernel(geometry, window, id_ref, *refs):
    priors, (w_ref, s_ref, rc_ref, span_ref) = refs[:window], refs[window:]
    levels, rows, share, row_scale, col_scale = geometry
    halves, groups, _, width = priors[0].shape
    piece = width if halves == 1 else min(2 * LANE, width)
    piece = min(piece, BLOCK)
    chunk = piece * halves
    counts = [ref[0, 0, share + 3 : share + 4, 0:LANE] for ref in priors]

    totals = [number(row, 0) for row in counts]
    for p in range(rows):
        span_ref[p] = number(counts[0], p + 1) // LANE * LANE
        span_ref[rows + p] = number(counts[-1], p) if p else jnp.int32(0)
    off = jnp.int32(0)
    starts = []
    for t, ref in enumerate(priors):
        count = totals[t]
        starts.append(off)

        def body(k, _, ref=ref, off=off, count=count):
            src = k * chunk
            at = pl.multiple_of(k * piece, piece)
            half = [(h ^ id_ref[1]) & (halves - 1) for h in range(halves)]

            def taken(g, begin, size):
                return jnp.concatenate(
                    [ref[h, g, begin : begin + size, pl.ds(at, piece)] for h in half], axis=1
                )

            dst = pl.multiple_of(off + src, LANE)
            slot = lax.broadcasted_iota(jnp.int32, (1, chunk), 1) + src
            live = (slot < count).astype(F32)
            prior = jnp.concatenate(
                [taken(id_ref[1] ^ g, 0, share) for g in range(groups)], axis=0
            )
            place = taken(0, share, SPARE)
            seen = taken(1, share, SPARE)
            members = prior.shape[0]
            weight, shift = weigh(prior, seen[0:1], seen[1:2], live)
            pad = jnp.zeros((DEEP - 3 * members, chunk), BF16)
            for l in range(levels):
                high, low = split(weight * (1.0 / (1.0 + jnp.abs(place[2:3] - float(l)))))
                w_ref[l, :, pl.ds(dst, chunk)] = jnp.concatenate([high, low, high, pad], axis=0)
            turned = jnp.concatenate([shift, jnp.zeros((LANE - members, chunk), F32)], axis=0).T
            high, low = split(turned)
            s_ref[pl.ds(dst, chunk), 0:LANE] = high
            s_ref[pl.ds(dst, chunk), LANE : 2 * LANE] = low
            rc_ref[0:1, pl.ds(dst, chunk)] = place[0:1] * row_scale
            rc_ref[1:2, pl.ds(dst, chunk)] = place[1:2] * col_scale
            rc_ref[2:3, pl.ds(dst, chunk)] = place[2:3]
            return 0

        lax.fori_loop(0, (count + chunk - 1) // chunk, body, 0)
        off = off + (count + LANE - 1) // LANE * LANE
    dst = pl.multiple_of(off, LANE)
    for l in range(levels):
        w_ref[l, :, pl.ds(dst, 2 * BLOCK)] = jnp.zeros((DEEP, 2 * BLOCK), BF16)
    s_ref[pl.ds(dst, 2 * BLOCK), :] = jnp.zeros((2 * BLOCK, 2 * LANE), BF16)
    rc_ref[:, pl.ds(dst, 2 * BLOCK)] = jnp.zeros((8, 2 * BLOCK), F32)
    for p in range(rows):
        span_ref[rows + p] = starts[-1] + span_ref[rows + p]
    span_ref[2 * rows] = off


def pack(geometry, ids, priors):
    levels, rows = geometry[:2]
    halves, _, _, width = priors[0].shape
    room = len(priors) * halves * width + 2 * BLOCK + LANE
    return pl.pallas_call(
        functools.partial(pack_kernel, geometry, len(priors)),
        out_shape=[
            jax.ShapeDtypeStruct((levels, DEEP, room), BF16),
            jax.ShapeDtypeStruct((room, 2 * LANE), BF16),
            jax.ShapeDtypeStruct((8, room), F32),
            jax.ShapeDtypeStruct((2 * rows + 1,), jnp.int32),
        ],
        in_specs=[SMEM] + [VMEM] * len(priors),
        out_specs=[VMEM, VMEM, VMEM, SMEM],
        compiler_params=PARAMS,
        cost_estimate=cost(5),
        name="pack",
    )(ids, *priors)


def triple(x):
    high, low = split(x)
    members, width = x.shape
    pad = jnp.zeros((DEEP - 3 * members, width), BF16)
    return jnp.concatenate([high, high, low, pad], axis=0).T


def points_kernel(
    geometry, id_ref, span_ref, att_ref, seen_ref, w_ref, s_ref, rc_ref, out_ref, acc_ref
):
    levels, rows, share, row_scale, col_scale = geometry
    groups, _, width = out_ref.shape
    chunk = min(2 * LANE, width)
    off = span_ref[2 * rows]
    counts = att_ref[5:6, 0:LANE]
    live = number(counts, 0)
    for c in range(width // chunk):
        lanes = slice(c * chunk, (c + 1) * chunk)
        begin = (2 * c + (id_ref[1] & 1)) * chunk
        at = pl.multiple_of(begin, chunk)
        att = att_ref[:, pl.ds(at, chunk)]
        for g in range(groups):

            def put(rows, g=g):
                out_ref[g, share : share + SPARE, lanes] = rows

            rest = jnp.zeros((1, chunk - LANE), F32)
            head = jnp.concatenate([counts, rest], axis=1) if chunk > LANE else counts
            fill_spare(put, jnp.concatenate([att[0:5], head, att[6:8]], axis=0), g % 2 == 1)

        @pl.when(begin >= live)
        def _():
            for g in range(groups):
                out_ref[g, 0:share, lanes] = jnp.zeros((share, chunk), F32)

        @pl.when(begin < live)
        def _():
            x = jnp.concatenate(
                [seen_ref[id_ref[1] ^ g, 0:share, pl.ds(at, chunk)] for g in range(groups)],
                axis=0,
            )
            cells = triple(x)
            place = jnp.concatenate([att, jnp.zeros((LANE - 8, chunk), F32)], axis=0).T
            cell_row = place[:, 0:1] * row_scale
            cell_col = place[:, 1:2] * col_scale
            cell_lev = place[:, 2:3]
            acc_ref[...] = jnp.zeros(acc_ref.shape, F32)

            def body(b, _):
                at = pl.multiple_of(b * BLOCK, BLOCK)
                row_gap = cell_row - rc_ref[0:1, pl.ds(at, BLOCK)]
                col_gap = cell_col - rc_ref[1:2, pl.ds(at, BLOCK)]
                near = jnp.maximum(1.0 - row_gap * row_gap - col_gap * col_gap, 0.0)
                level = rc_ref[2:3, pl.ds(at, BLOCK)]
                ratio = jnp.ones((chunk, BLOCK), F32)
                for l in range(1, levels):
                    other = (1.0 + level) / (1.0 + jnp.abs(level - float(l)))
                    ratio = jnp.where(cell_lev == float(l), other, ratio)
                cov = jnp.dot(cells, w_ref[0, :, pl.ds(at, BLOCK)], preferred_element_type=F32)
                high, low = split(cov * (near * near) * ratio)
                s = s_ref[pl.ds(at, BLOCK), :]
                acc_ref[...] += jnp.dot(high, s, preferred_element_type=F32)
                acc_ref[:, 0:LANE] += jnp.dot(low, s[:, 0:LANE], preferred_element_type=F32)
                return 0

            def pair(b, _):
                body(2 * b, 0)
                body(2 * b + 1, 0)
                return 0

            lax.fori_loop(0, (off + 2 * BLOCK - 1) // (2 * BLOCK), pair, 0)
            out = x + (acc_ref[:, 0:LANE] + acc_ref[:, LANE : 2 * LANE]).T[0 : groups * share]
            for g in range(groups):
                out_ref[id_ref[1] ^ g, 0:share, lanes] = out[g * share : (g + 1) * share]


def update_points(geometry, ids, att, seen, packed):
    w, s, rc, span = packed
    groups, padded, slots = seen.shape
    return pl.pallas_call(
        functools.partial(points_kernel, geometry),
        out_shape=jax.ShapeDtypeStruct((groups, padded, slots // 2), F32),
        in_specs=[SMEM] * 2 + [VMEM] * 5,
        out_specs=VMEM,
        scratch_shapes=[pltpu.VMEM((min(2 * LANE, slots // 2), 2 * LANE), F32)],
        compiler_params=PARAMS,
        cost_estimate=cost(8),
        name="update_points",
    )(ids, span, att, seen, w, s, rc)


def grid_kernel(geometry, begin, groups, id_ref, span_ref, w_ref, s_ref, rc_ref, *refs):
    levels, all_rows, share, row_scale, col_scale = geometry
    xs, outs, refs = refs[:groups], refs[groups : 2 * groups], refs[2 * groups :]
    xt_ref, acc_ref, q_ref, high_ref, low_ref = refs
    bands = xs[0].shape[0]
    height = levels * all_rows
    rows = outs[0].shape[1] // (share * levels)
    first = [span_ref[begin + p] for p in range(rows)]
    last = [span_ref[all_rows + begin + p] for p in range(rows)]
    cols = bands * LANE
    members = groups * share
    q_ref[...] = (
        lax.broadcasted_iota(jnp.int32, (cols, LANE), 0) + id_ref[1] * cols
    ).astype(F32) * col_scale

    def cells(i):
        return jnp.concatenate(
            [
                jnp.concatenate(
                    [x.at[b][pl.ds(i, share, stride=height), :] for x in xs], axis=0
                )
                for b in range(bands)
            ],
            axis=1,
        )

    for l in range(levels):
        for p in range(rows):
            xt_ref[l * rows + p] = triple(cells(l * all_rows + begin + p))

    steps = [jnp.maximum(last[p] - first[p] + BLOCK - 1, 0) // BLOCK for p in range(rows)]
    ends = [steps[0]]
    for n in steps[1:]:
        ends.append(ends[-1] + n)
    acc_ref[...] = jnp.zeros(acc_ref.shape, F32)

    def locate(i):
        p = jnp.int32(0)
        at = first[0] + i * BLOCK
        for j in range(1, rows):
            past = i >= ends[j - 1]
            p = jnp.where(past, j, p)
            at = jnp.where(past, first[j] + (i - ends[j - 1]) * BLOCK, at)
        return p, pl.multiple_of(at, LANE)

    def spread(i, l):
        p, at = locate(i)
        s = s_ref[pl.ds(at, BLOCK), :]
        acc_ref[p, l] += jnp.dot(high_ref[l], s, preferred_element_type=F32)
        acc_ref[p, l, :, 0:LANE] += jnp.dot(low_ref[l], s[:, 0:LANE], preferred_element_type=F32)

    def step(i, _):
        p, at = locate(i)
        row_gap = (id_ref[0] * all_rows + begin + p).astype(F32) * row_scale - rc_ref[0:1, pl.ds(at, BLOCK)]
        base = 1.0 - row_gap * row_gap
        q = q_ref[...]
        col_gap = jnp.concatenate([q] * (BLOCK // LANE), axis=1) - rc_ref[1:2, pl.ds(at, BLOCK)]
        near = jnp.maximum(base - col_gap * col_gap, 0.0)
        taper = near * near
        for l in range(levels):
            cov = jnp.dot(
                xt_ref[l * rows + p], w_ref[l, :, pl.ds(at, BLOCK)], preferred_element_type=F32
            )
            high, low = split(cov * taper)
            if l == 0:
                spread(jnp.maximum(i - 1, 0), levels - 1)
            else:
                spread(i, l - 1)
            high_ref[l], low_ref[l] = high, low
        return 0

    high_ref[levels - 1] = jnp.zeros(high_ref.shape[1:], BF16)
    low_ref[levels - 1] = jnp.zeros(low_ref.shape[1:], BF16)
    def pair(i, _):
        step(2 * i, 0)
        step(2 * i + 1, 0)
        return 0

    pairs = (ends[-1] + 1) // 2
    lax.fori_loop(0, pairs, pair, 0)
    spread(jnp.maximum(2 * pairs - 1, 0), levels - 1)

    def store(p, _):
        for l in range(levels):
            at = pl.ds(l * all_rows + begin + p, share, stride=height)
            to = pl.ds(l * rows + p, share, stride=levels * rows)
            inc = (acc_ref[p, l, :, 0:LANE] + acc_ref[p, l, :, LANE : 2 * LANE]).T[0:members]
            for g in range(groups):
                for b in range(bands):
                    outs[g].at[b][to, :] = (
                        xs[g].at[b][at, :]
                        + inc[g * share : (g + 1) * share, b * LANE : (b + 1) * LANE]
                    )
        return 0

    lax.fori_loop(0, rows, store, 0)


def update_grid(geometry, ids, packed, parts, begin, rows):
    w, s, rc, span = packed
    levels, all_rows = geometry[:2]
    groups = len(parts)
    bands, depth, _ = parts[0].shape
    cols = bands * LANE
    out = jax.ShapeDtypeStruct((bands, depth // all_rows * rows, LANE), F32)
    return pl.pallas_call(
        functools.partial(grid_kernel, geometry, begin, groups),
        out_shape=[out] * groups,
        in_specs=[SMEM] * 2 + [VMEM] * (3 + groups),
        out_specs=[VMEM] * groups,
        scratch_shapes=[
            pltpu.VMEM((levels * rows, cols, DEEP), BF16),
            pltpu.VMEM((rows, levels, cols, 2 * LANE), F32),
            pltpu.VMEM((cols, LANE), F32),
            pltpu.VMEM((levels, cols, BLOCK), BF16),
            pltpu.VMEM((levels, cols, BLOCK), BF16),
        ],
        compiler_params=PARAMS,
        cost_estimate=cost(7 * rows),
        name="update_grid",
    )(ids, span, w, s, rc, *parts)


def restore_kernel(groups, id_ref, *refs):
    pieces, befores, out_ref = refs[:groups], refs[groups:-1], refs[-1]
    members, levels, all_rows, _ = out_ref.shape
    bands = pieces[0].shape[0]
    height = pieces[0].shape[1] // members
    rows = height // levels
    begin = all_rows - rows

    def body(m, _):
        at = pl.multiple_of(m * height, height)
        for before in befores:
            for l in range(levels):
                out_ref[m, l, 0:begin, :] = before[m, l]
        for k in range(groups):
            for band in range(bands):
                block = pieces[k][band, pl.ds(at, height), :]
                first = pl.multiple_of((id_ref[1] ^ k) * (bands * LANE) + band * LANE, LANE)
                for l in range(levels):
                    out_ref[m, l, begin:all_rows, pl.ds(first, LANE)] = block[
                        l * rows : (l + 1) * rows
                    ]
        return 0

    lax.fori_loop(0, members, body, 0)


def restore(ids, pieces, befores, shape):
    return pl.pallas_call(
        functools.partial(restore_kernel, len(pieces)),
        out_shape=jax.ShapeDtypeStruct(shape, F32),
        in_specs=[SMEM] + [VMEM] * (len(pieces) + len(befores)),
        out_specs=VMEM,
        compiler_params=PARAMS,
        cost_estimate=cost(2),
        name="restore",
    )(ids, *pieces, *befores)


def shifted(value, steps):
    count = lax.axis_size("tile")
    pairs = [(i, i + steps) for i in range(count) if 0 <= i + steps < count]
    return lax.ppermute(value, "tile", pairs)


def paired(value, odd):
    count = lax.axis_size("tile")
    firsts = range(odd, count - 1, 2)
    pairs = [(i, i + 1) for i in firsts] + [(i + 1, i) for i in firsts]
    return lax.ppermute(value, "tile", pairs)


def window_of(value):
    return [
        shifted(value, 2),
        paired(value, 0),
        value,
        paired(value, 1),
        shifted(value, -2),
    ]


def crossed(value, step):
    count = lax.axis_size("ens")
    return lax.ppermute(value, "ens", [(i, i ^ step) for i in range(count)])


def exchanged(parts):
    return [parts[0]] + [crossed(parts[k], k) for k in range(1, len(parts))]


def on_device(initial_sample_set, flow_velocity, obs_loc, obs_count, obs_value, obs_error):
    x = initial_sample_set
    share, levels, rows, col_total = x.shape
    ens = lax.axis_size("ens")
    ids = jnp.stack([lax.axis_index("tile"), lax.axis_index("ens")]).astype(jnp.int32)
    geometry = (levels, rows, share, 1.0 / (REACH * rows), 1.0 / (col_total // 2))

    top = shifted(x[:, :, rows - 1, :], 1)
    bottom = shifted(lax.optimization_barrier(x)[:, :, 0, :], -1)
    att = order(ids, obs_loc, obs_value, obs_error, obs_count, rows)
    parts = forecast(ids, x, flow_velocity, ens)
    inner, edges = [(1, rows - 2)], [(0, 0), (rows - 1, rows - 1)]
    seen = observe(ids, att[0], parts, levels, share, inner)
    parts = mend(ids, top, bottom, flow_velocity, parts)
    seen = observe(ids, att[0], parts, levels, share, edges, (seen,))
    seen = lax.all_gather(seen, "ens", axis=0)
    parts, seen = lax.optimization_barrier((parts, seen))
    priors = window_of(seen[None])
    ahead = observe(ids, att[1], parts, levels, share, [(0, rows - 1)])
    ahead = lax.all_gather(ahead, "ens", axis=0)
    parts = exchanged(parts)
    priors, parts, ahead = lax.optimization_barrier((priors, parts, ahead))
    packed = pack(geometry, ids, priors)
    later = update_points(geometry, ids, att[1], ahead, packed)
    later = window_of(jnp.stack([later, crossed(later, 1)]))
    parts = update_grid(geometry, ids, packed, parts, 0, rows)
    packed = pack(geometry, ids, later)
    half = rows // 2
    upper = update_grid(geometry, ids, packed, parts, 0, half)
    parts, upper = lax.optimization_barrier((parts, upper))
    lower = update_grid(geometry, ids, packed, parts, half, rows - half)
    done = restore(ids, exchanged(upper), (), (share, levels, half, col_total))
    return restore(ids, exchanged(lower), (done,), x.shape)


def solution(mesh):
    in_specs = (
        P("ens", None, "tile", None),
        P(None, None, "tile", None),
        P(None, None, "tile"),
        P(None, "tile"),
        P(None, "tile"),
        P(None, "tile"),
    )
    out_specs = P("ens", None, "tile", None)
    return jax.shard_map(
        on_device, mesh=mesh, in_specs=in_specs, out_specs=out_specs, check_vma=False
    )
```

```python
import functools

import jax
import jax.numpy as jnp
from jax import lax
from jax.experimental import pallas as pl
from jax.experimental.pallas import tpu as pltpu
from jax.sharding import PartitionSpec as P

BATCHES = 2
REACH = 2
SPARE = 4
SPREAD_RATE = 0.05
EPSILON = 1e-06
LANE = 128
DEEP = 256
BLOCK = 512
F32 = jnp.float32
BF16 = jnp.bfloat16
VMEM = pl.BlockSpec(memory_space=pltpu.VMEM)
SMEM = pl.BlockSpec(memory_space=pltpu.SMEM)
PARAMS = pltpu.CompilerParams(vmem_limit_bytes=32 << 20)


def cost(micros):
    return pl.CostEstimate(flops=int(micros * 1e9), bytes_accessed=0, transcendentals=0)


def split(value):
    high = value.astype(BF16)
    return high, (value - high.astype(F32)).astype(BF16)


def order_kernel(rows, id_ref, loc_ref, value_ref, error_ref, count_ref, att_ref):
    batches, slots = value_ref.shape
    earlier = (
        lax.broadcasted_iota(jnp.int32, (slots, slots), 0)
        < lax.broadcasted_iota(jnp.int32, (slots, slots), 1)
    ).astype(BF16)
    slot = lax.broadcasted_iota(jnp.int32, (1, slots), 1)
    key_of = lax.broadcasted_iota(jnp.int32, (8, slots), 0)
    for b in range(batches):
        count = count_ref[b, 0]
        local_row = loc_ref[0, b : b + 1, :] - id_ref[0] * rows
        key = jnp.where(slot < count, local_row, rows)
        mine = key_of == jnp.broadcast_to(key, (8, slots))
        ones = mine.astype(F32)
        before = jnp.dot(ones.astype(BF16), earlier, preferred_element_type=F32)
        totals = jnp.sum(ones, axis=1, keepdims=True)
        start = jnp.zeros((1, slots), F32)
        place = jnp.zeros((1, slots), F32)
        cumulative = jnp.where(slot == 0, count.astype(F32), 0.0)
        for r in range(rows + 1):
            place = place + ones[r : r + 1] * (before[r : r + 1] + start)
            start = start + totals[r : r + 1]
            cumulative = jnp.where(slot == r + 1, start, cumulative)
        level = loc_ref[2, b : b + 1, :]
        fields = [
            loc_ref[0, b : b + 1, :].astype(F32),
            loc_ref[1, b : b + 1, :].astype(F32),
            level.astype(F32),
            value_ref[b : b + 1, :],
            error_ref[b : b + 1, :],
            (level * rows + local_row).astype(F32),
        ]
        table = jnp.concatenate(fields + [jnp.zeros((2, slots), F32)], axis=0)
        high, low = split(table)
        rest = (table - high.astype(F32) - low.astype(F32)).astype(BF16)
        target = lax.broadcasted_iota(jnp.int32, (slots, slots), 0)
        moved = (target == jnp.broadcast_to(place.astype(jnp.int32), (slots, slots))).astype(BF16)
        out = lax.dot_general(
            jnp.concatenate([high.astype(F32), low.astype(F32), rest.astype(F32)], axis=0).astype(BF16),
            moved,
            (((1,), (1,)), ((), ())),
            preferred_element_type=F32,
        )
        out = (out[0:8] + out[8:16]) + out[16:24]
        att_ref[b] = jnp.concatenate([out[0:5], cumulative, out[5:6], jnp.zeros((1, slots), F32)], axis=0)


def order(ids, obs_loc, obs_value, obs_error, obs_count, rows):
    batches, slots = obs_value.shape
    return pl.pallas_call(
        functools.partial(order_kernel, rows),
        out_shape=jax.ShapeDtypeStruct((batches, 8, slots), F32),
        in_specs=[SMEM, VMEM, VMEM, VMEM, SMEM],
        out_specs=VMEM,
        compiler_params=PARAMS,
        cost_estimate=cost(2),
        name="order",
    )(ids, obs_loc, obs_value, obs_error, obs_count)


def forecast_kernel(id_ref, x_ref, flow_ref, *refs):
    outs, row_ref = refs[:-1], refs[-1]
    members, levels, rows, cols = x_ref.shape
    height = levels * rows
    parts, bands = len(outs), outs[0].shape[0]
    row = lax.broadcasted_iota(jnp.int32, (height, cols), 0)
    col = lax.broadcasted_iota(jnp.int32, (height, cols), 1)
    winds = [
        jnp.concatenate([flow_ref[d, l] for l in range(levels)], axis=0) for d in range(2)
    ]

    def body(m, _):
        x = jnp.concatenate([x_ref[m, l] for l in range(levels)], axis=0)
        above = jnp.where(row % rows == 0, 0.0, pltpu.roll(x, 1, 0))
        below = jnp.where(row % rows == rows - 1, 0.0, pltpu.roll(x, height - 1, 0))
        left = jnp.where(col == 0, 0.0, pltpu.roll(x, 1, 1))
        right = jnp.where(col == cols - 1, 0.0, pltpu.roll(x, cols - 1, 1))
        tendency = (
            jnp.maximum(winds[0], 0.0) * (x - above)
            + jnp.minimum(winds[0], 0.0) * (below - x)
            + jnp.maximum(winds[1], 0.0) * (x - left)
            + jnp.minimum(winds[1], 0.0) * (right - x)
        )
        row_ref[...] = x - tendency + SPREAD_RATE * (above + below + left + right - 4.0 * x)
        at = pl.multiple_of(m * height, height)
        for k in range(parts):
            first = (id_ref[1] ^ k) * (bands * LANE)
            for band in range(bands):
                source = pl.multiple_of(first + band * LANE, LANE)
                outs[k][band, pl.ds(at, height), :] = row_ref[:, pl.ds(source, LANE)]
        return 0

    lax.fori_loop(0, members, body, 0)


def forecast(ids, x, flow, parts):
    members, levels, rows, cols = x.shape
    out = jax.ShapeDtypeStruct((cols // parts // LANE, members * levels * rows, LANE), F32)
    return pl.pallas_call(
        forecast_kernel,
        out_shape=[out] * parts,
        in_specs=[SMEM] + [VMEM] * 2,
        out_specs=[VMEM] * parts,
        scratch_shapes=[pltpu.VMEM((levels * rows, cols), F32)],
        compiler_params=PARAMS,
        cost_estimate=cost(3),
        name="forecast",
    )(ids, x, flow)


def mend_kernel(id_ref, top_ref, bottom_ref, flow_ref, *refs):
    groups = (len(refs) - 1) // 2
    parts, outs, rate_ref = refs[:groups], refs[groups : 2 * groups], refs[-1]
    members, levels, cols = top_ref.shape
    rows = flow_ref.shape[2]
    height = levels * rows
    bands = parts[0].shape[0]
    row = lax.broadcasted_iota(jnp.int32, (height, cols), 0)
    wind = jnp.concatenate([flow_ref[0, l] for l in range(levels)], axis=0)
    rate_ref[0] = jnp.where(row % rows == 0, jnp.maximum(wind, 0.0) + SPREAD_RATE, 0.0)
    rate_ref[1] = jnp.where(row % rows == rows - 1, SPREAD_RATE - jnp.minimum(wind, 0.0), 0.0)

    def spread_rows(value):
        return jnp.concatenate(
            [jnp.broadcast_to(value[l : l + 1], (rows, LANE)) for l in range(levels)], axis=0
        )

    def body(m, _):
        at = pl.multiple_of(m * height, height)
        for k in range(groups):
            for band in range(bands):
                source = pl.multiple_of((id_ref[1] ^ k) * (bands * LANE) + band * LANE, LANE)
                there = pl.ds(source, LANE)
                outs[k][band, pl.ds(at, height), :] = (
                    parts[k][band, pl.ds(at, height), :]
                    + rate_ref[0, :, there] * spread_rows(top_ref[m, :, there])
                    + rate_ref[1, :, there] * spread_rows(bottom_ref[m, :, there])
                )
        return 0

    lax.fori_loop(0, members, body, 0)


def mend(ids, top, bottom, flow, parts):
    _, levels, cols = top.shape
    return pl.pallas_call(
        mend_kernel,
        out_shape=[jax.ShapeDtypeStruct(parts[0].shape, F32)] * len(parts),
        in_specs=[SMEM] + [VMEM] * (3 + len(parts)),
        out_specs=[VMEM] * len(parts),
        scratch_shapes=[pltpu.VMEM((2, levels * flow.shape[2], cols), F32)],
        compiler_params=PARAMS,
        cost_estimate=cost(1),
        name="mend",
    )(ids, top, bottom, flow, *parts)


def fill_spare(put, att, odd):
    even_rows = jnp.concatenate([att[0:3], att[5:6]], axis=0)
    odd_rows = jnp.concatenate([att[3:5], att[3:5]], axis=0)
    put(jnp.where(odd, odd_rows, even_rows))


def number(row, at):
    lane = lax.broadcasted_iota(jnp.int32, (1, LANE), 1)
    return jnp.sum(jnp.where(lane == at, row, 0.0)).astype(jnp.int32)


def observe_kernel(levels, share, groups, ranges, id_ref, att_ref, *refs):
    parts, befores, out_ref = refs[:groups], refs[groups:-1], refs[-1]
    bands = parts[0].shape[0]
    slots = att_ref.shape[1]
    height = parts[0].shape[1] // share
    rows = height // levels
    att = att_ref[...]
    counts = att[5:6, 0:LANE]
    odd = (id_ref[1] & 1) == 1

    def put(rows):
        out_ref[share : share + SPARE, :] = rows

    fill_spare(put, att, odd)

    count = number(counts, 0)
    ends = [number(counts, r + 1) for r in range(rows)]

    def body(n, _, count=count, ends=ends):
        at = pl.multiple_of(n * LANE, LANE)
        begin, end = n * LANE, jnp.minimum(n * LANE + LANE, count) - 1
        low = sum((e <= begin).astype(jnp.int32) for e in ends)
        high = sum((e <= end).astype(jnp.int32) for e in ends)
        column = att_ref[1:2, pl.ds(at, LANE)].astype(jnp.int32)
        flat_row = jnp.broadcast_to(att_ref[6:7, pl.ds(at, LANE)].astype(jnp.int32), (8, LANE))
        band_of = jnp.broadcast_to(column >> 7, (8, LANE))
        lane_of = jnp.broadcast_to(column & (LANE - 1), (8, LANE))
        here = [
            band_of == (id_ref[1] ^ k) * bands + band
            for k in range(len(parts))
            for band in range(bands)
        ]

        def one_row(r, found):
            found = list(found)
            for l in range(levels):
                i = l * rows + r
                mine = flat_row == i
                for c, m in enumerate(range(0, share, 8)):
                    size = min(8, share - m)
                    value = jnp.zeros((8, LANE), F32)
                    for j in range(len(parts) * bands):
                        block = parts[j // bands].at[j % bands][
                            pl.ds(m * height + i, size, stride=height), :
                        ]
                        if size < 8:
                            block = jnp.concatenate(
                                [block, jnp.zeros((8 - size, LANE), F32)], axis=0
                            )
                        picked = jnp.take_along_axis(block, lane_of, axis=1)
                        value = jnp.where(here[j], picked, value)
                    found[c] = jnp.where(mine, value, found[c])
            return tuple(found)

        found = []
        for m in range(0, share, 8):
            size = min(8, share - m)
            value = jnp.zeros((8, LANE), F32)
            for before in befores:
                value = before[m : m + size, pl.ds(at, LANE)]
                if size < 8:
                    value = jnp.concatenate([value, jnp.zeros((8 - size, LANE), F32)], axis=0)
            found.append(value)
        found = tuple(found)
        for begin_row, end_row in ranges:
            found = lax.fori_loop(
                jnp.maximum(low, begin_row), jnp.minimum(high, end_row) + 1, one_row, found
            )
        for c, m in enumerate(range(0, share, 8)):
            size = min(8, share - m)
            out_ref[m : m + size, pl.ds(at, LANE)] = found[c][0:size]
        return 0

    out_ref[0:share, :] = jnp.zeros((share, slots), F32)
    lax.fori_loop(0, (count + LANE - 1) // LANE, body, 0)


def observe(ids, att, parts, levels, share, ranges, befores=()):
    slots = att.shape[1]
    padded = (share + SPARE + 7) // 8 * 8
    return pl.pallas_call(
        functools.partial(observe_kernel, levels, share, len(parts), ranges),
        out_shape=jax.ShapeDtypeStruct((padded, slots), F32),
        in_specs=[SMEM] + [VMEM] * (1 + len(parts) + len(befores)),
        out_specs=VMEM,
        compiler_params=PARAMS,
        cost_estimate=cost(3),
        name="observe",
    )(ids, att, *parts, *befores)


def weigh(prior, value, error, live):
    members = prior.shape[0]
    average = jnp.sum(prior, axis=0, keepdims=True) / members
    deviation = prior - average
    var_prior = jnp.sum(deviation * deviation, axis=0, keepdims=True) / (members - 1) + EPSILON
    combined = var_prior + error
    shrink = jnp.sqrt(error / combined)
    post = (error * average + var_prior * value) / combined
    shift = live * ((shrink - 1.0) * deviation + (post - average))
    weight = (live / ((members - 1) * var_prior)) * deviation
    return weight, shift


def pack_kernel(geometry, window, id_ref, *refs):
    priors, (w_ref, s_ref, rc_ref, span_ref) = refs[:window], refs[window:]
    levels, rows, share, row_scale, col_scale = geometry
    halves, groups, _, width = priors[0].shape
    piece = min(width, BLOCK) if halves == 1 else LANE
    chunk = min(BLOCK, halves * width)
    lane = lax.broadcasted_iota(jnp.int32, (1, LANE), 1)
    counts = [ref[0, 0, share + 3 : share + 4, 0:LANE] for ref in priors]

    totals = [number(row, 0) for row in counts]
    for p in range(rows):
        span_ref[p] = number(counts[0], p + 1) // LANE * LANE
        span_ref[rows + p] = number(counts[-1], p) if p else jnp.int32(0)
    w_ref[:, :, 0:LANE] = jnp.zeros((levels, DEEP, LANE), BF16)
    s_ref[0:LANE, :] = jnp.zeros((LANE, 2 * LANE), BF16)
    rc_ref[:, 0:LANE] = jnp.zeros((8, LANE), F32)
    off = jnp.int32(0)
    starts = []
    for t, ref in enumerate(priors):
        count = totals[t]
        starts.append(off)

        def body(k, _, ref=ref, off=off, count=count):
            src = k * chunk
            each = chunk // (piece * halves)
            half = [(h ^ id_ref[1]) & (halves - 1) for h in range(halves)]

            def taken(g, begin, size):
                return jnp.concatenate(
                    [
                        ref[h, g, begin : begin + size, pl.ds(pl.multiple_of((k * each + n) * piece, piece), piece)]
                        for n in range(each)
                        for h in half
                    ],
                    axis=1,
                )

            slot = lax.broadcasted_iota(jnp.int32, (1, chunk), 1) + src
            live = (slot < count).astype(F32)
            prior = jnp.concatenate(
                [taken(id_ref[1] ^ g, 0, share) for g in range(groups)], axis=0
            )
            place = taken(0, share, SPARE) * live
            seen = taken(1, share, SPARE)
            members = prior.shape[0]
            weight, shift = weigh(prior, seen[0:1], seen[1:2], live)
            table = jnp.concatenate(
                [
                    weight,
                    shift,
                    place[0:1] * row_scale,
                    place[1:2] * col_scale,
                    place[2:3],
                    jnp.zeros((5, chunk), F32),
                ],
                axis=0,
            )
            filled = off & (LANE - 1)
            dst = pl.multiple_of(off - filled + src, LANE)
            turned = [
                pltpu.roll(table[:, n : n + LANE], filled, 1) for n in range(0, chunk, LANE)
            ]
            none = jnp.zeros_like(turned[0])
            table = jnp.concatenate(
                [jnp.where(lane < filled, a, b) for a, b in zip([none] + turned, turned + [none])],
                axis=1,
            )
            first, rest = pl.ds(dst, LANE), pl.ds(pl.multiple_of(dst + LANE, LANE), chunk)
            weight, shift = table[0:members], table[members : 2 * members]
            level = table[2 * members + 2 : 2 * members + 3]
            pad = jnp.zeros((DEEP - 3 * members, chunk + LANE), BF16)
            high, low = split(weight)
            stacked = jnp.concatenate([high, low, high, pad], axis=0)
            for l in range(levels):
                factor = 1.0 / (1.0 + jnp.abs(level - float(l)))
                if levels <= 2:
                    stack = stacked * factor.astype(BF16)
                else:
                    high, low = split(weight * factor)
                    stack = jnp.concatenate([high, low, high, pad], axis=0)
                w_ref[l, :, first] += stack[:, 0:LANE]
                w_ref[l, :, rest] = stack[:, LANE:]
            pad = jnp.zeros((LANE - members, chunk + LANE), F32)
            high, low = split(jnp.concatenate([shift, pad], axis=0).T)
            s_ref[first, 0:LANE] += high[0:LANE]
            s_ref[rest, 0:LANE] = high[LANE:]
            s_ref[first, LANE : 2 * LANE] += low[0:LANE]
            s_ref[rest, LANE : 2 * LANE] = low[LANE:]
            rc_ref[:, first] += table[2 * members :, 0:LANE]
            rc_ref[:, rest] = table[2 * members :, LANE:]
            return 0

        lax.fori_loop(0, (count + chunk - 1) // chunk, body, 0)
        off = off + count
    dst = pl.multiple_of((off + LANE - 1) // LANE * LANE, LANE)
    for l in range(levels):
        w_ref[l, :, pl.ds(dst, 2 * BLOCK)] = jnp.zeros((DEEP, 2 * BLOCK), BF16)
    s_ref[pl.ds(dst, 2 * BLOCK), :] = jnp.zeros((2 * BLOCK, 2 * LANE), BF16)
    rc_ref[:, pl.ds(dst, 2 * BLOCK)] = jnp.zeros((8, 2 * BLOCK), F32)
    for p in range(rows):
        span_ref[rows + p] = starts[-1] + span_ref[rows + p]
    span_ref[2 * rows] = off


def pack(geometry, ids, priors):
    levels, rows = geometry[:2]
    halves, _, _, width = priors[0].shape
    room = len(priors) * halves * width + 2 * BLOCK + 2 * LANE
    return pl.pallas_call(
        functools.partial(pack_kernel, geometry, len(priors)),
        out_shape=[
            jax.ShapeDtypeStruct((levels, DEEP, room), BF16),
            jax.ShapeDtypeStruct((room, 2 * LANE), BF16),
            jax.ShapeDtypeStruct((8, room), F32),
            jax.ShapeDtypeStruct((2 * rows + 1,), jnp.int32),
        ],
        in_specs=[SMEM] + [VMEM] * len(priors),
        out_specs=[VMEM, VMEM, VMEM, SMEM],
        compiler_params=PARAMS,
        cost_estimate=cost(5),
        name="pack",
    )(ids, *priors)


def triple(x):
    high, low = split(x)
    members, width = x.shape
    pad = jnp.zeros((DEEP - 3 * members, width), BF16)
    return jnp.concatenate([high, high, low, pad], axis=0).T


def points_kernel(
    geometry, id_ref, span_ref, att_ref, seen_ref, w_ref, s_ref, rc_ref, out_ref, acc_ref
):
    levels, rows, share, row_scale, col_scale = geometry
    groups, _, width = out_ref.shape
    off = span_ref[2 * rows]
    counts = att_ref[5:6, 0:LANE]
    live = number(counts, 0)
    core = id_ref[1] & 1
    pieces = jnp.maximum((live + LANE - 1) // LANE + 1 - core, 0) // 2

    def lanes(ref, n, count, *index):
        return jnp.concatenate(
            [
                ref[(*index, pl.ds(pl.multiple_of((2 * (n + j) + core) * LANE, LANE), LANE))]
                for j in range(count)
            ],
            axis=-1,
        )

    for n in range(width // LANE):
        att = lanes(att_ref, n, 1, slice(None))
        for g in range(groups):

            def put(value, g=g):
                out_ref[g, share : share + SPARE, n * LANE : (n + 1) * LANE] = value

            fill_spare(put, jnp.concatenate([att[0:5], counts, att[6:8]], axis=0), g % 2 == 1)
            out_ref[g, 0:share, n * LANE : (n + 1) * LANE] = jnp.zeros((share, LANE), F32)

    def update(n, count):
        size = count * LANE
        att = lanes(att_ref, n, count, slice(None))
        x = jnp.concatenate(
            [lanes(seen_ref, n, count, id_ref[1] ^ g, slice(0, share)) for g in range(groups)],
            axis=0,
        )
        cells = triple(x)
        place = jnp.concatenate([att, jnp.zeros((LANE - 8, size), F32)], axis=0).T
        cell_row = place[:, 0:1] * row_scale
        cell_col = place[:, 1:2] * col_scale
        cell_lev = place[:, 2:3]
        acc_ref[0:size] = jnp.zeros((size, 2 * LANE), F32)

        def body(b):
            at = pl.multiple_of(b * BLOCK, BLOCK)
            row_gap = cell_row - rc_ref[0:1, pl.ds(at, BLOCK)]
            col_gap = cell_col - rc_ref[1:2, pl.ds(at, BLOCK)]
            near = jnp.maximum(1.0 - row_gap * row_gap - col_gap * col_gap, 0.0)
            level = rc_ref[2:3, pl.ds(at, BLOCK)]
            ratio = jnp.ones((size, BLOCK), F32)
            for l in range(1, levels):
                other = (1.0 + level) / (1.0 + jnp.abs(level - float(l)))
                ratio = jnp.where(cell_lev == float(l), other, ratio)
            cov = jnp.dot(cells, w_ref[0, :, pl.ds(at, BLOCK)], preferred_element_type=F32)
            high, low = split(cov * (near * near) * ratio)
            s = s_ref[pl.ds(at, BLOCK), :]
            acc_ref[0:size] += jnp.dot(high, s, preferred_element_type=F32)
            acc_ref[0:size, 0:LANE] += jnp.dot(low, s[:, 0:LANE], preferred_element_type=F32)

        def pair(b, _):
            body(2 * b)
            body(2 * b + 1)
            return 0

        lax.fori_loop(0, (off + 2 * BLOCK - 1) // (2 * BLOCK), pair, 0)
        out = x + (acc_ref[0:size, 0:LANE] + acc_ref[0:size, LANE : 2 * LANE]).T[0 : groups * share]
        for g in range(groups):
            out_ref[id_ref[1] ^ g, 0:share, n * LANE : n * LANE + size] = out[
                g * share : (g + 1) * share
            ]

    for n in range(0, width // LANE, 2):
        if n + 2 <= width // LANE:
            pl.when(pieces >= n + 2)(functools.partial(update, n, 2))
        pl.when(pieces == n + 1)(functools.partial(update, n, 1))


def update_points(geometry, ids, att, seen, packed):
    w, s, rc, span = packed
    groups, padded, slots = seen.shape
    return pl.pallas_call(
        functools.partial(points_kernel, geometry),
        out_shape=jax.ShapeDtypeStruct((groups, padded, slots // 2), F32),
        in_specs=[SMEM] * 2 + [VMEM] * 5,
        out_specs=VMEM,
        scratch_shapes=[pltpu.VMEM((2 * LANE, 2 * LANE), F32)],
        compiler_params=PARAMS,
        cost_estimate=cost(8),
        name="update_points",
    )(ids, span, att, seen, w, s, rc)


def grid_kernel(geometry, begin, groups, id_ref, span_ref, w_ref, s_ref, rc_ref, *refs):
    levels, all_rows, share, row_scale, col_scale = geometry
    xs, outs, refs = refs[:groups], refs[groups : 2 * groups], refs[2 * groups :]
    xt_ref, acc_ref, q_ref, high_ref, low_ref = refs
    bands = xs[0].shape[0]
    height = levels * all_rows
    rows = outs[0].shape[1] // (share * levels)
    first = [span_ref[begin + p] for p in range(rows)]
    last = [span_ref[all_rows + begin + p] for p in range(rows)]
    cols = bands * LANE
    members = groups * share
    q_ref[...] = (
        lax.broadcasted_iota(jnp.int32, (cols, LANE), 0) + id_ref[1] * cols
    ).astype(F32) * col_scale

    def cells(i):
        return jnp.concatenate(
            [
                jnp.concatenate(
                    [x.at[b][pl.ds(i, share, stride=height), :] for x in xs], axis=0
                )
                for b in range(bands)
            ],
            axis=1,
        )

    for l in range(levels):
        for p in range(rows):
            xt_ref[l * rows + p] = triple(cells(l * all_rows + begin + p))

    half = BLOCK // 2
    spans = [jnp.maximum(last[p] - first[p], 0) for p in range(rows)]
    steps = [(n + half - 1) // BLOCK for n in spans]
    ends = [steps[0]]
    for n in steps[1:]:
        ends.append(ends[-1] + n)
    acc_ref[...] = jnp.zeros(acc_ref.shape, F32)

    def locate(i):
        p = jnp.int32(0)
        at = first[0] + i * BLOCK
        for j in range(1, rows):
            past = i >= ends[j - 1]
            p = jnp.where(past, j, p)
            at = jnp.where(past, first[j] + (i - ends[j - 1]) * BLOCK, at)
        return p, pl.multiple_of(at, LANE)

    def tapered(p, at, width):
        row_gap = (id_ref[0] * all_rows + begin + p).astype(F32) * row_scale - rc_ref[
            0:1, pl.ds(at, width)
        ]
        base = 1.0 - row_gap * row_gap
        q = q_ref[...]
        col_gap = jnp.concatenate([q] * (width // LANE), axis=1) - rc_ref[1:2, pl.ds(at, width)]
        near = jnp.maximum(base - col_gap * col_gap, 0.0)
        return near * near

    def gains(p, l, at, width, taper):
        w = w_ref[l, :, pl.ds(at, width)]
        return split(jnp.dot(xt_ref[l * rows + p], w, preferred_element_type=F32) * taper)

    def add(p, l, at, high, low):
        s = s_ref[pl.ds(at, high.shape[1]), :]
        acc_ref[p, l] += jnp.dot(high, s, preferred_element_type=F32)
        acc_ref[p, l, :, 0:LANE] += jnp.dot(low, s[:, 0:LANE], preferred_element_type=F32)

    def spread(i, l):
        p, at = locate(i)
        add(p, l, at, high_ref[l], low_ref[l])

    def step(i):
        p, at = locate(i)
        taper = tapered(p, at, BLOCK)
        for l in range(levels):
            high, low = gains(p, l, at, BLOCK, taper)
            if l == 0:
                spread(jnp.maximum(i - 1, 0), levels - 1)
            else:
                spread(i, l - 1)
            high_ref[l], low_ref[l] = high, low

    def several(i, _):
        for n in range(4):
            step(4 * i + n)
        return 0

    def single(i, _):
        step(i)
        return 0

    high_ref[levels - 1] = jnp.zeros(high_ref.shape[1:], BF16)
    low_ref[levels - 1] = jnp.zeros(low_ref.shape[1:], BF16)
    lax.fori_loop(0, ends[-1] // 4, several, 0)
    lax.fori_loop(ends[-1] // 4 * 4, ends[-1], single, 0)
    spread(jnp.maximum(ends[-1] - 1, 0), levels - 1)

    def remainder(p, _):
        def of(values):
            chosen = values[0]
            for j in range(1, rows):
                chosen = jnp.where(p == j, values[j], chosen)
            return chosen

        at = pl.multiple_of(of([first[j] + steps[j] * BLOCK for j in range(rows)]), LANE)

        @pl.when(of(spans) > of(steps) * BLOCK)
        def _():
            taper = tapered(p, at, half)
            for l in range(levels):
                add(p, l, at, *gains(p, l, at, half, taper))

        return 0

    lax.fori_loop(0, rows, remainder, 0)

    def store(p, _):
        for l in range(levels):
            at = pl.ds(l * all_rows + begin + p, share, stride=height)
            to = pl.ds(l * rows + p, share, stride=levels * rows)
            inc = (acc_ref[p, l, :, 0:LANE] + acc_ref[p, l, :, LANE : 2 * LANE]).T[0:members]
            for g in range(groups):
                for b in range(bands):
                    outs[g].at[b][to, :] = (
                        xs[g].at[b][at, :]
                        + inc[g * share : (g + 1) * share, b * LANE : (b + 1) * LANE]
                    )
        return 0

    lax.fori_loop(0, rows, store, 0)


def update_grid(geometry, ids, packed, parts, begin, rows):
    w, s, rc, span = packed
    levels, all_rows = geometry[:2]
    groups = len(parts)
    bands, depth, _ = parts[0].shape
    cols = bands * LANE
    out = jax.ShapeDtypeStruct((bands, depth // all_rows * rows, LANE), F32)
    return pl.pallas_call(
        functools.partial(grid_kernel, geometry, begin, groups),
        out_shape=[out] * groups,
        in_specs=[SMEM] * 2 + [VMEM] * (3 + groups),
        out_specs=[VMEM] * groups,
        scratch_shapes=[
            pltpu.VMEM((levels * rows, cols, DEEP), BF16),
            pltpu.VMEM((rows, levels, cols, 2 * LANE), F32),
            pltpu.VMEM((cols, LANE), F32),
            pltpu.VMEM((levels, cols, BLOCK), BF16),
            pltpu.VMEM((levels, cols, BLOCK), BF16),
        ],
        compiler_params=PARAMS,
        cost_estimate=cost(7 * rows),
        name="update_grid",
    )(ids, span, w, s, rc, *parts)


def restore_kernel(groups, id_ref, *refs):
    pieces, befores, out_ref = refs[:groups], refs[groups:-1], refs[-1]
    members, levels, all_rows, _ = out_ref.shape
    bands = pieces[0].shape[0]
    height = pieces[0].shape[1] // members
    rows = height // levels
    begin = all_rows - rows

    def body(m, _):
        at = pl.multiple_of(m * height, height)
        for before in befores:
            for l in range(levels):
                out_ref[m, l, 0:begin, :] = before[m, l]
        for k in range(groups):
            for band in range(bands):
                block = pieces[k][band, pl.ds(at, height), :]
                first = pl.multiple_of((id_ref[1] ^ k) * (bands * LANE) + band * LANE, LANE)
                for l in range(levels):
                    out_ref[m, l, begin:all_rows, pl.ds(first, LANE)] = block[
                        l * rows : (l + 1) * rows
                    ]
        return 0

    lax.fori_loop(0, members, body, 0)


def restore(ids, pieces, befores, shape):
    return pl.pallas_call(
        functools.partial(restore_kernel, len(pieces)),
        out_shape=jax.ShapeDtypeStruct(shape, F32),
        in_specs=[SMEM] + [VMEM] * (len(pieces) + len(befores)),
        out_specs=VMEM,
        compiler_params=PARAMS,
        cost_estimate=cost(2),
        name="restore",
    )(ids, *pieces, *befores)


def shifted(value, steps):
    count = lax.axis_size("tile")
    pairs = [(i, i + steps) for i in range(count) if 0 <= i + steps < count]
    return lax.ppermute(value, "tile", pairs)


def paired(value, odd):
    count = lax.axis_size("tile")
    firsts = range(odd, count - 1, 2)
    pairs = [(i, i + 1) for i in firsts] + [(i + 1, i) for i in firsts]
    return lax.ppermute(value, "tile", pairs)


def window_of(value):
    return [
        shifted(value, 2),
        paired(value, 0),
        value,
        paired(value, 1),
        shifted(value, -2),
    ]


def crossed(value, step):
    count = lax.axis_size("ens")
    return lax.ppermute(value, "ens", [(i, i ^ step) for i in range(count)])


def exchanged(parts):
    return [parts[0]] + [crossed(parts[k], k) for k in range(1, len(parts))]


def on_device(initial_sample_set, flow_velocity, obs_loc, obs_count, obs_value, obs_error):
    x = initial_sample_set
    share, levels, rows, col_total = x.shape
    ens = lax.axis_size("ens")
    ids = jnp.stack([lax.axis_index("tile"), lax.axis_index("ens")]).astype(jnp.int32)
    geometry = (levels, rows, share, 1.0 / (REACH * rows), 1.0 / (col_total // 2))

    top = shifted(x[:, :, rows - 1, :], 1)
    bottom = shifted(lax.optimization_barrier(x)[:, :, 0, :], -1)
    att = order(ids, obs_loc, obs_value, obs_error, obs_count, rows)
    parts = forecast(ids, x, flow_velocity, ens)
    inner, edges = [(1, rows - 2)], [(0, 0), (rows - 1, rows - 1)]
    seen = observe(ids, att[0], parts, levels, share, inner)
    parts = mend(ids, top, bottom, flow_velocity, parts)
    seen = observe(ids, att[0], parts, levels, share, edges, (seen,))
    seen = lax.all_gather(seen, "ens", axis=0)
    parts, seen = lax.optimization_barrier((parts, seen))
    priors = window_of(seen[None])
    ahead = observe(ids, att[1], parts, levels, share, [(0, rows - 1)])
    ahead = lax.all_gather(ahead, "ens", axis=0)
    parts = exchanged(parts)
    priors, parts, ahead = lax.optimization_barrier((priors, parts, ahead))
    packed = pack(geometry, ids, priors)
    later = update_points(geometry, ids, att[1], ahead, packed)
    later = window_of(jnp.stack([later, crossed(later, 1)]))
    parts = update_grid(geometry, ids, packed, parts, 0, rows)
    packed = pack(geometry, ids, later)
    half = rows // 2
    upper = update_grid(geometry, ids, packed, parts, 0, half)
    parts, upper = lax.optimization_barrier((parts, upper))
    lower = update_grid(geometry, ids, packed, parts, half, rows - half)
    done = restore(ids, exchanged(upper), (), (share, levels, half, col_total))
    return restore(ids, exchanged(lower), (done,), x.shape)


def solution(mesh):
    in_specs = (
        P("ens", None, "tile", None),
        P(None, None, "tile", None),
        P(None, None, "tile"),
        P(None, "tile"),
        P(None, "tile"),
        P(None, "tile"),
    )
    out_specs = P("ens", None, "tile", None)
    return jax.shard_map(
        on_device, mesh=mesh, in_specs=in_specs, out_specs=out_specs, check_vma=False
    )
```

```python
import functools

import jax
import jax.numpy as jnp
from jax import lax
from jax.experimental import pallas as pl
from jax.experimental.pallas import tpu as pltpu
from jax.sharding import PartitionSpec as P

BATCHES = 2
REACH = 2
SPARE = 4
SPREAD_RATE = 0.05
EPSILON = 1e-06
LANE = 128
DEEP = 256
BLOCK = 512
F32 = jnp.float32
BF16 = jnp.bfloat16
VMEM = pl.BlockSpec(memory_space=pltpu.VMEM)
SMEM = pl.BlockSpec(memory_space=pltpu.SMEM)
PARAMS = pltpu.CompilerParams(vmem_limit_bytes=32 << 20)


def cost(micros):
    return pl.CostEstimate(flops=int(micros * 1e9), bytes_accessed=0, transcendentals=0)


def split(value):
    high = value.astype(BF16)
    return high, (value - high.astype(F32)).astype(BF16)


def order_kernel(rows, id_ref, loc_ref, value_ref, error_ref, count_ref, att_ref):
    batches, slots = value_ref.shape
    earlier = (
        lax.broadcasted_iota(jnp.int32, (slots, slots), 0)
        < lax.broadcasted_iota(jnp.int32, (slots, slots), 1)
    ).astype(BF16)
    slot = lax.broadcasted_iota(jnp.int32, (1, slots), 1)
    key_of = lax.broadcasted_iota(jnp.int32, (8, slots), 0)
    for b in range(batches):
        count = count_ref[b, 0]
        local_row = loc_ref[0, b : b + 1, :] - id_ref[0] * rows
        key = jnp.where(slot < count, local_row, rows)
        mine = key_of == jnp.broadcast_to(key, (8, slots))
        ones = mine.astype(F32)
        before = jnp.dot(ones.astype(BF16), earlier, preferred_element_type=F32)
        totals = jnp.sum(ones, axis=1, keepdims=True)
        start = jnp.zeros((1, slots), F32)
        place = jnp.zeros((1, slots), F32)
        cumulative = jnp.where(slot == 0, count.astype(F32), 0.0)
        for r in range(rows + 1):
            place = place + ones[r : r + 1] * (before[r : r + 1] + start)
            start = start + totals[r : r + 1]
            cumulative = jnp.where(slot == r + 1, start, cumulative)
        level = loc_ref[2, b : b + 1, :]
        fields = [
            loc_ref[0, b : b + 1, :].astype(F32),
            loc_ref[1, b : b + 1, :].astype(F32),
            level.astype(F32),
            value_ref[b : b + 1, :],
            error_ref[b : b + 1, :],
            (level * rows + local_row).astype(F32),
        ]
        table = jnp.concatenate(fields + [jnp.zeros((2, slots), F32)], axis=0)
        high, low = split(table)
        rest = (table - high.astype(F32) - low.astype(F32)).astype(BF16)
        target = lax.broadcasted_iota(jnp.int32, (slots, slots), 0)
        moved = (target == jnp.broadcast_to(place.astype(jnp.int32), (slots, slots))).astype(BF16)
        out = lax.dot_general(
            jnp.concatenate([high.astype(F32), low.astype(F32), rest.astype(F32)], axis=0).astype(BF16),
            moved,
            (((1,), (1,)), ((), ())),
            preferred_element_type=F32,
        )
        out = (out[0:8] + out[8:16]) + out[16:24]
        att_ref[b] = jnp.concatenate([out[0:5], cumulative, out[5:6], jnp.zeros((1, slots), F32)], axis=0)


def order(ids, obs_loc, obs_value, obs_error, obs_count, rows):
    batches, slots = obs_value.shape
    return pl.pallas_call(
        functools.partial(order_kernel, rows),
        out_shape=jax.ShapeDtypeStruct((batches, 8, slots), F32),
        in_specs=[SMEM, VMEM, VMEM, VMEM, SMEM],
        out_specs=VMEM,
        compiler_params=PARAMS,
        cost_estimate=cost(2),
        name="order",
    )(ids, obs_loc, obs_value, obs_error, obs_count)


def forecast_kernel(id_ref, x_ref, flow_ref, *refs):
    outs, row_ref = refs[:-1], refs[-1]
    members, levels, rows, cols = x_ref.shape
    height = levels * rows
    parts, bands = len(outs), outs[0].shape[0]
    row = lax.broadcasted_iota(jnp.int32, (height, cols), 0)
    col = lax.broadcasted_iota(jnp.int32, (height, cols), 1)
    winds = [
        jnp.concatenate([flow_ref[d, l] for l in range(levels)], axis=0) for d in range(2)
    ]

    def body(m, _):
        x = jnp.concatenate([x_ref[m, l] for l in range(levels)], axis=0)
        above = jnp.where(row % rows == 0, 0.0, pltpu.roll(x, 1, 0))
        below = jnp.where(row % rows == rows - 1, 0.0, pltpu.roll(x, height - 1, 0))
        left = jnp.where(col == 0, 0.0, pltpu.roll(x, 1, 1))
        right = jnp.where(col == cols - 1, 0.0, pltpu.roll(x, cols - 1, 1))
        tendency = (
            jnp.maximum(winds[0], 0.0) * (x - above)
            + jnp.minimum(winds[0], 0.0) * (below - x)
            + jnp.maximum(winds[1], 0.0) * (x - left)
            + jnp.minimum(winds[1], 0.0) * (right - x)
        )
        row_ref[...] = x - tendency + SPREAD_RATE * (above + below + left + right - 4.0 * x)
        at = pl.multiple_of(m * height, height)
        for k in range(parts):
            first = (id_ref[1] ^ k) * (bands * LANE)
            for band in range(bands):
                source = pl.multiple_of(first + band * LANE, LANE)
                outs[k][band, pl.ds(at, height), :] = row_ref[:, pl.ds(source, LANE)]
        return 0

    lax.fori_loop(0, members, body, 0)


def forecast(ids, x, flow, parts):
    members, levels, rows, cols = x.shape
    out = jax.ShapeDtypeStruct((cols // parts // LANE, members * levels * rows, LANE), F32)
    return pl.pallas_call(
        forecast_kernel,
        out_shape=[out] * parts,
        in_specs=[SMEM] + [VMEM] * 2,
        out_specs=[VMEM] * parts,
        scratch_shapes=[pltpu.VMEM((levels * rows, cols), F32)],
        compiler_params=PARAMS,
        cost_estimate=cost(3),
        name="forecast",
    )(ids, x, flow)


def mend_kernel(id_ref, top_ref, bottom_ref, flow_ref, *refs):
    groups = (len(refs) - 1) // 2
    parts, outs, rate_ref = refs[:groups], refs[groups : 2 * groups], refs[-1]
    members, levels, cols = top_ref.shape
    rows = flow_ref.shape[2]
    height = levels * rows
    bands = parts[0].shape[0]
    row = lax.broadcasted_iota(jnp.int32, (height, cols), 0)
    wind = jnp.concatenate([flow_ref[0, l] for l in range(levels)], axis=0)
    rate_ref[0] = jnp.where(row % rows == 0, jnp.maximum(wind, 0.0) + SPREAD_RATE, 0.0)
    rate_ref[1] = jnp.where(row % rows == rows - 1, SPREAD_RATE - jnp.minimum(wind, 0.0), 0.0)

    def spread_rows(value):
        return jnp.concatenate(
            [jnp.broadcast_to(value[l : l + 1], (rows, LANE)) for l in range(levels)], axis=0
        )

    def body(m, _):
        at = pl.multiple_of(m * height, height)
        for k in range(groups):
            for band in range(bands):
                source = pl.multiple_of((id_ref[1] ^ k) * (bands * LANE) + band * LANE, LANE)
                there = pl.ds(source, LANE)
                outs[k][band, pl.ds(at, height), :] = (
                    parts[k][band, pl.ds(at, height), :]
                    + rate_ref[0, :, there] * spread_rows(top_ref[m, :, there])
                    + rate_ref[1, :, there] * spread_rows(bottom_ref[m, :, there])
                )
        return 0

    lax.fori_loop(0, members, body, 0)


def mend(ids, top, bottom, flow, parts):
    _, levels, cols = top.shape
    return pl.pallas_call(
        mend_kernel,
        out_shape=[jax.ShapeDtypeStruct(parts[0].shape, F32)] * len(parts),
        in_specs=[SMEM] + [VMEM] * (3 + len(parts)),
        out_specs=[VMEM] * len(parts),
        scratch_shapes=[pltpu.VMEM((2, levels * flow.shape[2], cols), F32)],
        compiler_params=PARAMS,
        cost_estimate=cost(1),
        name="mend",
    )(ids, top, bottom, flow, *parts)


def fill_spare(put, att, odd):
    even_rows = jnp.concatenate([att[0:3], att[5:6]], axis=0)
    odd_rows = jnp.concatenate([att[3:5], att[3:5]], axis=0)
    put(jnp.where(odd, odd_rows, even_rows))


def number(row, at):
    lane = lax.broadcasted_iota(jnp.int32, (1, LANE), 1)
    return jnp.sum(jnp.where(lane == at, row, 0.0)).astype(jnp.int32)


def observe_kernel(levels, share, groups, ranges, id_ref, att_ref, *refs):
    parts, befores, out_ref = refs[:groups], refs[groups:-1], refs[-1]
    bands = parts[0].shape[0]
    slots = att_ref.shape[1]
    height = parts[0].shape[1] // share
    rows = height // levels
    att = att_ref[...]
    counts = att[5:6, 0:LANE]
    odd = (id_ref[1] & 1) == 1

    def put(rows):
        out_ref[share : share + SPARE, :] = rows

    fill_spare(put, att, odd)

    count = number(counts, 0)
    ends = [number(counts, r + 1) for r in range(rows)]

    def body(n, _, count=count, ends=ends):
        at = pl.multiple_of(n * LANE, LANE)
        begin, end = n * LANE, jnp.minimum(n * LANE + LANE, count) - 1
        low = sum((e <= begin).astype(jnp.int32) for e in ends)
        high = sum((e <= end).astype(jnp.int32) for e in ends)
        column = att_ref[1:2, pl.ds(at, LANE)].astype(jnp.int32)
        flat_row = jnp.broadcast_to(att_ref[6:7, pl.ds(at, LANE)].astype(jnp.int32), (8, LANE))
        band_of = jnp.broadcast_to(column >> 7, (8, LANE))
        lane_of = jnp.broadcast_to(column & (LANE - 1), (8, LANE))
        here = [
            band_of == (id_ref[1] ^ k) * bands + band
            for k in range(len(parts))
            for band in range(bands)
        ]

        def one_row(r, found):
            found = list(found)
            for l in range(levels):
                i = l * rows + r
                mine = flat_row == i
                for c, m in enumerate(range(0, share, 8)):
                    size = min(8, share - m)
                    value = jnp.zeros((8, LANE), F32)
                    for j in range(len(parts) * bands):
                        block = parts[j // bands].at[j % bands][
                            pl.ds(m * height + i, size, stride=height), :
                        ]
                        if size < 8:
                            block = jnp.concatenate(
                                [block, jnp.zeros((8 - size, LANE), F32)], axis=0
                            )
                        picked = jnp.take_along_axis(block, lane_of, axis=1)
                        value = jnp.where(here[j], picked, value)
                    found[c] = jnp.where(mine, value, found[c])
            return tuple(found)

        found = []
        for m in range(0, share, 8):
            size = min(8, share - m)
            value = jnp.zeros((8, LANE), F32)
            for before in befores:
                value = before[m : m + size, pl.ds(at, LANE)]
                if size < 8:
                    value = jnp.concatenate([value, jnp.zeros((8 - size, LANE), F32)], axis=0)
            found.append(value)
        found = tuple(found)
        for begin_row, end_row in ranges:
            found = lax.fori_loop(
                jnp.maximum(low, begin_row), jnp.minimum(high, end_row) + 1, one_row, found
            )
        for c, m in enumerate(range(0, share, 8)):
            size = min(8, share - m)
            out_ref[m : m + size, pl.ds(at, LANE)] = found[c][0:size]
        return 0

    out_ref[0:share, :] = jnp.zeros((share, slots), F32)
    lax.fori_loop(0, (count + LANE - 1) // LANE, body, 0)


def observe(ids, att, parts, levels, share, ranges, befores=()):
    slots = att.shape[1]
    padded = (share + SPARE + 7) // 8 * 8
    return pl.pallas_call(
        functools.partial(observe_kernel, levels, share, len(parts), ranges),
        out_shape=jax.ShapeDtypeStruct((padded, slots), F32),
        in_specs=[SMEM] + [VMEM] * (1 + len(parts) + len(befores)),
        out_specs=VMEM,
        compiler_params=PARAMS,
        cost_estimate=cost(3),
        name="observe",
    )(ids, att, *parts, *befores)


def weigh(prior, value, error, live):
    members = prior.shape[0]
    average = jnp.sum(prior, axis=0, keepdims=True) / members
    deviation = prior - average
    var_prior = jnp.sum(deviation * deviation, axis=0, keepdims=True) / (members - 1) + EPSILON
    combined = var_prior + error
    shrink = jnp.sqrt(error / combined)
    post = (error * average + var_prior * value) / combined
    shift = live * ((shrink - 1.0) * deviation + (post - average))
    weight = (live / ((members - 1) * var_prior)) * deviation
    return weight, shift


def pack_kernel(geometry, window, id_ref, *refs):
    priors, (w_ref, s_ref, rc_ref, span_ref) = refs[:window], refs[window:]
    priors = [priors[0], *priors[2:], priors[1]]
    levels, rows, share, row_scale, col_scale = geometry
    halves, groups, _, width = priors[0].shape
    piece = min(width, BLOCK) if halves == 1 else LANE
    chunk = min(BLOCK, halves * width)
    lane = lax.broadcasted_iota(jnp.int32, (1, LANE), 1)
    counts = [ref[0, 0, share + 3 : share + 4, 0:LANE] for ref in priors]

    totals = [number(row, 0) for row in counts]
    for p in range(rows):
        span_ref[p] = number(counts[0], p + 1) // LANE * LANE
        span_ref[rows + p] = number(counts[-1], p) if p else jnp.int32(0)
    w_ref[:, :, 0:LANE] = jnp.zeros((levels, DEEP, LANE), BF16)
    s_ref[0:LANE, :] = jnp.zeros((LANE, 2 * LANE), BF16)
    rc_ref[:, 0:LANE] = jnp.zeros((8, LANE), F32)
    off = jnp.int32(0)
    starts = []
    for t, ref in enumerate(priors):
        count = totals[t]
        starts.append(off)

        def body(k, _, ref=ref, off=off, count=count):
            src = k * chunk
            each = chunk // (piece * halves)
            half = [(h ^ id_ref[1]) & (halves - 1) for h in range(halves)]

            def taken(g, begin, size):
                return jnp.concatenate(
                    [
                        ref[h, g, begin : begin + size, pl.ds(pl.multiple_of((k * each + n) * piece, piece), piece)]
                        for n in range(each)
                        for h in half
                    ],
                    axis=1,
                )

            slot = lax.broadcasted_iota(jnp.int32, (1, chunk), 1) + src
            live = (slot < count).astype(F32)
            prior = jnp.concatenate(
                [taken(id_ref[1] ^ g, 0, share) for g in range(groups)], axis=0
            )
            place = taken(0, share, SPARE) * live
            seen = taken(1, share, SPARE)
            members = prior.shape[0]
            weight, shift = weigh(prior, seen[0:1], seen[1:2], live)
            table = jnp.concatenate(
                [
                    weight,
                    shift,
                    place[0:1] * row_scale,
                    place[1:2] * col_scale,
                    place[2:3],
                    jnp.zeros((5, chunk), F32),
                ],
                axis=0,
            )
            filled = off & (LANE - 1)
            dst = pl.multiple_of(off - filled + src, LANE)
            turned = [
                pltpu.roll(table[:, n : n + LANE], filled, 1) for n in range(0, chunk, LANE)
            ]
            none = jnp.zeros_like(turned[0])
            table = jnp.concatenate(
                [jnp.where(lane < filled, a, b) for a, b in zip([none] + turned, turned + [none])],
                axis=1,
            )
            first, rest = pl.ds(dst, LANE), pl.ds(pl.multiple_of(dst + LANE, LANE), chunk)
            weight, shift = table[0:members], table[members : 2 * members]
            level = table[2 * members + 2 : 2 * members + 3]
            pad = jnp.zeros((DEEP - 3 * members, chunk + LANE), BF16)
            high, low = split(weight)
            stacked = jnp.concatenate([high, low, high, pad], axis=0)
            for l in range(levels):
                factor = 1.0 / (1.0 + jnp.abs(level - float(l)))
                if levels <= 2:
                    stack = stacked * factor.astype(BF16)
                else:
                    high, low = split(weight * factor)
                    stack = jnp.concatenate([high, low, high, pad], axis=0)
                w_ref[l, :, first] += stack[:, 0:LANE]
                w_ref[l, :, rest] = stack[:, LANE:]
            pad = jnp.zeros((LANE - members, chunk + LANE), F32)
            high, low = split(jnp.concatenate([shift, pad], axis=0).T)
            s_ref[first, 0:LANE] += high[0:LANE]
            s_ref[rest, 0:LANE] = high[LANE:]
            s_ref[first, LANE : 2 * LANE] += low[0:LANE]
            s_ref[rest, LANE : 2 * LANE] = low[LANE:]
            rc_ref[:, first] += table[2 * members :, 0:LANE]
            rc_ref[:, rest] = table[2 * members :, LANE:]
            return 0

        lax.fori_loop(0, (count + chunk - 1) // chunk, body, 0)
        off = off + count
    dst = pl.multiple_of((off + LANE - 1) // LANE * LANE, LANE)
    for l in range(levels):
        w_ref[l, :, pl.ds(dst, 2 * BLOCK)] = jnp.zeros((DEEP, 2 * BLOCK), BF16)
    s_ref[pl.ds(dst, 2 * BLOCK), :] = jnp.zeros((2 * BLOCK, 2 * LANE), BF16)
    rc_ref[:, pl.ds(dst, 2 * BLOCK)] = jnp.zeros((8, 2 * BLOCK), F32)
    for p in range(rows):
        span_ref[rows + p] = starts[-1] + span_ref[rows + p]
    span_ref[2 * rows] = off


def pack(geometry, ids, priors):
    levels, rows = geometry[:2]
    halves, _, _, width = priors[0].shape
    room = len(priors) * halves * width + 2 * BLOCK + 2 * LANE
    return pl.pallas_call(
        functools.partial(pack_kernel, geometry, len(priors)),
        out_shape=[
            jax.ShapeDtypeStruct((levels, DEEP, room), BF16),
            jax.ShapeDtypeStruct((room, 2 * LANE), BF16),
            jax.ShapeDtypeStruct((8, room), F32),
            jax.ShapeDtypeStruct((2 * rows + 1,), jnp.int32),
        ],
        in_specs=[SMEM] + [VMEM] * len(priors),
        out_specs=[VMEM, VMEM, VMEM, SMEM],
        compiler_params=PARAMS,
        cost_estimate=cost(5),
        name="pack",
    )(ids, *priors)


def triple(x):
    high, low = split(x)
    members, width = x.shape
    pad = jnp.zeros((DEEP - 3 * members, width), BF16)
    return jnp.concatenate([high, high, low, pad], axis=0).T


def points_kernel(
    geometry, id_ref, span_ref, att_ref, seen_ref, w_ref, s_ref, rc_ref, out_ref, acc_ref
):
    levels, rows, share, row_scale, col_scale = geometry
    groups, _, width = out_ref.shape
    off = span_ref[2 * rows]
    counts = att_ref[5:6, 0:LANE]
    live = number(counts, 0)
    core = id_ref[1] & 1
    pieces = jnp.maximum((live + LANE - 1) // LANE + 1 - core, 0) // 2

    def lanes(ref, n, count, *index):
        return jnp.concatenate(
            [
                ref[(*index, pl.ds(pl.multiple_of((2 * (n + j) + core) * LANE, LANE), LANE))]
                for j in range(count)
            ],
            axis=-1,
        )

    for n in range(width // LANE):
        att = lanes(att_ref, n, 1, slice(None))
        for g in range(groups):

            def put(value, g=g):
                out_ref[g, share : share + SPARE, n * LANE : (n + 1) * LANE] = value

            fill_spare(put, jnp.concatenate([att[0:5], counts, att[6:8]], axis=0), g % 2 == 1)
            out_ref[g, 0:share, n * LANE : (n + 1) * LANE] = jnp.zeros((share, LANE), F32)

    def update(n, count):
        size = count * LANE
        att = lanes(att_ref, n, count, slice(None))
        x = jnp.concatenate(
            [lanes(seen_ref, n, count, id_ref[1] ^ g, slice(0, share)) for g in range(groups)],
            axis=0,
        )
        cells = triple(x)
        place = jnp.concatenate([att, jnp.zeros((LANE - 8, size), F32)], axis=0).T
        cell_row = place[:, 0:1] * row_scale
        cell_col = place[:, 1:2] * col_scale
        cell_lev = place[:, 2:3]
        acc_ref[0:size] = jnp.zeros((size, 2 * LANE), F32)

        def body(b, width):
            at = pl.multiple_of(b * width, width)
            row_gap = cell_row - rc_ref[0:1, pl.ds(at, width)]
            col_gap = cell_col - rc_ref[1:2, pl.ds(at, width)]
            near = jnp.maximum(1.0 - row_gap * row_gap - col_gap * col_gap, 0.0)
            level = rc_ref[2:3, pl.ds(at, width)]
            ratio = jnp.ones((size, width), F32)
            for l in range(1, levels):
                other = (1.0 + level) / (1.0 + jnp.abs(level - float(l)))
                ratio = jnp.where(cell_lev == float(l), other, ratio)
            cov = jnp.dot(cells, w_ref[0, :, pl.ds(at, width)], preferred_element_type=F32)
            high, low = split(cov * (near * near) * ratio)
            s = s_ref[pl.ds(at, width), :]
            acc_ref[0:size] += jnp.dot(high, s, preferred_element_type=F32)
            acc_ref[0:size, 0:LANE] += jnp.dot(low, s[:, 0:LANE], preferred_element_type=F32)

        def pair(b, _):
            body(2 * b, BLOCK)
            body(2 * b + 1, BLOCK)
            return 0

        def half(b, _):
            body(b, BLOCK // 2)
            return 0

        pairs = off // (2 * BLOCK)
        lax.fori_loop(0, pairs, pair, 0)
        lax.fori_loop(4 * pairs, (off + BLOCK // 2 - 1) // (BLOCK // 2), half, 0)
        out = x + (acc_ref[0:size, 0:LANE] + acc_ref[0:size, LANE : 2 * LANE]).T[0 : groups * share]
        for g in range(groups):
            out_ref[id_ref[1] ^ g, 0:share, n * LANE : n * LANE + size] = out[
                g * share : (g + 1) * share
            ]

    for n in range(0, width // LANE, 2):
        if n + 2 <= width // LANE:
            pl.when(pieces >= n + 2)(functools.partial(update, n, 2))
        pl.when(pieces == n + 1)(functools.partial(update, n, 1))


def update_points(geometry, ids, att, seen, packed):
    w, s, rc, span = packed
    groups, padded, slots = seen.shape
    return pl.pallas_call(
        functools.partial(points_kernel, geometry),
        out_shape=jax.ShapeDtypeStruct((groups, padded, slots // 2), F32),
        in_specs=[SMEM] * 2 + [VMEM] * 5,
        out_specs=VMEM,
        scratch_shapes=[pltpu.VMEM((2 * LANE, 2 * LANE), F32)],
        compiler_params=PARAMS,
        cost_estimate=cost(8),
        name="update_points",
    )(ids, span, att, seen, w, s, rc)


def grid_kernel(geometry, begin, groups, id_ref, span_ref, w_ref, s_ref, rc_ref, *refs):
    levels, all_rows, share, row_scale, col_scale = geometry
    xs, outs, refs = refs[:groups], refs[groups : 2 * groups], refs[2 * groups :]
    xt_ref, acc_ref, q_ref, high_ref, low_ref = refs
    bands = xs[0].shape[0]
    height = levels * all_rows
    rows = outs[0].shape[1] // (share * levels)
    first = [span_ref[begin + p] for p in range(rows)]
    last = [span_ref[all_rows + begin + p] for p in range(rows)]
    cols = bands * LANE
    members = groups * share
    q_ref[...] = (
        lax.broadcasted_iota(jnp.int32, (cols, LANE), 0) + id_ref[1] * cols
    ).astype(F32) * col_scale

    def cells(i):
        return jnp.concatenate(
            [
                jnp.concatenate(
                    [x.at[b][pl.ds(i, share, stride=height), :] for x in xs], axis=0
                )
                for b in range(bands)
            ],
            axis=1,
        )

    for l in range(levels):
        for p in range(rows):
            xt_ref[l * rows + p] = triple(cells(l * all_rows + begin + p))

    half = BLOCK // 2
    spans = [jnp.maximum(last[p] - first[p], 0) for p in range(rows)]
    steps = [(n + half - 1) // BLOCK for n in spans]
    ends = [steps[0]]
    for n in steps[1:]:
        ends.append(ends[-1] + n)
    acc_ref[...] = jnp.zeros(acc_ref.shape, F32)

    def locate(i):
        p = jnp.int32(0)
        at = first[0] + i * BLOCK
        for j in range(1, rows):
            past = i >= ends[j - 1]
            p = jnp.where(past, j, p)
            at = jnp.where(past, first[j] + (i - ends[j - 1]) * BLOCK, at)
        return p, pl.multiple_of(at, LANE)

    def tapered(p, at, width):
        row_gap = (id_ref[0] * all_rows + begin + p).astype(F32) * row_scale - rc_ref[
            0:1, pl.ds(at, width)
        ]
        base = 1.0 - row_gap * row_gap
        q = q_ref[...]
        col_gap = jnp.concatenate([q] * (width // LANE), axis=1) - rc_ref[1:2, pl.ds(at, width)]
        near = jnp.maximum(base - col_gap * col_gap, 0.0)
        return near * near

    def gains(p, l, at, width, taper):
        w = w_ref[l, :, pl.ds(at, width)]
        return split(jnp.dot(xt_ref[l * rows + p], w, preferred_element_type=F32) * taper)

    def add(p, l, at, high, low):
        s = s_ref[pl.ds(at, high.shape[1]), :]
        acc_ref[p, l] += jnp.dot(high, s, preferred_element_type=F32)
        acc_ref[p, l, :, 0:LANE] += jnp.dot(low, s[:, 0:LANE], preferred_element_type=F32)

    def spread(i, l):
        p, at = locate(i)
        add(p, l, at, high_ref[l], low_ref[l])

    def step(i):
        p, at = locate(i)
        taper = tapered(p, at, BLOCK)
        for l in range(levels):
            high, low = gains(p, l, at, BLOCK, taper)
            if l == 0:
                spread(jnp.maximum(i - 1, 0), levels - 1)
            else:
                spread(i, l - 1)
            high_ref[l], low_ref[l] = high, low

    def several(i, _):
        for n in range(4):
            step(4 * i + n)
        return 0

    def single(i, _):
        step(i)
        return 0

    high_ref[levels - 1] = jnp.zeros(high_ref.shape[1:], BF16)
    low_ref[levels - 1] = jnp.zeros(low_ref.shape[1:], BF16)
    lax.fori_loop(0, ends[-1] // 4, several, 0)
    lax.fori_loop(ends[-1] // 4 * 4, ends[-1], single, 0)
    spread(jnp.maximum(ends[-1] - 1, 0), levels - 1)

    def remainder(p, _):
        def of(values):
            chosen = values[0]
            for j in range(1, rows):
                chosen = jnp.where(p == j, values[j], chosen)
            return chosen

        at = pl.multiple_of(of([first[j] + steps[j] * BLOCK for j in range(rows)]), LANE)

        @pl.when(of(spans) > of(steps) * BLOCK)
        def _():
            taper = tapered(p, at, half)
            for l in range(levels):
                add(p, l, at, *gains(p, l, at, half, taper))

        return 0

    lax.fori_loop(0, rows, remainder, 0)

    def store(p, _):
        for l in range(levels):
            at = pl.ds(l * all_rows + begin + p, share, stride=height)
            to = pl.ds(l * rows + p, share, stride=levels * rows)
            inc = (acc_ref[p, l, :, 0:LANE] + acc_ref[p, l, :, LANE : 2 * LANE]).T[0:members]
            for g in range(groups):
                for b in range(bands):
                    outs[g].at[b][to, :] = (
                        xs[g].at[b][at, :]
                        + inc[g * share : (g + 1) * share, b * LANE : (b + 1) * LANE]
                    )
        return 0

    lax.fori_loop(0, rows, store, 0)


def update_grid(geometry, ids, packed, parts, begin, rows):
    w, s, rc, span = packed
    levels, all_rows = geometry[:2]
    groups = len(parts)
    bands, depth, _ = parts[0].shape
    cols = bands * LANE
    out = jax.ShapeDtypeStruct((bands, depth // all_rows * rows, LANE), F32)
    return pl.pallas_call(
        functools.partial(grid_kernel, geometry, begin, groups),
        out_shape=[out] * groups,
        in_specs=[SMEM] * 2 + [VMEM] * (3 + groups),
        out_specs=[VMEM] * groups,
        scratch_shapes=[
            pltpu.VMEM((levels * rows, cols, DEEP), BF16),
            pltpu.VMEM((rows, levels, cols, 2 * LANE), F32),
            pltpu.VMEM((cols, LANE), F32),
            pltpu.VMEM((levels, cols, BLOCK), BF16),
            pltpu.VMEM((levels, cols, BLOCK), BF16),
        ],
        compiler_params=PARAMS,
        cost_estimate=cost(7 * rows),
        name="update_grid",
    )(ids, span, w, s, rc, *parts)


def restore_kernel(groups, id_ref, *refs):
    pieces, befores, out_ref = refs[:groups], refs[groups:-1], refs[-1]
    members, levels, all_rows, _ = out_ref.shape
    bands = pieces[0].shape[0]
    height = pieces[0].shape[1] // members
    rows = height // levels
    begin = all_rows - rows

    def body(m, _):
        at = pl.multiple_of(m * height, height)
        for before in befores:
            for l in range(levels):
                out_ref[m, l, 0:begin, :] = before[m, l]
        for k in range(groups):
            for band in range(bands):
                block = pieces[k][band, pl.ds(at, height), :]
                first = pl.multiple_of((id_ref[1] ^ k) * (bands * LANE) + band * LANE, LANE)
                for l in range(levels):
                    out_ref[m, l, begin:all_rows, pl.ds(first, LANE)] = block[
                        l * rows : (l + 1) * rows
                    ]
        return 0

    lax.fori_loop(0, members, body, 0)


def restore(ids, pieces, befores, shape):
    return pl.pallas_call(
        functools.partial(restore_kernel, len(pieces)),
        out_shape=jax.ShapeDtypeStruct(shape, F32),
        in_specs=[SMEM] + [VMEM] * (len(pieces) + len(befores)),
        out_specs=VMEM,
        compiler_params=PARAMS,
        cost_estimate=cost(2),
        name="restore",
    )(ids, *pieces, *befores)


def shifted(value, steps):
    count = lax.axis_size("tile")
    pairs = [(i, i + steps) for i in range(count) if 0 <= i + steps < count]
    return lax.ppermute(value, "tile", pairs)


def paired(value, odd):
    count = lax.axis_size("tile")
    firsts = range(odd, count - 1, 2)
    pairs = [(i, i + 1) for i in firsts] + [(i + 1, i) for i in firsts]
    return lax.ppermute(value, "tile", pairs)


def window_of(value):
    return [
        shifted(value, 2),
        shifted(value, -2),
        value,
        paired(value, 0),
        paired(value, 1),
    ]


def crossed(value, step):
    count = lax.axis_size("ens")
    return lax.ppermute(value, "ens", [(i, i ^ step) for i in range(count)])


def exchanged(parts):
    return [parts[0]] + [crossed(parts[k], k) for k in range(1, len(parts))]


def on_device(initial_sample_set, flow_velocity, obs_loc, obs_count, obs_value, obs_error):
    x = initial_sample_set
    share, levels, rows, col_total = x.shape
    ens = lax.axis_size("ens")
    ids = jnp.stack([lax.axis_index("tile"), lax.axis_index("ens")]).astype(jnp.int32)
    geometry = (levels, rows, share, 1.0 / (REACH * rows), 1.0 / (col_total // 2))

    top = shifted(x[:, :, rows - 1, :], 1)
    bottom = shifted(lax.optimization_barrier(x)[:, :, 0, :], -1)
    att = order(ids, obs_loc, obs_value, obs_error, obs_count, rows)
    parts = forecast(ids, x, flow_velocity, ens)
    inner, edges = [(1, rows - 2)], [(0, 0), (rows - 1, rows - 1)]
    seen = observe(ids, att[0], parts, levels, share, inner)
    parts = mend(ids, top, bottom, flow_velocity, parts)
    seen = observe(ids, att[0], parts, levels, share, edges, (seen,))
    seen = lax.all_gather(seen, "ens", axis=0)
    parts, seen = lax.optimization_barrier((parts, seen))
    priors = window_of(seen[None])
    ahead = observe(ids, att[1], parts, levels, share, [(0, rows - 1)])
    ahead = lax.all_gather(ahead, "ens", axis=0)
    parts, ahead = lax.optimization_barrier((parts, ahead))
    parts = exchanged(parts)
    priors, ahead = lax.optimization_barrier((priors, ahead))
    packed = pack(geometry, ids, priors)
    later = update_points(geometry, ids, att[1], ahead, packed)
    later = window_of(jnp.stack([later, crossed(later, 1)]))
    parts = update_grid(geometry, ids, packed, parts, 0, rows)
    packed = pack(geometry, ids, later)
    half = rows // 2
    upper = update_grid(geometry, ids, packed, parts, 0, half)
    parts, upper = lax.optimization_barrier((parts, upper))
    lower = update_grid(geometry, ids, packed, parts, half, rows - half)
    done = restore(ids, exchanged(upper), (), (share, levels, half, col_total))
    return restore(ids, exchanged(lower), (done,), x.shape)


def solution(mesh):
    in_specs = (
        P("ens", None, "tile", None),
        P(None, None, "tile", None),
        P(None, None, "tile"),
        P(None, "tile"),
        P(None, "tile"),
        P(None, "tile"),
    )
    out_specs = P("ens", None, "tile", None)
    return jax.shard_map(
        on_device, mesh=mesh, in_specs=in_specs, out_specs=out_specs, check_vma=False
    )
```

```python
import functools

import jax
import jax.numpy as jnp
from jax import lax
from jax.experimental import pallas as pl
from jax.experimental.pallas import tpu as pltpu
from jax.sharding import PartitionSpec as P

BATCHES = 2
REACH = 2
SPARE = 4
SPREAD_RATE = 0.05
EPSILON = 1e-06
LANE = 128
DEEP = 256
BLOCK = 512
F32 = jnp.float32
BF16 = jnp.bfloat16
VMEM = pl.BlockSpec(memory_space=pltpu.VMEM)
SMEM = pl.BlockSpec(memory_space=pltpu.SMEM)
PARAMS = pltpu.CompilerParams(vmem_limit_bytes=32 << 20)


def cost(micros):
    return pl.CostEstimate(flops=int(micros * 1e9), bytes_accessed=0, transcendentals=0)


def split(value):
    high = value.astype(BF16)
    return high, (value - high.astype(F32)).astype(BF16)


def order_kernel(rows, id_ref, loc_ref, value_ref, error_ref, count_ref, att_ref):
    batches, slots = value_ref.shape
    earlier = (
        lax.broadcasted_iota(jnp.int32, (slots, slots), 0)
        < lax.broadcasted_iota(jnp.int32, (slots, slots), 1)
    ).astype(BF16)
    slot = lax.broadcasted_iota(jnp.int32, (1, slots), 1)
    key_of = lax.broadcasted_iota(jnp.int32, (8, slots), 0)
    for b in range(batches):
        count = count_ref[b, 0]
        local_row = loc_ref[0, b : b + 1, :] - id_ref[0] * rows
        key = jnp.where(slot < count, local_row, rows)
        mine = key_of == jnp.broadcast_to(key, (8, slots))
        ones = mine.astype(F32)
        before = jnp.dot(ones.astype(BF16), earlier, preferred_element_type=F32)
        totals = jnp.sum(ones, axis=1, keepdims=True)
        start = jnp.zeros((1, slots), F32)
        place = jnp.zeros((1, slots), F32)
        cumulative = jnp.where(slot == 0, count.astype(F32), 0.0)
        for r in range(rows + 1):
            place = place + ones[r : r + 1] * (before[r : r + 1] + start)
            start = start + totals[r : r + 1]
            cumulative = jnp.where(slot == r + 1, start, cumulative)
        level = loc_ref[2, b : b + 1, :]
        fields = [
            loc_ref[0, b : b + 1, :].astype(F32),
            loc_ref[1, b : b + 1, :].astype(F32),
            level.astype(F32),
            value_ref[b : b + 1, :],
            error_ref[b : b + 1, :],
            (level * rows + local_row).astype(F32),
        ]
        table = jnp.concatenate(fields + [jnp.zeros((2, slots), F32)], axis=0)
        high, low = split(table)
        rest = (table - high.astype(F32) - low.astype(F32)).astype(BF16)
        target = lax.broadcasted_iota(jnp.int32, (slots, slots), 0)
        moved = (target == jnp.broadcast_to(place.astype(jnp.int32), (slots, slots))).astype(BF16)
        out = lax.dot_general(
            jnp.concatenate([high.astype(F32), low.astype(F32), rest.astype(F32)], axis=0).astype(BF16),
            moved,
            (((1,), (1,)), ((), ())),
            preferred_element_type=F32,
        )
        out = (out[0:8] + out[8:16]) + out[16:24]
        att_ref[b] = jnp.concatenate([out[0:5], cumulative, out[5:6], jnp.zeros((1, slots), F32)], axis=0)


def order(ids, obs_loc, obs_value, obs_error, obs_count, rows):
    batches, slots = obs_value.shape
    return pl.pallas_call(
        functools.partial(order_kernel, rows),
        out_shape=jax.ShapeDtypeStruct((batches, 8, slots), F32),
        in_specs=[SMEM, VMEM, VMEM, VMEM, SMEM],
        out_specs=VMEM,
        compiler_params=PARAMS,
        cost_estimate=cost(2),
        name="order",
    )(ids, obs_loc, obs_value, obs_error, obs_count)


def forecast_kernel(id_ref, x_ref, flow_ref, *refs):
    outs, row_ref = refs[:-1], refs[-1]
    members, levels, rows, cols = x_ref.shape
    height = levels * rows
    parts, bands = len(outs), outs[0].shape[0]
    row = lax.broadcasted_iota(jnp.int32, (height, cols), 0)
    col = lax.broadcasted_iota(jnp.int32, (height, cols), 1)
    winds = [
        jnp.concatenate([flow_ref[d, l] for l in range(levels)], axis=0) for d in range(2)
    ]

    def body(m, _):
        x = jnp.concatenate([x_ref[m, l] for l in range(levels)], axis=0)
        above = jnp.where(row % rows == 0, 0.0, pltpu.roll(x, 1, 0))
        below = jnp.where(row % rows == rows - 1, 0.0, pltpu.roll(x, height - 1, 0))
        left = jnp.where(col == 0, 0.0, pltpu.roll(x, 1, 1))
        right = jnp.where(col == cols - 1, 0.0, pltpu.roll(x, cols - 1, 1))
        tendency = (
            jnp.maximum(winds[0], 0.0) * (x - above)
            + jnp.minimum(winds[0], 0.0) * (below - x)
            + jnp.maximum(winds[1], 0.0) * (x - left)
            + jnp.minimum(winds[1], 0.0) * (right - x)
        )
        row_ref[...] = x - tendency + SPREAD_RATE * (above + below + left + right - 4.0 * x)
        at = pl.multiple_of(m * height, height)
        for k in range(parts):
            first = (id_ref[1] ^ k) * (bands * LANE)
            for band in range(bands):
                source = pl.multiple_of(first + band * LANE, LANE)
                outs[k][band, pl.ds(at, height), :] = row_ref[:, pl.ds(source, LANE)]
        return 0

    lax.fori_loop(0, members, body, 0)


def forecast(ids, x, flow, parts):
    members, levels, rows, cols = x.shape
    out = jax.ShapeDtypeStruct((cols // parts // LANE, members * levels * rows, LANE), F32)
    return pl.pallas_call(
        forecast_kernel,
        out_shape=[out] * parts,
        in_specs=[SMEM] + [VMEM] * 2,
        out_specs=[VMEM] * parts,
        scratch_shapes=[pltpu.VMEM((levels * rows, cols), F32)],
        compiler_params=PARAMS,
        cost_estimate=cost(3),
        name="forecast",
    )(ids, x, flow)


def mend_kernel(id_ref, even_ref, odd_ref, flow_ref, *refs):
    groups = (len(refs) - 1) // 2
    parts, outs, rate_ref = refs[:groups], refs[groups : 2 * groups], refs[-1]
    members, levels, cols = even_ref.shape
    odd = (id_ref[0] & 1) == 1
    rows = flow_ref.shape[2]
    height = levels * rows
    bands = parts[0].shape[0]
    row = lax.broadcasted_iota(jnp.int32, (height, cols), 0)
    wind = jnp.concatenate([flow_ref[0, l] for l in range(levels)], axis=0)
    rate_ref[0] = jnp.where(row % rows == 0, jnp.maximum(wind, 0.0) + SPREAD_RATE, 0.0)
    rate_ref[1] = jnp.where(row % rows == rows - 1, SPREAD_RATE - jnp.minimum(wind, 0.0), 0.0)

    def spread_rows(value):
        return jnp.concatenate(
            [jnp.broadcast_to(value[l : l + 1], (rows, LANE)) for l in range(levels)], axis=0
        )

    def body(m, _):
        at = pl.multiple_of(m * height, height)
        for k in range(groups):
            for band in range(bands):
                source = pl.multiple_of((id_ref[1] ^ k) * (bands * LANE) + band * LANE, LANE)
                there = pl.ds(source, LANE)
                by_even, by_odd = even_ref[m, :, there], odd_ref[m, :, there]
                outs[k][band, pl.ds(at, height), :] = (
                    parts[k][band, pl.ds(at, height), :]
                    + rate_ref[0, :, there] * spread_rows(jnp.where(odd, by_even, by_odd))
                    + rate_ref[1, :, there] * spread_rows(jnp.where(odd, by_odd, by_even))
                )
        return 0

    lax.fori_loop(0, members, body, 0)


def mend(ids, even_row, odd_row, flow, parts):
    _, levels, cols = even_row.shape
    return pl.pallas_call(
        mend_kernel,
        out_shape=[jax.ShapeDtypeStruct(parts[0].shape, F32)] * len(parts),
        in_specs=[SMEM] + [VMEM] * (3 + len(parts)),
        out_specs=[VMEM] * len(parts),
        scratch_shapes=[pltpu.VMEM((2, levels * flow.shape[2], cols), F32)],
        compiler_params=PARAMS,
        cost_estimate=cost(1),
        name="mend",
    )(ids, even_row, odd_row, flow, *parts)


def fill_spare(put, att, odd):
    even_rows = jnp.concatenate([att[0:3], att[5:6]], axis=0)
    odd_rows = jnp.concatenate([att[3:5], att[3:5]], axis=0)
    put(jnp.where(odd, odd_rows, even_rows))


def number(row, at):
    lane = lax.broadcasted_iota(jnp.int32, (1, LANE), 1)
    return jnp.sum(jnp.where(lane == at, row, 0.0)).astype(jnp.int32)


def observe_kernel(levels, share, groups, ranges, id_ref, att_ref, *refs):
    parts, befores, out_ref = refs[:groups], refs[groups:-1], refs[-1]
    bands = parts[0].shape[0]
    slots = att_ref.shape[1]
    height = parts[0].shape[1] // share
    rows = height // levels
    att = att_ref[...]
    counts = att[5:6, 0:LANE]
    odd = (id_ref[1] & 1) == 1

    def put(rows):
        out_ref[share : share + SPARE, :] = rows

    fill_spare(put, att, odd)

    count = number(counts, 0)
    ends = [number(counts, r + 1) for r in range(rows)]

    def body(n, _, count=count, ends=ends):
        at = pl.multiple_of(n * LANE, LANE)
        begin, end = n * LANE, jnp.minimum(n * LANE + LANE, count) - 1
        low = sum((e <= begin).astype(jnp.int32) for e in ends)
        high = sum((e <= end).astype(jnp.int32) for e in ends)
        column = att_ref[1:2, pl.ds(at, LANE)].astype(jnp.int32)
        flat_row = jnp.broadcast_to(att_ref[6:7, pl.ds(at, LANE)].astype(jnp.int32), (8, LANE))
        band_of = jnp.broadcast_to(column >> 7, (8, LANE))
        lane_of = jnp.broadcast_to(column & (LANE - 1), (8, LANE))
        here = [
            band_of == (id_ref[1] ^ k) * bands + band
            for k in range(len(parts))
            for band in range(bands)
        ]

        def one_row(r, found):
            found = list(found)
            for l in range(levels):
                i = l * rows + r
                mine = flat_row == i
                for c, m in enumerate(range(0, share, 8)):
                    size = min(8, share - m)
                    value = jnp.zeros((8, LANE), F32)
                    for j in range(len(parts) * bands):
                        block = parts[j // bands].at[j % bands][
                            pl.ds(m * height + i, size, stride=height), :
                        ]
                        if size < 8:
                            block = jnp.concatenate(
                                [block, jnp.zeros((8 - size, LANE), F32)], axis=0
                            )
                        picked = jnp.take_along_axis(block, lane_of, axis=1)
                        value = jnp.where(here[j], picked, value)
                    found[c] = jnp.where(mine, value, found[c])
            return tuple(found)

        found = []
        for m in range(0, share, 8):
            size = min(8, share - m)
            value = jnp.zeros((8, LANE), F32)
            for before in befores:
                value = before[m : m + size, pl.ds(at, LANE)]
                if size < 8:
                    value = jnp.concatenate([value, jnp.zeros((8 - size, LANE), F32)], axis=0)
            found.append(value)
        found = tuple(found)
        for begin_row, end_row in ranges:
            found = lax.fori_loop(
                jnp.maximum(low, begin_row), jnp.minimum(high, end_row) + 1, one_row, found
            )
        for c, m in enumerate(range(0, share, 8)):
            size = min(8, share - m)
            out_ref[m : m + size, pl.ds(at, LANE)] = found[c][0:size]
        return 0

    out_ref[0:share, :] = jnp.zeros((share, slots), F32)
    lax.fori_loop(0, (count + LANE - 1) // LANE, body, 0)


def observe(ids, att, parts, levels, share, ranges, befores=()):
    slots = att.shape[1]
    padded = (share + SPARE + 7) // 8 * 8
    return pl.pallas_call(
        functools.partial(observe_kernel, levels, share, len(parts), ranges),
        out_shape=jax.ShapeDtypeStruct((padded, slots), F32),
        in_specs=[SMEM] + [VMEM] * (1 + len(parts) + len(befores)),
        out_specs=VMEM,
        compiler_params=PARAMS,
        cost_estimate=cost(3),
        name="observe",
    )(ids, att, *parts, *befores)


def weigh(prior, value, error, live):
    members = prior.shape[0]
    average = jnp.sum(prior, axis=0, keepdims=True) / members
    deviation = prior - average
    var_prior = jnp.sum(deviation * deviation, axis=0, keepdims=True) / (members - 1) + EPSILON
    combined = var_prior + error
    shrink = jnp.sqrt(error / combined)
    post = (error * average + var_prior * value) / combined
    shift = live * ((shrink - 1.0) * deviation + (post - average))
    weight = (live / ((members - 1) * var_prior)) * deviation
    return weight, shift


def pack_kernel(geometry, window, id_ref, *refs):
    priors, (w_ref, s_ref, rc_ref, span_ref) = refs[:window], refs[window:]
    priors = [priors[0], *priors[2:], priors[1]]
    levels, rows, share, row_scale, col_scale = geometry
    halves, groups, _, width = priors[0].shape
    piece = min(width, BLOCK) if halves == 1 else LANE
    chunk = min(BLOCK, halves * width)
    lane = lax.broadcasted_iota(jnp.int32, (1, LANE), 1)
    counts = [ref[0, 0, share + 3 : share + 4, 0:LANE] for ref in priors]

    totals = [number(row, 0) for row in counts]
    for p in range(rows):
        span_ref[p] = number(counts[0], p + 1) // LANE * LANE
        span_ref[rows + p] = number(counts[-1], p) if p else jnp.int32(0)
    w_ref[:, :, 0:LANE] = jnp.zeros((levels, DEEP, LANE), BF16)
    s_ref[0:LANE, :] = jnp.zeros((LANE, 2 * LANE), BF16)
    rc_ref[:, 0:LANE] = jnp.zeros((8, LANE), F32)
    off = jnp.int32(0)
    starts = []
    for t, ref in enumerate(priors):
        count = totals[t]
        starts.append(off)

        def body(k, _, ref=ref, off=off, count=count):
            src = k * chunk
            each = chunk // (piece * halves)
            half = [(h ^ id_ref[1]) & (halves - 1) for h in range(halves)]

            def taken(g, begin, size):
                return jnp.concatenate(
                    [
                        ref[h, g, begin : begin + size, pl.ds(pl.multiple_of((k * each + n) * piece, piece), piece)]
                        for n in range(each)
                        for h in half
                    ],
                    axis=1,
                )

            slot = lax.broadcasted_iota(jnp.int32, (1, chunk), 1) + src
            live = (slot < count).astype(F32)
            prior = jnp.concatenate(
                [taken(id_ref[1] ^ g, 0, share) for g in range(groups)], axis=0
            )
            place = taken(0, share, SPARE) * live
            seen = taken(1, share, SPARE)
            members = prior.shape[0]
            weight, shift = weigh(prior, seen[0:1], seen[1:2], live)
            table = jnp.concatenate(
                [
                    weight,
                    shift,
                    place[0:1] * row_scale,
                    place[1:2] * col_scale,
                    place[2:3],
                    jnp.zeros((5, chunk), F32),
                ],
                axis=0,
            )
            filled = off & (LANE - 1)
            dst = pl.multiple_of(off - filled + src, LANE)
            turned = [
                pltpu.roll(table[:, n : n + LANE], filled, 1) for n in range(0, chunk, LANE)
            ]
            none = jnp.zeros_like(turned[0])
            table = jnp.concatenate(
                [jnp.where(lane < filled, a, b) for a, b in zip([none] + turned, turned + [none])],
                axis=1,
            )
            first, rest = pl.ds(dst, LANE), pl.ds(pl.multiple_of(dst + LANE, LANE), chunk)
            weight, shift = table[0:members], table[members : 2 * members]
            level = table[2 * members + 2 : 2 * members + 3]
            pad = jnp.zeros((DEEP - 3 * members, chunk + LANE), BF16)
            high, low = split(weight)
            stacked = jnp.concatenate([high, low, high, pad], axis=0)
            for l in range(levels):
                factor = 1.0 / (1.0 + jnp.abs(level - float(l)))
                if levels <= 2:
                    stack = stacked * factor.astype(BF16)
                else:
                    high, low = split(weight * factor)
                    stack = jnp.concatenate([high, low, high, pad], axis=0)
                w_ref[l, :, first] += stack[:, 0:LANE]
                w_ref[l, :, rest] = stack[:, LANE:]
            pad = jnp.zeros((LANE - members, chunk + LANE), F32)
            high, low = split(jnp.concatenate([shift, pad], axis=0).T)
            s_ref[first, 0:LANE] += high[0:LANE]
            s_ref[rest, 0:LANE] = high[LANE:]
            s_ref[first, LANE : 2 * LANE] += low[0:LANE]
            s_ref[rest, LANE : 2 * LANE] = low[LANE:]
            rc_ref[:, first] += table[2 * members :, 0:LANE]
            rc_ref[:, rest] = table[2 * members :, LANE:]
            return 0

        lax.fori_loop(0, (count + chunk - 1) // chunk, body, 0)
        off = off + count
    dst = pl.multiple_of((off + LANE - 1) // LANE * LANE, LANE)
    for l in range(levels):
        w_ref[l, :, pl.ds(dst, 2 * BLOCK)] = jnp.zeros((DEEP, 2 * BLOCK), BF16)
    s_ref[pl.ds(dst, 2 * BLOCK), :] = jnp.zeros((2 * BLOCK, 2 * LANE), BF16)
    rc_ref[:, pl.ds(dst, 2 * BLOCK)] = jnp.zeros((8, 2 * BLOCK), F32)
    for p in range(rows):
        span_ref[rows + p] = starts[-1] + span_ref[rows + p]
    span_ref[2 * rows] = off


def pack(geometry, ids, priors):
    levels, rows = geometry[:2]
    halves, _, _, width = priors[0].shape
    room = len(priors) * halves * width + 2 * BLOCK + 2 * LANE
    return pl.pallas_call(
        functools.partial(pack_kernel, geometry, len(priors)),
        out_shape=[
            jax.ShapeDtypeStruct((levels, DEEP, room), BF16),
            jax.ShapeDtypeStruct((room, 2 * LANE), BF16),
            jax.ShapeDtypeStruct((8, room), F32),
            jax.ShapeDtypeStruct((2 * rows + 1,), jnp.int32),
        ],
        in_specs=[SMEM] + [VMEM] * len(priors),
        out_specs=[VMEM, VMEM, VMEM, SMEM],
        compiler_params=PARAMS,
        cost_estimate=cost(5),
        name="pack",
    )(ids, *priors)


def triple(x):
    high, low = split(x)
    members, width = x.shape
    pad = jnp.zeros((DEEP - 3 * members, width), BF16)
    return jnp.concatenate([high, high, low, pad], axis=0).T


def points_kernel(
    geometry, id_ref, span_ref, att_ref, seen_ref, w_ref, s_ref, rc_ref, out_ref, acc_ref
):
    levels, rows, share, row_scale, col_scale = geometry
    groups, _, width = out_ref.shape
    off = span_ref[2 * rows]
    counts = att_ref[5:6, 0:LANE]
    live = number(counts, 0)
    core = id_ref[1] & 1
    pieces = jnp.maximum((live + LANE - 1) // LANE + 1 - core, 0) // 2

    def lanes(ref, n, count, *index):
        return jnp.concatenate(
            [
                ref[(*index, pl.ds(pl.multiple_of((2 * (n + j) + core) * LANE, LANE), LANE))]
                for j in range(count)
            ],
            axis=-1,
        )

    for n in range(width // LANE):
        att = lanes(att_ref, n, 1, slice(None))
        for g in range(groups):

            def put(value, g=g):
                out_ref[g, share : share + SPARE, n * LANE : (n + 1) * LANE] = value

            fill_spare(put, jnp.concatenate([att[0:5], counts, att[6:8]], axis=0), g % 2 == 1)
            out_ref[g, 0:share, n * LANE : (n + 1) * LANE] = jnp.zeros((share, LANE), F32)

    def update(n, count):
        size = count * LANE
        att = lanes(att_ref, n, count, slice(None))
        x = jnp.concatenate(
            [lanes(seen_ref, n, count, id_ref[1] ^ g, slice(0, share)) for g in range(groups)],
            axis=0,
        )
        cells = triple(x)
        place = jnp.concatenate([att, jnp.zeros((LANE - 8, size), F32)], axis=0).T
        cell_row = place[:, 0:1] * row_scale
        cell_col = place[:, 1:2] * col_scale
        cell_lev = place[:, 2:3]
        acc_ref[0:size] = jnp.zeros((size, 2 * LANE), F32)

        def body(b, width):
            at = pl.multiple_of(b * width, width)
            row_gap = cell_row - rc_ref[0:1, pl.ds(at, width)]
            col_gap = cell_col - rc_ref[1:2, pl.ds(at, width)]
            near = jnp.maximum(1.0 - row_gap * row_gap - col_gap * col_gap, 0.0)
            level = rc_ref[2:3, pl.ds(at, width)]
            ratio = jnp.ones((size, width), F32)
            for l in range(1, levels):
                other = (1.0 + level) / (1.0 + jnp.abs(level - float(l)))
                ratio = jnp.where(cell_lev == float(l), other, ratio)
            cov = jnp.dot(cells, w_ref[0, :, pl.ds(at, width)], preferred_element_type=F32)
            high, low = split(cov * (near * near) * ratio)
            s = s_ref[pl.ds(at, width), :]
            acc_ref[0:size] += jnp.dot(high, s, preferred_element_type=F32)
            acc_ref[0:size, 0:LANE] += jnp.dot(low, s[:, 0:LANE], preferred_element_type=F32)

        def pair(b, _):
            body(2 * b, BLOCK)
            body(2 * b + 1, BLOCK)
            return 0

        def half(b, _):
            body(b, BLOCK // 2)
            return 0

        pairs = off // (2 * BLOCK)
        lax.fori_loop(0, pairs, pair, 0)
        lax.fori_loop(4 * pairs, (off + BLOCK // 2 - 1) // (BLOCK // 2), half, 0)
        out = x + (acc_ref[0:size, 0:LANE] + acc_ref[0:size, LANE : 2 * LANE]).T[0 : groups * share]
        for g in range(groups):
            out_ref[id_ref[1] ^ g, 0:share, n * LANE : n * LANE + size] = out[
                g * share : (g + 1) * share
            ]

    for n in range(0, width // LANE, 2):
        if n + 2 <= width // LANE:
            pl.when(pieces >= n + 2)(functools.partial(update, n, 2))
        pl.when(pieces == n + 1)(functools.partial(update, n, 1))


def update_points(geometry, ids, att, seen, packed):
    w, s, rc, span = packed
    groups, padded, slots = seen.shape
    return pl.pallas_call(
        functools.partial(points_kernel, geometry),
        out_shape=jax.ShapeDtypeStruct((groups, padded, slots // 2), F32),
        in_specs=[SMEM] * 2 + [VMEM] * 5,
        out_specs=VMEM,
        scratch_shapes=[pltpu.VMEM((2 * LANE, 2 * LANE), F32)],
        compiler_params=PARAMS,
        cost_estimate=cost(8),
        name="update_points",
    )(ids, span, att, seen, w, s, rc)


def grid_kernel(geometry, begin, groups, id_ref, span_ref, w_ref, s_ref, rc_ref, *refs):
    levels, all_rows, share, row_scale, col_scale = geometry
    xs, outs, refs = refs[:groups], refs[groups : 2 * groups], refs[2 * groups :]
    xt_ref, acc_ref, q_ref, high_ref, low_ref = refs
    bands = xs[0].shape[0]
    height = levels * all_rows
    rows = outs[0].shape[1] // (share * levels)
    first = [span_ref[begin + p] for p in range(rows)]
    last = [span_ref[all_rows + begin + p] for p in range(rows)]
    cols = bands * LANE
    members = groups * share
    q_ref[...] = (
        lax.broadcasted_iota(jnp.int32, (cols, LANE), 0) + id_ref[1] * cols
    ).astype(F32) * col_scale

    def cells(i):
        return jnp.concatenate(
            [
                jnp.concatenate(
                    [x.at[b][pl.ds(i, share, stride=height), :] for x in xs], axis=0
                )
                for b in range(bands)
            ],
            axis=1,
        )

    for l in range(levels):
        for p in range(rows):
            xt_ref[l * rows + p] = triple(cells(l * all_rows + begin + p))

    half = BLOCK // 2
    spans = [jnp.maximum(last[p] - first[p], 0) for p in range(rows)]
    steps = [(n + half - 1) // BLOCK for n in spans]
    ends = [steps[0]]
    for n in steps[1:]:
        ends.append(ends[-1] + n)
    acc_ref[...] = jnp.zeros(acc_ref.shape, F32)

    def locate(i):
        p = jnp.int32(0)
        at = first[0] + i * BLOCK
        for j in range(1, rows):
            past = i >= ends[j - 1]
            p = jnp.where(past, j, p)
            at = jnp.where(past, first[j] + (i - ends[j - 1]) * BLOCK, at)
        return p, pl.multiple_of(at, LANE)

    def tapered(p, at, width):
        row_gap = (id_ref[0] * all_rows + begin + p).astype(F32) * row_scale - rc_ref[
            0:1, pl.ds(at, width)
        ]
        base = 1.0 - row_gap * row_gap
        q = q_ref[...]
        col_gap = jnp.concatenate([q] * (width // LANE), axis=1) - rc_ref[1:2, pl.ds(at, width)]
        near = jnp.maximum(base - col_gap * col_gap, 0.0)
        return near * near

    def gains(p, l, at, width, taper):
        w = w_ref[l, :, pl.ds(at, width)]
        return split(jnp.dot(xt_ref[l * rows + p], w, preferred_element_type=F32) * taper)

    def add(p, l, at, high, low):
        s = s_ref[pl.ds(at, high.shape[1]), :]
        acc_ref[p, l] += jnp.dot(high, s, preferred_element_type=F32)
        acc_ref[p, l, :, 0:LANE] += jnp.dot(low, s[:, 0:LANE], preferred_element_type=F32)

    def spread(i, l):
        p, at = locate(i)
        add(p, l, at, high_ref[l], low_ref[l])

    def step(i):
        p, at = locate(i)
        taper = tapered(p, at, BLOCK)
        for l in range(levels):
            high, low = gains(p, l, at, BLOCK, taper)
            if l == 0:
                spread(jnp.maximum(i - 1, 0), levels - 1)
            else:
                spread(i, l - 1)
            high_ref[l], low_ref[l] = high, low

    def several(i, _):
        for n in range(4):
            step(4 * i + n)
        return 0

    def single(i, _):
        step(i)
        return 0

    high_ref[levels - 1] = jnp.zeros(high_ref.shape[1:], BF16)
    low_ref[levels - 1] = jnp.zeros(low_ref.shape[1:], BF16)
    lax.fori_loop(0, ends[-1] // 4, several, 0)
    lax.fori_loop(ends[-1] // 4 * 4, ends[-1], single, 0)
    spread(jnp.maximum(ends[-1] - 1, 0), levels - 1)

    def remainder(p, _):
        def of(values):
            chosen = values[0]
            for j in range(1, rows):
                chosen = jnp.where(p == j, values[j], chosen)
            return chosen

        at = pl.multiple_of(of([first[j] + steps[j] * BLOCK for j in range(rows)]), LANE)

        @pl.when(of(spans) > of(steps) * BLOCK)
        def _():
            taper = tapered(p, at, half)
            for l in range(levels):
                add(p, l, at, *gains(p, l, at, half, taper))

        return 0

    lax.fori_loop(0, rows, remainder, 0)

    def store(p, _):
        for l in range(levels):
            at = pl.ds(l * all_rows + begin + p, share, stride=height)
            to = pl.ds(l * rows + p, share, stride=levels * rows)
            inc = (acc_ref[p, l, :, 0:LANE] + acc_ref[p, l, :, LANE : 2 * LANE]).T[0:members]
            for g in range(groups):
                for b in range(bands):
                    outs[g].at[b][to, :] = (
                        xs[g].at[b][at, :]
                        + inc[g * share : (g + 1) * share, b * LANE : (b + 1) * LANE]
                    )
        return 0

    lax.fori_loop(0, rows, store, 0)


def update_grid(geometry, ids, packed, parts, begin, rows):
    w, s, rc, span = packed
    levels, all_rows = geometry[:2]
    groups = len(parts)
    bands, depth, _ = parts[0].shape
    cols = bands * LANE
    out = jax.ShapeDtypeStruct((bands, depth // all_rows * rows, LANE), F32)
    return pl.pallas_call(
        functools.partial(grid_kernel, geometry, begin, groups),
        out_shape=[out] * groups,
        in_specs=[SMEM] * 2 + [VMEM] * (3 + groups),
        out_specs=[VMEM] * groups,
        scratch_shapes=[
            pltpu.VMEM((levels * rows, cols, DEEP), BF16),
            pltpu.VMEM((rows, levels, cols, 2 * LANE), F32),
            pltpu.VMEM((cols, LANE), F32),
            pltpu.VMEM((levels, cols, BLOCK), BF16),
            pltpu.VMEM((levels, cols, BLOCK), BF16),
        ],
        compiler_params=PARAMS,
        cost_estimate=cost(7 * rows),
        name="update_grid",
    )(ids, span, w, s, rc, *parts)


def restore_kernel(groups, id_ref, *refs):
    pieces, befores, out_ref = refs[:groups], refs[groups:-1], refs[-1]
    members, levels, all_rows, _ = out_ref.shape
    bands = pieces[0].shape[0]
    height = pieces[0].shape[1] // members
    rows = height // levels
    begin = all_rows - rows

    def body(m, _):
        at = pl.multiple_of(m * height, height)
        for before in befores:
            for l in range(levels):
                out_ref[m, l, 0:begin, :] = before[m, l]
        for k in range(groups):
            for band in range(bands):
                block = pieces[k][band, pl.ds(at, height), :]
                first = pl.multiple_of((id_ref[1] ^ k) * (bands * LANE) + band * LANE, LANE)
                for l in range(levels):
                    out_ref[m, l, begin:all_rows, pl.ds(first, LANE)] = block[
                        l * rows : (l + 1) * rows
                    ]
        return 0

    lax.fori_loop(0, members, body, 0)


def restore(ids, pieces, befores, shape):
    return pl.pallas_call(
        functools.partial(restore_kernel, len(pieces)),
        out_shape=jax.ShapeDtypeStruct(shape, F32),
        in_specs=[SMEM] + [VMEM] * (len(pieces) + len(befores)),
        out_specs=VMEM,
        compiler_params=PARAMS,
        cost_estimate=cost(2),
        name="restore",
    )(ids, *pieces, *befores)


def shifted(value, steps):
    count = lax.axis_size("tile")
    pairs = [(i, i + steps) for i in range(count) if 0 <= i + steps < count]
    return lax.ppermute(value, "tile", pairs)


def paired(value, odd):
    count = lax.axis_size("tile")
    firsts = range(odd, count - 1, 2)
    pairs = [(i, i + 1) for i in firsts] + [(i + 1, i) for i in firsts]
    return lax.ppermute(value, "tile", pairs)


def window_of(value):
    return [
        shifted(value, 2),
        shifted(value, -2),
        value,
        paired(value, 0),
        paired(value, 1),
    ]


def crossed(value, step):
    count = lax.axis_size("ens")
    return lax.ppermute(value, "ens", [(i, i ^ step) for i in range(count)])


def exchanged(parts):
    return [parts[0]] + [crossed(parts[k], k) for k in range(1, len(parts))]


def on_device(initial_sample_set, flow_velocity, obs_loc, obs_count, obs_value, obs_error):
    x = initial_sample_set
    share, levels, rows, col_total = x.shape
    ens = lax.axis_size("ens")
    ids = jnp.stack([lax.axis_index("tile"), lax.axis_index("ens")]).astype(jnp.int32)
    geometry = (levels, rows, share, 1.0 / (REACH * rows), 1.0 / (col_total // 2))

    odd = lax.axis_index("tile") % 2
    near, far = (1 - odd) * (rows - 1), odd * (rows - 1)
    even_row = paired(lax.dynamic_index_in_dim(x, near, 2, False), 0)
    odd_row = paired(lax.dynamic_index_in_dim(lax.optimization_barrier(x), far, 2, False), 1)
    att = order(ids, obs_loc, obs_value, obs_error, obs_count, rows)
    parts = forecast(ids, x, flow_velocity, ens)
    inner, edges = [(1, rows - 2)], [(0, 0), (rows - 1, rows - 1)]
    seen = observe(ids, att[0], parts, levels, share, inner)
    parts = mend(ids, even_row, odd_row, flow_velocity, parts)
    seen = observe(ids, att[0], parts, levels, share, edges, (seen,))
    seen = lax.all_gather(seen, "ens", axis=0)
    parts, seen = lax.optimization_barrier((parts, seen))
    priors = window_of(seen[None])
    ahead = observe(ids, att[1], parts, levels, share, [(0, rows - 1)])
    ahead = lax.all_gather(ahead, "ens", axis=0)
    parts, ahead = lax.optimization_barrier((parts, ahead))
    parts = exchanged(parts)
    priors, ahead = lax.optimization_barrier((priors, ahead))
    packed = pack(geometry, ids, priors)
    later = update_points(geometry, ids, att[1], ahead, packed)
    later = window_of(jnp.stack([later, crossed(later, 1)]))
    parts = update_grid(geometry, ids, packed, parts, 0, rows)
    packed = pack(geometry, ids, later)
    half = rows // 2
    upper = update_grid(geometry, ids, packed, parts, 0, half)
    parts, upper = lax.optimization_barrier((parts, upper))
    lower = update_grid(geometry, ids, packed, parts, half, rows - half)
    done = restore(ids, exchanged(upper), (), (share, levels, half, col_total))
    return restore(ids, exchanged(lower), (done,), x.shape)


def solution(mesh):
    in_specs = (
        P("ens", None, "tile", None),
        P(None, None, "tile", None),
        P(None, None, "tile"),
        P(None, "tile"),
        P(None, "tile"),
        P(None, "tile"),
    )
    out_specs = P("ens", None, "tile", None)
    return jax.shard_map(
        on_device, mesh=mesh, in_specs=in_specs, out_specs=out_specs, check_vma=False
    )
```
